128 devices in a mesh: node: 16 (over x, z), tensor: 8 (over y, core).
Axes of the slice: x: 4, y: 4, z: 4, core: 2. Of those that a mesh axis runs over, the one named last changes fastest.
Arguments:
- tokens: bfloat16 [4096, 3584], P(('node', 'tensor')), may hold values from -24 to 24
- out_grad: bfloat16 [4096, 3584], P(('node', 'tensor')), may hold values from -24 to 24
- gate_weights: bfloat16 [4096, 2], P(('node', 'tensor')), may hold values from 0.099609375 to 1
- expert_ids: int32 [4096, 2], P(('node', 'tensor')), may hold values from 0 to 15, as said below
- dense_gate: bfloat16 [3584, 3072], P(None, 'tensor'), may hold values from -0.09375 to 0.09375
- dense_up: bfloat16 [3584, 3072], P(None, 'tensor'), may hold values from -0.09375 to 0.09375
- dense_down: bfloat16 [3584, 3072], P(None, 'tensor'), may hold values from -0.109375 to 0.109375
- expert_gate: bfloat16 [16, 3584, 3072], P('node', None, 'tensor'), may hold values from -0.09375 to 0.09375
- expert_up: bfloat16 [16, 3584, 3072], P('node', None, 'tensor'), may hold values from -0.09375 to 0.09375
- expert_down: bfloat16 [16, 3584, 3072], P('node', None, 'tensor'), may hold values from -0.109375 to 0.109375
Outputs:
- input_grad: bfloat16 [4096, 3584], P(('node', 'tensor'))
- gate_weight_grad: float32 [4096, 2], P(('node', 'tensor'))
- dense_gate_grad: bfloat16 [3584, 3072], P('node', 'tensor')
- dense_up_grad: bfloat16 [3584, 3072], P('node', 'tensor')
- dense_down_grad: bfloat16 [3584, 3072], P('node', 'tensor')
- expert_gate_grad: bfloat16 [16, 3584, 3072], P('node', None, 'tensor')
- expert_up_grad: bfloat16 [16, 3584, 3072], P('node', None, 'tensor')
- expert_down_grad: bfloat16 [16, 3584, 3072], P('node', None, 'tensor')
The draws below stay inside these ranges and needn't reach their ends.
Inputs may be any that keep to these rules, and one draw needn't show every extreme that they name: `expert_ids`: each row names two different experts. In the rows of one device (aligned blocks of 32 rows) no expert is named more than 8 times, and one expert is named exactly 8 times in the rows of every device.
All inputs are finite; a program needn't handle non-finite values.
Results may differ from the reference program's by a relative error of at most 0.02.
Values may be sent and summed in bfloat16 or wider, within the bound.
A program may use at most 192 MiB of HBM per device.

```python
import math
import jax
import jax.numpy as jnp
from jax import lax

D = 3584
FF = 3072
HE = 3072
TOK_NODE = 256
TOK_DEV = 32
TOKENS = 4096
EXPERTS = 16
CAP = 8
N_NODE = 16
N_TENSOR = 8


def draw_expert_ids(key, part):
    key = jax.random.fold_in(key, 11)
    blocks = TOKENS // TOK_DEV
    others = EXPERTS - 1
    remain = 2 * TOK_DEV - CAP
    ranks = jnp.arange(others + 1, dtype=jnp.int32)
    level_square = remain * (others - ranks) ** 2 // (others * others)
    level_linear = remain * (others - ranks) // others
    bound_square = remain - level_square
    bound_linear = remain - level_linear
    hot_key, rest_key = jax.random.split(key)
    hot_expert = jax.random.randint(hot_key, (), 0, EXPERTS)
    position = jnp.arange(2 * TOK_DEV, dtype=jnp.int32)

    def one_block(block_key):
        order_key, row_key, flip_key, shape_key = jax.random.split(block_key, 4)
        pick_shape = jax.random.randint(shape_key, (), 0, 2)
        bounds = jnp.where(pick_shape == 1, bound_square, bound_linear)
        rank_of = jnp.sum((bounds[None, 1:] <= (position - CAP)[:, None]).astype(jnp.int32), axis=1)
        order = jax.random.permutation(order_key, others)
        label_rest = order[jnp.clip(rank_of, 0, others - 1)]
        label_rest = jnp.where(label_rest >= hot_expert, label_rest + 1, label_rest)
        labels = jnp.where(position < CAP, hot_expert, label_rest)
        pairs = jnp.stack([labels[:TOK_DEV], labels[TOK_DEV:]], axis=1)
        flip = jax.random.randint(flip_key, (TOK_DEV, 1), 0, 2)
        pairs = jnp.where(flip == 1, pairs[:, ::-1], pairs)
        row_order = jax.random.permutation(row_key, TOK_DEV)
        return pairs[row_order]
    block_keys = jax.random.split(rest_key, blocks)
    return jax.vmap(one_block)(block_keys).reshape(TOKENS, 2).astype(jnp.int32)


def with_spikes(entries, stream_key, source, target, shards_of, factor):
    owner, partner = [(jnp.arange(entries.shape[dim]) // (entries.shape[dim] // shards_of)).reshape([-1 if axis == dim else 1 for axis in range(entries.ndim)]) for dim in (source, target)]
    chosen = jax.random.permutation(stream_key, shards_of)[partner]
    strong = (owner == chosen) | (owner == (partner + shards_of // 2) % shards_of)
    return jnp.where(strong, factor * entries, entries)


def block_scale(key, extent, cuts, smallest, high):
    gain, own = 1.0, jax.random.fold_in(key, 6)
    for dim, parts in cuts:
        heights = jnp.exp(jax.random.uniform(jax.random.fold_in(own, dim), (parts,), jnp.float32, smallest / len(cuts), high / len(cuts)))
        gain = gain * jnp.repeat(heights, extent[dim] // parts).reshape([-1 if axis == dim else 1 for axis in range(len(extent))])
    return gain


def normal_values(own_key, dims, deviation, most, shards=(), kind=jnp.bfloat16):
    array = deviation * jax.random.normal(own_key, dims, jnp.float32)
    if shards:
        array = array * block_scale(own_key, dims, shards, -0.22, 0.18)
    return jnp.clip(array, -most, most).astype(kind)


def noise_with(rng, extent, width, reach, shards, heavy, kind=jnp.bfloat16):
    result = width * jax.random.normal(rng, extent, jnp.float32)
    if shards:
        result = result * block_scale(rng, extent, shards, -0.22, 0.18)
    return jnp.clip(with_spikes(result, jax.random.fold_in(rng, 3), *heavy), -reach, reach).astype(kind)


def setup_inputs(seed: int = 0) -> dict:
    splits = jax.random.split(jax.random.key(seed), 11)
    return {
        "tokens": noise_with(splits[0], (TOKENS, D), 1.0, 24.0, ((0, 128),), (0, 1, 128, 5.5)),
        "out_grad": noise_with(splits[1], (TOKENS, D), 1.0, 24.0, ((0, 128),), (0, 1, 128, 5.5)),
        "gate_weights": jnp.clip(jnp.exp(math.log(1.0) - 2.306499 * jax.random.uniform(splits[2], (TOKENS, 2), jnp.float32) ** block_scale(splits[2], (TOKENS, 2), ((0, 128),), -0.2, 0.2)), 0.099609375, 1.0).astype(jnp.bfloat16),
        "expert_ids": draw_expert_ids(jax.random.fold_in(splits[10], 71), 0),
        "dense_gate": normal_values(splits[4], (D, FF), D ** -0.5, 0.09375, ((1, 8),)),
        "dense_up": normal_values(splits[5], (D, FF), D ** -0.5, 0.09375, ((1, 8),)),
        "dense_down": normal_values(splits[6], (D, FF), FF ** -0.5, 0.109375, ((1, 8),)),
        "expert_gate": normal_values(splits[7], (EXPERTS, D, HE), D ** -0.5, 0.09375, ((0, 16), (2, 8))),
        "expert_up": normal_values(splits[8], (EXPERTS, D, HE), D ** -0.5, 0.09375, ((0, 16), (2, 8))),
        "expert_down": normal_values(splits[9], (EXPERTS, D, HE), HE ** -0.5, 0.109375, ((0, 16), (2, 8))),
    }


def silu_parts(pre_gate):
    sigma = jax.nn.sigmoid(pre_gate)
    return pre_gate * sigma, sigma * (1.0 + pre_gate * (1.0 - sigma))


def reference(tokens, out_grad, gate_weights, expert_ids, dense_gate, dense_up, dense_down, expert_gate, expert_up, expert_down):
    wide = jnp.float32
    narrow = jnp.bfloat16
    pre_gate = jnp.dot(tokens, dense_gate, preferred_element_type=wide)
    pre_up = jnp.dot(tokens, dense_up, preferred_element_type=wide)
    hidden_grad = jnp.dot(out_grad, dense_down, preferred_element_type=wide)
    activated, derivative = silu_parts(pre_gate)
    dense_hidden = (activated * pre_up).astype(narrow)
    gate_part = (hidden_grad * pre_up * derivative).astype(narrow)
    up_part = (hidden_grad * activated).astype(narrow)
    dense_input = jnp.dot(gate_part, dense_gate.T, preferred_element_type=wide) + jnp.dot(up_part, dense_up.T, preferred_element_type=wide)

    def node_step(carry, node_index):
        row_start = (node_index * TOK_NODE).astype(jnp.int32)
        node_tokens = lax.dynamic_slice_in_dim(tokens, row_start, TOK_NODE, 0)
        node_grad = lax.dynamic_slice_in_dim(out_grad, row_start, TOK_NODE, 0)
        node_gate = lax.dynamic_slice_in_dim(gate_part, row_start, TOK_NODE, 0)
        node_up = lax.dynamic_slice_in_dim(up_part, row_start, TOK_NODE, 0)
        node_hidden = lax.dynamic_slice_in_dim(dense_hidden, row_start, TOK_NODE, 0)
        sums = (jnp.dot(node_tokens.T, node_gate, preferred_element_type=wide),
                jnp.dot(node_tokens.T, node_up, preferred_element_type=wide),
                jnp.dot(node_grad.T, node_hidden, preferred_element_type=wide))
        rounded = [lax.optimization_barrier(value.astype(narrow)).astype(wide) for value in sums]
        return (carry[0] + rounded[0], carry[1] + rounded[1], carry[2] + rounded[2]), None

    empty = jnp.zeros((D, FF), wide)
    totals, unused = lax.scan(node_step, (empty, empty, empty), jnp.arange(N_NODE, dtype=jnp.int32))
    dense_grads = [(value / N_NODE).astype(narrow) for value in totals]

    blocks = TOKENS // TOK_DEV
    flat_ids = expert_ids.reshape(blocks, 2 * TOK_DEV)
    onehot = (flat_ids[:, :, None] == jnp.arange(EXPERTS, dtype=jnp.int32)[None, None, :]).astype(jnp.int32)
    before = jnp.cumsum(onehot, axis=1) - onehot
    slot_index = jnp.sum(before * onehot, axis=2)
    position = (jnp.arange(blocks, dtype=jnp.int32)[:, None] * CAP + slot_index).reshape(-1).astype(jnp.int32)
    sentinel = 2 * TOKENS
    table = jnp.full((EXPERTS, blocks * CAP), sentinel, jnp.int32)
    table = table.at[flat_ids.reshape(-1), position].set(jnp.arange(sentinel, dtype=jnp.int32))
    padded_tokens = jnp.concatenate([tokens, jnp.zeros((1, D), tokens.dtype)], 0)
    padded_grad = jnp.concatenate([out_grad, jnp.zeros((1, D), out_grad.dtype)], 0)
    padded_gates = jnp.concatenate([gate_weights.reshape(-1), jnp.zeros((1,), gate_weights.dtype)], 0)
    block_width = HE // N_TENSOR

    def one_expert(inputs):
        assigned, w_gate, w_up, w_down = inputs
        token_index = jnp.where(assigned < sentinel, assigned // 2, TOKENS).astype(jnp.int32)
        rows_x = padded_tokens[token_index]
        rows_dy = padded_grad[token_index]
        weight = padded_gates[assigned].astype(wide)[:, None]
        row_count = rows_x.shape[0]
        e_gate = jnp.dot(rows_x, w_gate, preferred_element_type=wide)
        e_up = jnp.dot(rows_x, w_up, preferred_element_type=wide)
        e_hidden_grad = jnp.dot(rows_dy, w_down, preferred_element_type=wide)
        e_act, e_deriv = silu_parts(e_gate)
        product = (e_act * e_up * e_hidden_grad).reshape(row_count, N_TENSOR, block_width)
        block_sums = lax.optimization_barrier(jnp.sum(product, axis=2).astype(narrow)).astype(wide)
        share = jnp.sum(block_sums, axis=1)
        e_gate_part = (weight * e_hidden_grad * e_up * e_deriv).astype(narrow)
        e_up_part = (weight * e_hidden_grad * e_act).astype(narrow)
        e_hidden = (weight * e_act * e_up).astype(narrow)
        terms = jnp.einsum("rbh,dbh->rbd", e_gate_part.astype(wide).reshape(row_count, N_TENSOR, block_width),
                           w_gate.astype(wide).reshape(D, N_TENSOR, block_width))
        terms = terms + jnp.einsum("rbh,dbh->rbd", e_up_part.astype(wide).reshape(row_count, N_TENSOR, block_width),
                                   w_up.astype(wide).reshape(D, N_TENSOR, block_width))
        terms = lax.optimization_barrier(terms.astype(narrow)).astype(wide)
        input_part = jnp.sum(terms, axis=1)
        grad_gate = jnp.dot(rows_x.T, e_gate_part, preferred_element_type=wide).astype(narrow)
        grad_up = jnp.dot(rows_x.T, e_up_part, preferred_element_type=wide).astype(narrow)
        grad_down = jnp.dot(rows_dy.T, e_hidden, preferred_element_type=wide).astype(narrow)
        return input_part, share, grad_gate, grad_up, grad_down

    input_parts, shares, grad_gate, grad_up, grad_down = lax.map(one_expert, (table, expert_gate, expert_up, expert_down))
    flat_table = table.reshape(-1)
    assigned_input = jnp.zeros((sentinel + 1, D), wide).at[flat_table].add(input_parts.reshape(-1, D))
    assigned_share = jnp.zeros((sentinel + 1,), wide).at[flat_table].add(shares.reshape(-1))
    pair_input = assigned_input[:sentinel].reshape(TOKENS, 2, D)
    gate_weight_grad = assigned_share[:sentinel].reshape(TOKENS, 2)
    input_grad = (out_grad.astype(wide) + dense_input + pair_input[:, 0] + pair_input[:, 1]).astype(narrow)
    return (input_grad, gate_weight_grad, dense_grads[0], dense_grads[1], dense_grads[2], grad_gate, grad_up, grad_down)
```

```python
import jax
import jax.numpy as jnp
from jax import lax
from jax.experimental import pallas as pl
from jax.experimental.pallas import tpu as pltpu
from jax.sharding import PartitionSpec as P

MESH = pl.DeviceIdType.MESH
BF16 = jnp.bfloat16
F32 = jnp.float32
SIDE = 4
CORES = 2
ANY = pl.BlockSpec(memory_space=pl.ANY)
VMEM = pl.BlockSpec(memory_space=pltpu.VMEM)


def place():
    node = lax.axis_index("node")
    tensor = lax.axis_index("tensor")
    return (
        lax.div(node, SIDE),
        lax.rem(node, SIDE),
        lax.div(tensor, CORES),
        lax.rem(tensor, CORES),
    )


def turn(position, steps):
    return lax.rem(position + steps, SIDE)


def meet(peers):
    barrier = pltpu.get_barrier_semaphore()
    for peer in peers:
        pl.semaphore_signal(barrier, inc=1, device_id=peer, device_id_type=MESH)
    pl.semaphore_wait(barrier, len(peers))


class Net:
    def __init__(self, send_sems, recv_sems):
        self.send_sems, self.recv_sems = send_sems, recv_sems
        self.copies = []

    def start(self, src, dst, peer):
        index = len(self.copies)
        copy = pltpu.make_async_remote_copy(
            src_ref=src,
            dst_ref=dst,
            send_sem=self.send_sems.at[index],
            recv_sem=self.recv_sems.at[index],
            device_id=peer,
            device_id_type=MESH,
        )
        copy.start()
        self.copies.append(copy)
        return copy

    def drain(self):
        for copy in self.copies:
            copy.wait_send()


def total(dst, sources, scale=None, slab=16):
    rows = dst.shape[-2]
    leads = [()]
    for size in dst.shape[:-2]:
        leads = [lead + (i,) for lead in leads for i in range(size)]
    for lead in leads:

        def body(i, carry, lead=lead):
            at = lead + (pl.ds(pl.multiple_of(i * slab, slab), slab), slice(None))
            value = sources[0][at].astype(F32)
            for source in sources[1:]:
                value = value + source[at].astype(F32)
            if scale is not None:
                value = value * scale
            dst[at] = value.astype(dst.dtype)
            return carry

        lax.fori_loop(0, rows // slab, body, 0)


def node_peers(x, z, tensor):
    peers = []
    for dx in range(SIDE):
        for dz in range(SIDE):
            if dx or dz:
                peers.append((turn(x, dx) * SIDE + turn(z, dz), tensor))
    return peers


class Gather:
    def __init__(self, net, node, y, core, own, whole, rows):
        self.net, self.own, self.whole, self.rows = net, own, whole, rows
        self.me = y * CORES + core
        self.right_at = turn(y, 1) * CORES + core
        self.left_at = turn(y, SIDE - 1) * CORES + core
        self.far_at = turn(y, 2) * CORES + core
        self.right = (node, self.right_at)
        self.left = (node, self.left_at)
        self.partner = (node, y * CORES + 1 - core)

    def chunk(self, half, at):
        return self.whole[half].at[pl.ds(pl.multiple_of(at * self.rows, self.rows), self.rows)]

    def start(self):
        send = self.net.start
        me, own = self.me, self.own
        self.to_right, self.to_left, self.to_partner = [None] * 2, [None] * 2, []
        for step in range(2):
            self.to_right[step] = send(own[step], self.chunk(step, me), self.right)
            self.to_left[1 - step] = send(own[1 - step], self.chunk(1 - step, me), self.left)
        for half in range(2):
            self.to_partner.append(send(own[half], self.chunk(half, me), self.partner))

    def relay(self):
        send = self.net.start
        left_at, right_at = self.left_at, self.right_at
        self.to_right[0].wait_recv()
        self.relay_right = send(self.chunk(0, left_at), self.chunk(0, left_at), self.right)
        self.to_partner.append(send(self.chunk(0, left_at), self.chunk(0, left_at), self.partner))
        self.to_left[1].wait_recv()
        self.relay_left = send(self.chunk(1, right_at), self.chunk(1, right_at), self.left)
        self.to_partner.append(send(self.chunk(1, right_at), self.chunk(1, right_at), self.partner))
        self.to_right[1].wait_recv()
        self.to_partner.append(send(self.chunk(1, left_at), self.chunk(1, left_at), self.partner))
        self.to_left[0].wait_recv()
        self.to_partner.append(send(self.chunk(0, right_at), self.chunk(0, right_at), self.partner))

    def finish(self):
        send = self.net.start
        far = self.far_at
        self.relay_right.wait_recv()
        self.to_partner.append(send(self.chunk(0, far), self.chunk(0, far), self.partner))
        self.relay_left.wait_recv()
        self.to_partner.append(send(self.chunk(1, far), self.chunk(1, far), self.partner))
        for copy in self.to_partner:
            copy.wait_recv()


class RingSum:
    def __init__(self, net, position, right, left, part, relayed, from_left, from_right):
        self.net, self.right, self.left, self.part = net, right, left, part
        self.relayed, self.from_left, self.from_right = relayed, from_left, from_right
        self.ahead, self.far, self.behind = (turn(position, k) for k in (1, 2, 3))

    def start_far(self):
        send, part = self.net.start, self.part
        self.relay_right = send(part(self.far, 0), self.relayed(0), self.right)
        self.relay_left = send(part(self.far, 1), self.relayed(1), self.left)

    def start_ahead(self):
        self.direct_right = self.net.start(self.part(self.ahead, 1), self.from_left(1), self.right)

    def start_behind(self):
        self.direct_left = self.net.start(self.part(self.behind, 0), self.from_right(0), self.left)

    def middle(self):
        send, part = self.net.start, self.part
        self.relay_right.wait_recv()
        mine = part(self.ahead, 0)
        total(mine, [mine, self.relayed(0)])
        self.sum_right = send(mine, self.from_left(0), self.right)
        self.relay_left.wait_recv()
        mine = part(self.behind, 1)
        total(mine, [mine, self.relayed(1)])
        self.sum_left = send(mine, self.from_right(1), self.left)

    def finish(self):
        for copy in (self.direct_right, self.direct_left, self.sum_right, self.sum_left):
            copy.wait_recv()


GATHER_COPIES = 2 * 14 + 15


def gather_kernel(
    tok, grad, outgoing, tok_all, grad_all, rows_x, rows_dy,
    landed, ordered, send_sems, recv_sems, local_sems,
):
    x, z, y, core = place()
    node, tensor = x * SIDE + z, y * CORES + core
    net = Net(send_sems, recv_sems)
    peers = node_peers(x, z, tensor)
    local_rows = tok.shape[0]
    block = landed.shape[0] // (SIDE * SIDE)
    slots = ordered.shape[0] // 2
    dense = Gather(net, node, y, core, (tok, grad), (tok_all, grad_all), local_rows)
    routed = Gather(
        net, node, y, core,
        (ordered.at[pl.ds(0, slots)], ordered.at[pl.ds(slots, slots)]),
        (rows_x, rows_dy), slots,
    )
    meet(peers + [dense.right, dense.left, dense.partner])

    def rows_of(ref, index):
        return ref.at[pl.ds(pl.multiple_of(index * block, block), block)]

    dense.start()
    arrivals = [net.start(rows_of(outgoing, peer[0]), rows_of(landed, node), peer) for peer in peers]
    local = [
        pltpu.make_async_copy(rows_of(outgoing, node), rows_of(landed, node), local_sems.at[0]),
        pltpu.make_async_copy(tok, dense.chunk(0, tensor), local_sems.at[1]),
        pltpu.make_async_copy(grad, dense.chunk(1, tensor), local_sems.at[2]),
    ]
    for copy in local:
        copy.start()
    dense.relay()
    for copy in arrivals:
        copy.wait_recv()
    local[0].wait()
    row = lax.broadcasted_iota(jnp.int32, (2 * slots, 2 * slots), 0)
    col = lax.broadcasted_iota(jnp.int32, (2 * slots, 2 * slots), 1)
    half = block // 2
    second = (row >= slots).astype(jnp.int32)
    within = row - second * slots
    source = lax.div(within, half) * block + lax.rem(within, half) + second * half
    table = (col == source).astype(F32).astype(BF16)
    width = 512

    def part(i, carry):
        cols = pl.ds(pl.multiple_of(i * width, width), width)
        ordered[:, cols] = jnp.dot(table, landed[:, cols], preferred_element_type=F32).astype(BF16)
        return carry

    lax.fori_loop(0, landed.shape[1] // width, part, 0)
    routed.start()
    own = [
        pltpu.make_async_copy(routed.own[h], routed.chunk(h, tensor), local_sems.at[3 + h])
        for h in range(2)
    ]
    for copy in own:
        copy.start()
    dense.finish()
    routed.relay()
    routed.finish()
    for copy in local[1:] + own:
        copy.wait()
    net.drain()


def gather_rows(tokens, out_grad, outgoing):
    rows, width = tokens.shape
    count = SIDE * CORES
    slots = outgoing.shape[0] // 2
    return pl.pallas_call(
        gather_kernel,
        out_shape=[
            jax.ShapeDtypeStruct((count * rows, width), BF16),
            jax.ShapeDtypeStruct((count * rows, width), BF16),
            jax.ShapeDtypeStruct((count * slots, width), BF16),
            jax.ShapeDtypeStruct((count * slots, width), BF16),
        ],
        in_specs=[ANY] * 3,
        out_specs=[ANY] * 4,
        scratch_shapes=[
            pltpu.VMEM(outgoing.shape, BF16),
            pltpu.VMEM(outgoing.shape, BF16),
            pltpu.SemaphoreType.DMA((GATHER_COPIES,)),
            pltpu.SemaphoreType.DMA((GATHER_COPIES,)),
            pltpu.SemaphoreType.DMA((5,)),
        ],
        compiler_params=pltpu.CompilerParams(
            collective_id=0, has_side_effects=True, vmem_limit_bytes=48 << 20
        ),
        name="gather_rows",
    )(tokens, out_grad, outgoing)


WEIGHT_COPIES = 4 * 6


def weight_kernel(
    both, down, out_gate, out_up, out_down,
    grads, relayed, from_left, from_right, relayed2, from_left2, from_right2,
    send_sems, recv_sems, local_sems,
):
    x, z, y, core = place()
    tensor = y * CORES + core
    net = Net(send_sems, recv_sems)
    wide = both.shape[-1]
    rows, width = grads.shape[2:]
    half = rows // 2
    local = [
        pltpu.make_async_copy(both, grads.at[:, :, :, pl.ds(0, wide)], local_sems.at[0]),
        pltpu.make_async_copy(down, grads.at[:, :, :, pl.ds(wide, width - wide)], local_sems.at[1]),
    ]
    for copy in local:
        copy.start()

    def at(xx, zz):
        return (xx * SIDE + zz, tensor)

    around_x = (at(turn(x, 1), z), at(turn(x, 3), z))
    around_z = (at(x, turn(z, 1)), at(x, turn(z, 3)))
    meet(list(around_x + around_z))
    for copy in local:
        copy.wait()

    pairs = SIDE // 2

    def x_part(position, h):
        return grads.at[position, pl.ds(h * pairs, pairs), pl.ds(0, half)]

    def z_part(position, h):
        return grads.at[pl.ds(h * pairs, pairs), position, pl.ds(half, half)]

    def slot(ref, index):
        return lambda h: ref.at[index, pl.ds(h * pairs, pairs)]

    first = [
        RingSum(net, x, *around_x, x_part, slot(relayed, 0), slot(from_left, 0), slot(from_right, 0)),
        RingSum(net, z, *around_z, z_part, slot(relayed, 1), slot(from_left, 1), slot(from_right, 1)),
    ]
    for ring in first:
        ring.start_far()
    for ring in first:
        ring.start_ahead()
        ring.start_behind()
    for ring in first:
        ring.middle()
    for ring in first:
        ring.finish()
    cut = (0, half // 32 * 16 + 16, half)

    def rows_half(h):
        return pl.ds(cut[h], cut[h + 1] - cut[h])

    def summed_x(position, h):
        return from_left.at[0, position, rows_half(h)]

    def summed_z(position, h):
        return from_left.at[1, position, rows_half(h)]

    def slot2(ref, index):
        return lambda h: ref.at[index, rows_half(h)]

    second = [
        RingSum(net, z, *around_z, summed_x, slot2(relayed2, 0), slot2(from_left2, 0), slot2(from_right2, 0)),
        RingSum(net, x, *around_x, summed_z, slot2(relayed2, 1), slot2(from_left2, 1), slot2(from_right2, 1)),
    ]
    for index, axis in ((0, x), (1, z)):
        ring = second[index]
        for steps in (2, 1, 3, 0):
            other = turn(z if index == 0 else x, steps)
            if index == 0:
                mine = grads.at[x, other, pl.ds(0, half)]
            else:
                mine = grads.at[other, z, pl.ds(half, half)]
            left, right = from_left.at[index, other], from_right.at[index, other]
            total(left, [mine, left, right])
            if steps == 2:
                ring.start_far()
            elif steps == 1:
                ring.start_ahead()
            elif steps == 3:
                ring.start_behind()
    for ring in second:
        ring.middle()
    for index, ring in enumerate(second):
        ring.finish()
        own = from_left.at[index, z if index == 0 else x]
        outs = ((out_gate, 0), (out_up, 1), (out_down, 2))
        for ref, block in outs:
            cols = pl.ds(block * ref.shape[1], ref.shape[1])
            total(
                ref.at[pl.ds(index * half, half)],
                [own.at[:, cols], from_left2.at[index, :, cols], from_right2.at[index, :, cols]],
                scale=1.0 / (SIDE * SIDE),
            )
    net.drain()


def sum_weights(both, down):
    rows, wide = both.shape
    width = wide + down.shape[1]
    rows = rows // (SIDE * SIDE)
    half = rows // 2
    return pl.pallas_call(
        weight_kernel,
        out_shape=[jax.ShapeDtypeStruct((rows, down.shape[1]), BF16)] * 3,
        in_specs=[ANY] * 2,
        out_specs=[VMEM] * 3,
        scratch_shapes=[pltpu.VMEM((SIDE, SIDE, rows, width), BF16)]
        + [pltpu.VMEM((2, SIDE, half, width), BF16)] * 3
        + [pltpu.VMEM((2, half, width), BF16)] * 3
        + [
            pltpu.SemaphoreType.DMA((WEIGHT_COPIES,)),
            pltpu.SemaphoreType.DMA((WEIGHT_COPIES,)),
            pltpu.SemaphoreType.DMA((2,)),
        ],
        compiler_params=pltpu.CompilerParams(
            collective_id=1, has_side_effects=True, vmem_limit_bytes=48 << 20
        ),
        name="sum_weights",
    )(both.reshape(SIDE, SIDE, rows, wide), down.reshape(SIDE, SIDE, rows, down.shape[1]))


RETURN_COPIES = 8 + 6 + 15 + 7 + 15


def return_kernel(
    routed, dense, shares, back, dense_sum, back_shares,
    partial, from_core, relayed, from_left, from_right, parted, share_in, share_sum,
    send_sems, recv_sems, local_sems,
):
    x, z, y, core = place()
    node, tensor = x * SIDE + z, y * CORES + core
    net = Net(send_sems, recv_sems)
    peers = node_peers(x, z, tensor)
    count = SIDE * CORES
    mates = [(node, lax.rem(tensor + k, count)) for k in range(1, count)]
    partner = (node, y * CORES + 1 - core)
    right = (node, turn(y, 1) * CORES + core)
    left = (node, turn(y, 3) * CORES + core)
    slots = routed.shape[0] // count
    tokens = dense.shape[0] // count
    rows = slots + tokens
    meet(peers + mates)

    def routed_chunk(at):
        return routed.at[pl.ds(pl.multiple_of(at * slots, slots), slots)]

    def dense_chunk(at):
        return dense.at[pl.ds(pl.multiple_of(at * tokens, tokens), tokens)]

    order = [turn(y, k) for k in (2, 1, 3, 0)]
    crossed = []
    mine = []
    for k, other in enumerate(order):
        theirs = other * CORES + 1 - core
        crossed.append(
            (
                net.start(routed_chunk(theirs), from_core.at[other, pl.ds(0, slots)], partner),
                net.start(dense_chunk(theirs), from_core.at[other, pl.ds(slots, tokens)], partner),
            )
        )
        ours = other * CORES + core
        mine.append(
            (
                pltpu.make_async_copy(
                    routed_chunk(ours), partial.at[other, pl.ds(0, slots)], local_sems.at[2 * k]
                ),
                pltpu.make_async_copy(
                    dense_chunk(ours),
                    partial.at[other, pl.ds(slots, tokens)],
                    local_sems.at[2 * k + 1],
                ),
            )
        )
        for copy in mine[-1]:
            copy.start()
    share_copies = [net.start(shares, share_in.at[tensor], mate) for mate in mates]

    half = rows // 2

    def in_half(ref):
        return lambda h: ref.at[pl.ds(h * half, half)]

    def part(position, h):
        return partial.at[position, pl.ds(h * half, half)]

    ring = RingSum(net, y, right, left, part, in_half(relayed), in_half(from_left), in_half(from_right))
    for k, other in enumerate(order):
        for copy in mine[k]:
            copy.wait()
        for copy in crossed[k]:
            copy.wait_recv()
        total(partial.at[other], [partial.at[other], from_core.at[other]])
        (ring.start_far, ring.start_ahead, ring.start_behind, lambda: None)[k]()
    for copy in share_copies:
        copy.wait_recv()
    value = shares[...]
    for k in range(1, count):
        value = value + share_in[lax.rem(tensor + k, count)]
    share_sum[...] = value
    back_shares[node] = value
    share_back = [net.start(share_sum, back_shares.at[node], peer) for peer in peers]
    ring.middle()
    ring.finish()
    own = partial.at[y]
    total(dense_sum, [r.at[pl.ds(slots, tokens)] for r in (own, from_left, from_right)])
    total(own.at[pl.ds(0, slots)], [r.at[pl.ds(0, slots)] for r in (own, from_left, from_right)])
    block = 2 * slots // (SIDE * SIDE)
    short = block // 2
    row = lax.broadcasted_iota(jnp.int32, (2 * slots, slots), 0)
    col = lax.broadcasted_iota(jnp.int32, (2 * slots, slots), 1)
    place_in = lax.rem(row, block)
    second = (place_in >= short).astype(jnp.int32)
    source = lax.div(row, block) * short + place_in - second * short
    hit = (col == source).astype(jnp.int32)
    tables = [(hit * (1 - second)).astype(F32).astype(BF16), (hit * second).astype(F32).astype(BF16)]
    width = 256
    columns = parted.shape[1]

    def cut(i, carry):
        cols = pl.multiple_of(i * width, width)
        value = jnp.dot(
            tables[0], own[pl.ds(0, slots), pl.ds(cols, width)], preferred_element_type=F32
        )
        value = value + jnp.dot(
            tables[1], own[pl.ds(0, slots), pl.ds(cols + columns, width)], preferred_element_type=F32
        )
        parted[:, pl.ds(cols, width)] = value.astype(BF16)
        return carry

    lax.fori_loop(0, columns // width, cut, 0)

    def rows_of(ref, index):
        return ref.at[pl.ds(pl.multiple_of(index * block, block), block)]

    returned = [net.start(rows_of(parted, peer[0]), rows_of(back, node), peer) for peer in peers]
    keep = pltpu.make_async_copy(rows_of(parted, node), rows_of(back, node), local_sems.at[8])
    keep.start()
    keep.wait()
    for copy in share_back + returned:
        copy.wait_recv()
    net.drain()


def return_rows(routed, dense, shares):
    count = SIDE * CORES
    width = routed.shape[1]
    slots = routed.shape[0] // count
    tokens = dense.shape[0] // count
    nodes = SIDE * SIDE
    rows = slots + tokens
    return pl.pallas_call(
        return_kernel,
        out_shape=[
            jax.ShapeDtypeStruct((2 * slots, width // 2), BF16),
            jax.ShapeDtypeStruct((tokens, width), F32),
            jax.ShapeDtypeStruct((nodes,) + shares.shape, F32),
        ],
        in_specs=[ANY, ANY, VMEM],
        out_specs=[VMEM] * 3,
        scratch_shapes=[
            pltpu.VMEM((SIDE, rows, width), BF16),
            pltpu.VMEM((SIDE, rows, width), BF16),
            pltpu.VMEM((rows, width), BF16),
            pltpu.VMEM((rows, width), BF16),
            pltpu.VMEM((rows, width), BF16),
            pltpu.VMEM((2 * slots, width // 2), BF16),
            pltpu.VMEM((count,) + shares.shape, F32),
            pltpu.VMEM(shares.shape, F32),
            pltpu.SemaphoreType.DMA((RETURN_COPIES,)),
            pltpu.SemaphoreType.DMA((RETURN_COPIES,)),
            pltpu.SemaphoreType.DMA((9,)),
        ],
        compiler_params=pltpu.CompilerParams(
            collective_id=2, has_side_effects=True, vmem_limit_bytes=48 << 20
        ),
        name="return_rows",
    )(routed, dense, shares)


def silu_parts(pre_gate):
    sigma = jax.nn.sigmoid(pre_gate)
    return (pre_gate * sigma, sigma * (1.0 + pre_gate * (1.0 - sigma)))


def contract_rows(first_mat, second_mat):
    return lax.dot_general(
        first_mat, second_mat, (((0,), (0,)), ((), ())), preferred_element_type=F32
    ).astype(BF16)


def contract_last(first_mat, second_mat):
    return lax.dot_general(
        first_mat, second_mat, (((1,), (1,)), ((), ())), preferred_element_type=F32
    )


def unit_grads(rows_x, rows_dy, w_gate, w_up, w_down):
    pre_gate = jnp.dot(rows_x, w_gate, preferred_element_type=F32)
    pre_up = jnp.dot(rows_x, w_up, preferred_element_type=F32)
    hidden_grad = jnp.dot(rows_dy, w_down, preferred_element_type=F32)
    activated, derivative = silu_parts(pre_gate)
    hidden = activated * pre_up
    gate_part = (hidden_grad * pre_up * derivative).astype(BF16)
    up_part = (hidden_grad * activated).astype(BF16)
    return hidden, hidden_grad, gate_part, up_part


def input_term(gate_part, up_part, w_gate, w_up):
    return (contract_last(gate_part, w_gate) + contract_last(up_part, w_up)).astype(BF16)


def local(
    tokens, out_grad, gate_weights, expert_ids, dense_gate, dense_up, dense_down,
    expert_gate, expert_up, expert_down,
):
    tok_dev, width = tokens.shape
    nodes = SIDE * SIDE
    capacity = 4 * tok_dev // nodes
    block = 2 * capacity
    flat_ids = expert_ids.reshape(-1)
    pair = jnp.arange(2 * tok_dev, dtype=jnp.int32)
    earlier = (flat_ids[:, None] == flat_ids[None, :]) & (pair[None, :] < pair[:, None])
    slot_index = jnp.sum(earlier.astype(jnp.int32), axis=1)
    position = (flat_ids * block + slot_index).reshape(tok_dev, 2)
    row = jnp.arange(nodes * block, dtype=jnp.int32)[None, :, None]
    first_hit = (row == position[:, None, :]).astype(F32)
    second_hit = (row == position[:, None, :] + capacity).astype(F32)
    first_table = jnp.sum(first_hit, axis=2).astype(BF16)
    second_table = jnp.sum(second_hit, axis=2).astype(BF16)
    weight_table = jnp.sum(second_hit * gate_weights.astype(F32)[:, None, :], axis=2).astype(BF16)
    outgoing = lax.dot_general(
        jnp.concatenate([first_table, weight_table], axis=0),
        jnp.concatenate([tokens, out_grad], axis=0),
        (((0,), (0,)), ((), ())),
        preferred_element_type=F32,
    ).astype(BF16)
    node_rows, node_grad, rows_x, rows_dy = gather_rows(tokens, out_grad, outgoing)

    hidden, unused, gate_part, up_part = unit_grads(
        node_rows, node_grad, dense_gate, dense_up, dense_down
    )
    dense_input = input_term(gate_part, up_part, dense_gate, dense_up)
    both = contract_rows(node_rows, jnp.concatenate([gate_part, up_part], axis=1))
    down = contract_rows(node_grad, hidden.astype(BF16))
    dense_gate_grad, dense_up_grad, dense_down_grad = sum_weights(both, down)

    w_gate, w_up, w_down = expert_gate[0], expert_up[0], expert_down[0]
    hidden, hidden_grad, gate_part, up_part = unit_grads(rows_x, rows_dy, w_gate, w_up, w_down)
    shares = jnp.sum(hidden * hidden_grad, axis=1).reshape(SIDE * CORES, nodes * capacity)
    routed_input = input_term(gate_part, up_part, w_gate, w_up)
    back, dense_sum, back_shares = return_rows(routed_input, dense_input, shares)
    gate_grad = contract_rows(rows_x, gate_part)
    up_grad = contract_rows(rows_x, up_part)
    down_grad = contract_rows(rows_dy, hidden.astype(BF16))

    picked = jnp.concatenate(
        [
            jnp.dot(first_table, back, preferred_element_type=F32),
            jnp.dot(second_table, back, preferred_element_type=F32),
        ],
        axis=1,
    )
    input_grad = (out_grad.astype(F32) + dense_sum + picked).astype(BF16)
    node, tensor = lax.axis_index("node"), lax.axis_index("tensor")
    mine = lax.dynamic_slice(
        back_shares, (0, tensor, node * capacity), (nodes, 1, capacity)
    ).reshape(1, 1, nodes, capacity)
    expert = jnp.arange(nodes, dtype=jnp.int32)[None, None, :, None]
    slot = jnp.arange(capacity, dtype=jnp.int32)[None, None, None, :]
    chosen = (expert == expert_ids[:, :, None, None]) & (
        slot == slot_index.reshape(tok_dev, 2)[:, :, None, None]
    )
    weighted = jnp.sum(jnp.where(chosen, mine, 0.0), axis=(2, 3))
    gate_weight_grad = weighted / gate_weights.astype(F32)
    return (
        input_grad,
        gate_weight_grad,
        dense_gate_grad,
        dense_up_grad,
        dense_down_grad,
        gate_grad[None],
        up_grad[None],
        down_grad[None],
    )


def solution(mesh):
    rows = P(("node", "tensor"), None)
    dense = P(None, "tensor")
    expert = P("node", None, "tensor")
    summed = P("node", "tensor")
    return jax.shard_map(
        local,
        mesh=mesh,
        in_specs=(rows,) * 4 + (dense,) * 3 + (expert,) * 3,
        out_specs=(rows, rows) + (summed,) * 3 + (expert,) * 3,
        check_vma=False,
    )
```

```python
import jax
import jax.numpy as jnp
from jax import lax
from jax.experimental import pallas as pl
from jax.experimental.pallas import tpu as pltpu
from jax.sharding import PartitionSpec as P

MESH = pl.DeviceIdType.MESH
BF16 = jnp.bfloat16
F32 = jnp.float32
SIDE = 4
CORES = 2
ANY = pl.BlockSpec(memory_space=pl.ANY)
VMEM = pl.BlockSpec(memory_space=pltpu.VMEM)


def place():
    node = lax.axis_index("node")
    tensor = lax.axis_index("tensor")
    return (
        lax.div(node, SIDE),
        lax.rem(node, SIDE),
        lax.div(tensor, CORES),
        lax.rem(tensor, CORES),
    )


def turn(position, steps):
    return lax.rem(position + steps, SIDE)


def meet(peers):
    barrier = pltpu.get_barrier_semaphore()
    for peer in peers:
        pl.semaphore_signal(barrier, inc=1, device_id=peer, device_id_type=MESH)
    pl.semaphore_wait(barrier, len(peers))


class Net:
    def __init__(self, send_sems, recv_sems):
        self.send_sems, self.recv_sems = send_sems, recv_sems
        self.copies = []

    def start(self, src, dst, peer):
        index = len(self.copies)
        copy = pltpu.make_async_remote_copy(
            src_ref=src,
            dst_ref=dst,
            send_sem=self.send_sems.at[index],
            recv_sem=self.recv_sems.at[index],
            device_id=peer,
            device_id_type=MESH,
        )
        copy.start()
        self.copies.append(copy)
        return copy

    def drain(self):
        for copy in self.copies:
            copy.wait_send()


def total(dst, sources, scale=None, slab=16):
    rows = dst.shape[-2]
    leads = [()]
    for size in dst.shape[:-2]:
        leads = [lead + (i,) for lead in leads for i in range(size)]
    for lead in leads:

        def body(i, carry, lead=lead):
            at = lead + (pl.ds(pl.multiple_of(i * slab, slab), slab), slice(None))
            value = sources[0][at].astype(F32)
            for source in sources[1:]:
                value = value + source[at].astype(F32)
            if scale is not None:
                value = value * scale
            dst[at] = value.astype(dst.dtype)
            return carry

        lax.fori_loop(0, rows // slab, body, 0)


def node_peers(x, z, tensor):
    peers = []
    for dx in range(SIDE):
        for dz in range(SIDE):
            if dx or dz:
                peers.append((turn(x, dx) * SIDE + turn(z, dz), tensor))
    return peers


class Gather:
    def __init__(self, net, node, y, core, own, whole, rows):
        self.net, self.own, self.whole, self.rows = net, own, whole, rows
        self.me = y * CORES + core
        self.right_at = turn(y, 1) * CORES + core
        self.left_at = turn(y, SIDE - 1) * CORES + core
        self.far_at = turn(y, 2) * CORES + core
        self.right = (node, self.right_at)
        self.left = (node, self.left_at)
        self.partner = (node, y * CORES + 1 - core)
        self.crossed = {}

    def chunk(self, half, at):
        return self.whole[half].at[pl.ds(pl.multiple_of(at * self.rows, self.rows), self.rows)]

    def pass_on(self, half, at, name):
        ref = self.chunk(half, at)
        self.crossed[name, half] = self.net.start(ref, ref, self.partner)

    def start(self):
        send = self.net.start
        me, own = self.me, self.own
        self.to_right, self.to_left = [None] * 2, [None] * 2
        for step in range(2):
            self.to_right[step] = send(own[step], self.chunk(step, me), self.right)
            self.to_left[1 - step] = send(own[1 - step], self.chunk(1 - step, me), self.left)
        for half in range(2):
            self.crossed["own", half] = send(own[half], self.chunk(half, me), self.partner)

    def relay(self):
        send = self.net.start
        left_at, right_at = self.left_at, self.right_at
        self.to_right[0].wait_recv()
        self.relay_right = send(self.chunk(0, left_at), self.chunk(0, left_at), self.right)
        self.pass_on(0, left_at, "left")
        self.to_left[1].wait_recv()
        self.relay_left = send(self.chunk(1, right_at), self.chunk(1, right_at), self.left)
        self.pass_on(1, right_at, "right")

    def relay_rest(self):
        self.to_right[1].wait_recv()
        self.pass_on(1, self.left_at, "left")
        self.to_left[0].wait_recv()
        self.pass_on(0, self.right_at, "right")

    def relay_far(self):
        self.relay_right.wait_recv()
        self.pass_on(0, self.far_at, "far")
        self.relay_left.wait_recv()
        self.pass_on(1, self.far_at, "far")

    def arrive(self, name):
        for half in range(2):
            self.crossed[name, half].wait_recv()


class RingSum:
    def __init__(self, net, position, right, left, part, relayed, from_left, from_right):
        self.net, self.right, self.left, self.part = net, right, left, part
        self.relayed, self.from_left, self.from_right = relayed, from_left, from_right
        self.ahead, self.far, self.behind = (turn(position, k) for k in (1, 2, 3))

    def start_far(self):
        send, part = self.net.start, self.part
        self.relay_right = send(part(self.far, 0), self.relayed(0), self.right)
        self.relay_left = send(part(self.far, 1), self.relayed(1), self.left)

    def start_ahead(self):
        self.direct_right = self.net.start(self.part(self.ahead, 1), self.from_left(1), self.right)

    def start_behind(self):
        self.direct_left = self.net.start(self.part(self.behind, 0), self.from_right(0), self.left)

    def middle(self):
        send, part = self.net.start, self.part
        self.relay_right.wait_recv()
        mine = part(self.ahead, 0)
        total(mine, [mine, self.relayed(0)])
        self.sum_right = send(mine, self.from_left(0), self.right)
        self.relay_left.wait_recv()
        mine = part(self.behind, 1)
        total(mine, [mine, self.relayed(1)])
        self.sum_left = send(mine, self.from_right(1), self.left)

    def finish(self):
        for copy in (self.direct_right, self.direct_left, self.sum_right, self.sum_left):
            copy.wait_recv()


NT = (((1,), (1,)), ((), ()))
TN = (((0,), (0,)), ((), ()))
TILE = 512
FORWARD_COPIES = 2 * 14 + 15 + 24


def silu_parts(pre_gate):
    sigma = jax.nn.sigmoid(pre_gate)
    return (pre_gate * sigma, sigma * (1.0 + pre_gate * (1.0 - sigma)))


def unit_grads(rows_x, rows_dy, w_both, w_down, parts, hidden_out):
    hid = w_down.shape[1]
    pre = jnp.dot(rows_x[...], w_both[...], preferred_element_type=F32)
    hidden_grad = jnp.dot(rows_dy[...], w_down[...], preferred_element_type=F32)
    pre_up = pre[:, hid:]
    activated, derivative = silu_parts(pre[:, :hid])
    hidden = activated * pre_up
    parts[:, pl.ds(0, hid)] = (hidden_grad * pre_up * derivative).astype(BF16)
    parts[:, pl.ds(hid, hid)] = (hidden_grad * activated).astype(BF16)
    hidden_out[...] = hidden.astype(BF16)
    return hidden * hidden_grad


def input_term(parts, w_both, out):
    def body(i, carry):
        cols = pl.ds(pl.multiple_of(i * TILE, TILE), TILE)
        out[:, cols] = lax.dot_general(
            parts[...], w_both[cols], NT, preferred_element_type=F32
        ).astype(BF16)
        return carry

    lax.fori_loop(0, out.shape[1] // TILE, body, 0)


def lane_sums(value):
    high = value.astype(BF16)
    low = (value - high.astype(F32)).astype(BF16)
    ones = jnp.ones((8, value.shape[1]), BF16)
    return lax.dot_general(ones, high, NT, preferred_element_type=F32) + lax.dot_general(
        ones, low, NT, preferred_element_type=F32
    )


class WeightSums:
    def __init__(self, net, x, z, tensor, grads, first_bufs, second_bufs):
        self.net, self.x, self.z, self.grads = net, x, z, grads
        self.half = half = grads.shape[2] // 2
        self.first_bufs, self.second_bufs = first_bufs, second_bufs
        pairs = SIDE // 2

        def at(xx, zz):
            return (xx * SIDE + zz, tensor)

        self.around_x = (at(turn(x, 1), z), at(turn(x, 3), z))
        self.around_z = (at(x, turn(z, 1)), at(x, turn(z, 3)))

        def x_part(position, h):
            return grads.at[position, pl.ds(h * pairs, pairs), pl.ds(0, half)]

        def z_part(position, h):
            return grads.at[pl.ds(h * pairs, pairs), position, pl.ds(half, half)]

        def slot(ref, index):
            return lambda h: ref.at[index, pl.ds(h * pairs, pairs)]

        self.rings = [
            RingSum(net, x, *self.around_x, x_part, *(slot(ref, 0) for ref in first_bufs)),
            RingSum(net, z, *self.around_z, z_part, *(slot(ref, 1) for ref in first_bufs)),
        ]

    def middle(self):
        for ring in self.rings:
            ring.middle()

    def second(self):
        half = self.half
        cut = (0, half // 32 * 16 + 16, half)
        unused, from_left, from_right = self.first_bufs

        def rows_half(h):
            return pl.ds(cut[h], cut[h + 1] - cut[h])

        def summed(index):
            return lambda position, h: from_left.at[index, position, rows_half(h)]

        def slot(ref, index):
            return lambda h: ref.at[index, rows_half(h)]

        later = [
            RingSum(self.net, self.z, *self.around_z, summed(0), *(slot(r, 0) for r in self.second_bufs)),
            RingSum(self.net, self.x, *self.around_x, summed(1), *(slot(r, 1) for r in self.second_bufs)),
        ]
        for ring in self.rings:
            ring.finish()
        for steps in (2, 1, 3, 0):
            for index, ring in enumerate(later):
                other = turn((self.z, self.x)[index], steps)
                if index == 0:
                    mine = self.grads.at[self.x, other, pl.ds(0, half)]
                else:
                    mine = self.grads.at[other, self.z, pl.ds(half, half)]
                left, right = from_left.at[index, other], from_right.at[index, other]
                total(left, [mine, left, right])
                if steps == 2:
                    ring.start_far()
                elif steps == 1:
                    ring.start_ahead()
                elif steps == 3:
                    ring.start_behind()
        self.rings = later

    def finish(self, outs):
        half = self.half
        from_left = self.first_bufs[1]
        unused, from_left2, from_right2 = self.second_bufs
        for index, ring in enumerate(self.rings):
            ring.finish()
            own = from_left.at[index, (self.z, self.x)[index]]
            for block, ref in enumerate(outs):
                cols = pl.ds(block * ref.shape[1], ref.shape[1])
                total(
                    ref.at[pl.ds(index * half, half)],
                    [own.at[:, cols], from_left2.at[index, :, cols], from_right2.at[index, :, cols]],
                    scale=1.0 / (SIDE * SIDE),
                )


def forward_kernel(
    tok, grad, outgoing, dense_gate, dense_up, dense_down, expert_gate, expert_up, expert_down,
    out_x, out_dy, out_parts, out_hidden, out_routed, out_dense, shares, out_gate, out_up, out_down,
    tok_all, grad_all, rows_x, rows_dy, landed, w_both, w_down, dense_parts, dense_hidden,
    dense_term, parts, hidden, term, grads, relayed, from_left, from_right,
    relayed2, from_left2, from_right2, send_sems, recv_sems, local_sems,
):
    x, z, y, core = place()
    node, tensor = x * SIDE + z, y * CORES + core
    net = Net(send_sems, recv_sems)
    peers = node_peers(x, z, tensor)
    local_rows, depth = tok.shape
    hid = w_down.shape[1]
    block = landed.shape[0] // (SIDE * SIDE)
    slots = landed.shape[0] // 2
    started = []

    def fetch(src, dst):
        copy = pltpu.make_async_copy(src, dst, local_sems.at[len(started)])
        copy.start()
        started.append(copy)
        return copy

    dense = Gather(net, node, y, core, (tok, grad), (tok_all, grad_all), local_rows)
    routed = Gather(net, node, y, core, None, (rows_x, rows_dy), slots)
    routed.own = [routed.chunk(h, tensor) for h in range(2)]
    sums = WeightSums(
        net, x, z, tensor, grads, (relayed, from_left, from_right),
        (relayed2, from_left2, from_right2),
    )
    meet(peers + [dense.right, dense.left, dense.partner])

    def rows_of(ref, index):
        return ref.at[pl.ds(pl.multiple_of(index * block, block), block)]

    def fetch_weights(gate, up, down):
        return [
            fetch(gate, w_both.at[:, pl.ds(0, hid)]),
            fetch(up, w_both.at[:, pl.ds(hid, hid)]),
            fetch(down, w_down),
        ]

    dense.start()
    arrivals = [net.start(rows_of(outgoing, peer[0]), rows_of(landed, node), peer) for peer in peers]
    kept = [
        fetch(rows_of(outgoing, node), rows_of(landed, node)),
        fetch(tok, dense.chunk(0, tensor)),
        fetch(grad, dense.chunk(1, tensor)),
    ] + fetch_weights(dense_gate, dense_up, dense_down)
    dense.relay()
    dense.relay_rest()
    for copy in arrivals:
        copy.wait_recv()
    kept[0].wait()
    row = lax.broadcasted_iota(jnp.int32, (2 * slots, 2 * slots), 0)
    col = lax.broadcasted_iota(jnp.int32, (2 * slots, 2 * slots), 1)
    half = block // 2
    second = (row >= slots).astype(jnp.int32)
    within = row - second * slots
    source = lax.div(within, half) * block + lax.rem(within, half) + second * half
    table = (col == source).astype(F32).astype(BF16)

    def part(i, carry):
        cols = pl.ds(pl.multiple_of(i * TILE, TILE), TILE)
        value = jnp.dot(table, landed[:, cols], preferred_element_type=F32).astype(BF16)
        routed.own[0][:, cols] = value[:slots]
        routed.own[1][:, cols] = value[slots:]
        return carry

    lax.fori_loop(0, depth // TILE, part, 0)
    routed.start()

    dense.relay_far()
    for name in ("own", "left", "right", "far"):
        dense.arrive(name)
    for copy in kept[1:]:
        copy.wait()
    unit_grads(tok_all, grad_all, w_both, w_down, dense_parts, dense_hidden)
    input_term(dense_parts, w_both, dense_term)
    leaving = [fetch(dense_term, out_dense)]
    weights = fetch_weights(expert_gate, expert_up, expert_down)
    band = depth // SIDE
    x_ring, z_ring = sums.rings
    for steps in (2, 1, 3, 0):
        other = turn(x, steps)
        cols = pl.ds(pl.multiple_of(other * band, band), band)
        value = lax.dot_general(
            tok_all[:, cols], dense_parts[...], TN, preferred_element_type=F32
        ).astype(BF16)
        grads[other, :, :, pl.ds(0, 2 * hid)] = value.reshape(SIDE, band // SIDE, 2 * hid)
        value = lax.dot_general(
            grad_all[:, cols], dense_hidden[...], TN, preferred_element_type=F32
        ).astype(BF16)
        grads[other, :, :, pl.ds(2 * hid, hid)] = value.reshape(SIDE, band // SIDE, hid)
        if steps == 2:
            x_ring.start_far()
        elif steps == 1:
            x_ring.start_ahead()
        elif steps == 3:
            x_ring.start_behind()
    z_ring.start_far()
    z_ring.start_ahead()
    z_ring.start_behind()
    for copy in weights:
        copy.wait()

    pair = CORES * slots
    held = [None, None]

    def expert_rows(which, at):
        rows = pl.ds(pl.multiple_of(at * pair, pair), pair)
        leaving.append(fetch(rows_x.at[rows], out_x.at[rows]))
        leaving.append(fetch(rows_dy.at[rows], out_dy.at[rows]))
        product = unit_grads(
            rows_x.at[rows], rows_dy.at[rows], w_both, w_down, parts.at[rows], hidden.at[rows]
        )
        shares[at] = lane_sums(product)
        if held[which] is not None:
            held[which].wait()
        input_term(parts.at[rows], w_both, term.at[which])
        held[which] = fetch(term.at[which], out_routed.at[rows])

    routed.arrive("own")
    expert_rows(0, y)
    routed.relay()
    routed.relay_rest()
    sums.middle()
    routed.arrive("left")
    expert_rows(1, turn(y, 3))
    routed.arrive("right")
    sums.second()
    expert_rows(0, turn(y, 1))
    routed.relay_far()
    sums.middle()
    routed.arrive("far")
    expert_rows(1, turn(y, 2))
    sums.finish((out_gate, out_up, out_down))
    leaving += [fetch(parts, out_parts), fetch(hidden, out_hidden)] + held
    for copy in leaving:
        copy.wait()
    net.drain()


def forward(tokens, out_grad, outgoing, dense, expert):
    rows, depth = tokens.shape
    hid = dense[0].shape[1]
    count = SIDE * CORES
    slots = outgoing.shape[0] // 2
    node_rows, slot_rows = count * rows, count * slots
    own = depth // (SIDE * SIDE)
    bands = (2, SIDE, own // 2, 3 * hid)
    shape = jax.ShapeDtypeStruct
    return pl.pallas_call(
        forward_kernel,
        out_shape=[
            shape((slot_rows, depth), BF16),
            shape((slot_rows, depth), BF16),
            shape((slot_rows, 2 * hid), BF16),
            shape((slot_rows, hid), BF16),
            shape((slot_rows, depth), BF16),
            shape((node_rows, depth), BF16),
            shape((SIDE, 8, CORES * slots), F32),
        ]
        + [shape((own, hid), BF16)] * 3,
        in_specs=[ANY] * 9,
        out_specs=[ANY] * 6 + [VMEM] * 4,
        scratch_shapes=[
            pltpu.VMEM((node_rows, depth), BF16),
            pltpu.VMEM((node_rows, depth), BF16),
            pltpu.VMEM((slot_rows, depth), BF16),
            pltpu.VMEM((slot_rows, depth), BF16),
            pltpu.VMEM(outgoing.shape, BF16),
            pltpu.VMEM((depth, 2 * hid), BF16),
            pltpu.VMEM((depth, hid), BF16),
            pltpu.VMEM((node_rows, 2 * hid), BF16),
            pltpu.VMEM((node_rows, hid), BF16),
            pltpu.VMEM((node_rows, depth), BF16),
            pltpu.VMEM((slot_rows, 2 * hid), BF16),
            pltpu.VMEM((slot_rows, hid), BF16),
            pltpu.VMEM((2, CORES * slots, depth), BF16),
            pltpu.VMEM((SIDE, SIDE, own, 3 * hid), BF16),
        ]
        + [pltpu.VMEM(bands, BF16)] * 3
        + [pltpu.VMEM((2,) + bands[2:], BF16)] * 3
        + [
            pltpu.SemaphoreType.DMA((FORWARD_COPIES,)),
            pltpu.SemaphoreType.DMA((FORWARD_COPIES,)),
            pltpu.SemaphoreType.DMA((32,)),
        ],
        compiler_params=pltpu.CompilerParams(
            collective_id=0, has_side_effects=True, vmem_limit_bytes=62 << 20
        ),
        name="forward",
    )(tokens, out_grad, outgoing, *dense, *expert)


RETURN_COPIES = 8 + 6 + 15 + 7 + 15


def return_kernel(
    routed, dense, shares, in_x, in_dy, in_parts, in_hidden,
    back, dense_sum, back_shares, gate_grad, up_grad, down_grad,
    partial, from_core, relayed, from_left, from_right, parted, share_in, share_sum,
    rows_x, rows_dy, parts, hidden, tiles, send_sems, recv_sems, local_sems,
):
    x, z, y, core = place()
    node, tensor = x * SIDE + z, y * CORES + core
    net = Net(send_sems, recv_sems)
    peers = node_peers(x, z, tensor)
    count = SIDE * CORES
    mates = [(node, lax.rem(tensor + k, count)) for k in range(1, count)]
    partner = (node, y * CORES + 1 - core)
    right = (node, turn(y, 1) * CORES + core)
    left = (node, turn(y, 3) * CORES + core)
    slots = routed.shape[0] // count
    tokens = dense.shape[0] // count
    rows = slots + tokens
    meet(peers + mates)

    def routed_chunk(at):
        return routed.at[pl.ds(pl.multiple_of(at * slots, slots), slots)]

    def dense_chunk(at):
        return dense.at[pl.ds(pl.multiple_of(at * tokens, tokens), tokens)]

    order = [turn(y, k) for k in (2, 1, 3, 0)]
    crossed = []
    mine = []
    used = [9]

    def fetch(src, dst):
        copy = pltpu.make_async_copy(src, dst, local_sems.at[used[0]])
        copy.start()
        used[0] += 1
        return copy

    for k, other in enumerate(order):
        theirs = other * CORES + 1 - core
        crossed.append(
            (
                net.start(routed_chunk(theirs), from_core.at[other, pl.ds(0, slots)], partner),
                net.start(dense_chunk(theirs), from_core.at[other, pl.ds(slots, tokens)], partner),
            )
        )
        ours = other * CORES + core
        mine.append(
            (
                pltpu.make_async_copy(
                    routed_chunk(ours), partial.at[other, pl.ds(0, slots)], local_sems.at[2 * k]
                ),
                pltpu.make_async_copy(
                    dense_chunk(ours),
                    partial.at[other, pl.ds(slots, tokens)],
                    local_sems.at[2 * k + 1],
                ),
            )
        )
        for copy in mine[-1]:
            copy.start()
    share_copies = [
        net.start(shares.at[lax.div(mate[1], CORES)], share_in.at[tensor], mate) for mate in mates
    ]
    count_tiles = routed.shape[1] // TILE
    hid = hidden.shape[1]
    loads = [[fetch(in_parts, parts), fetch(in_hidden, hidden)]]
    for i in range(count_tiles):
        cols = pl.ds(i * TILE, TILE)
        loads.append(
            [fetch(in_x.at[:, cols], rows_x.at[:, cols]), fetch(in_dy.at[:, cols], rows_dy.at[:, cols])]
        )
    written = []

    def weight_tiles(first, last):
        for i in range(first, last):
            for copy in (loads[0] if i == 0 else []) + loads[i + 1]:
                copy.wait()
            if i >= 2:
                for copy in written[i - 2]:
                    copy.wait()
            cols, tile = pl.ds(i * TILE, TILE), tiles.at[i % 2]
            tile[:, pl.ds(0, 2 * hid)] = lax.dot_general(
                rows_x[:, cols], parts[...], TN, preferred_element_type=F32
            ).astype(BF16)
            tile[:, pl.ds(2 * hid, hid)] = lax.dot_general(
                rows_dy[:, cols], hidden[...], TN, preferred_element_type=F32
            ).astype(BF16)
            written.append(
                [
                    fetch(tile.at[:, pl.ds(k * hid, hid)], out.at[cols])
                    for k, out in enumerate((gate_grad, up_grad, down_grad))
                ]
            )

    half = rows // 2

    def in_half(ref):
        return lambda h: ref.at[pl.ds(h * half, half)]

    def part(position, h):
        return partial.at[position, pl.ds(h * half, half)]

    ring = RingSum(net, y, right, left, part, in_half(relayed), in_half(from_left), in_half(from_right))
    for k, other in enumerate(order):
        for copy in mine[k]:
            copy.wait()
        for copy in crossed[k]:
            copy.wait_recv()
        total(partial.at[other], [partial.at[other], from_core.at[other]])
        (ring.start_far, ring.start_ahead, ring.start_behind, lambda: None)[k]()
    weight_tiles(0, 1)
    for copy in share_copies:
        copy.wait_recv()
    value = shares[y]
    for k in range(1, count):
        value = value + share_in[lax.rem(tensor + k, count)]
    share_sum[...] = value
    back_shares[node] = value
    share_back = [net.start(share_sum, back_shares.at[node], peer) for peer in peers]
    weight_tiles(1, 4)
    ring.middle()
    weight_tiles(4, 6)
    ring.finish()
    own = partial.at[y]
    total(dense_sum, [r.at[pl.ds(slots, tokens)] for r in (own, from_left, from_right)])
    total(own.at[pl.ds(0, slots)], [r.at[pl.ds(0, slots)] for r in (own, from_left, from_right)])
    block = 2 * slots // (SIDE * SIDE)
    short = block // 2
    row = lax.broadcasted_iota(jnp.int32, (2 * slots, slots), 0)
    col = lax.broadcasted_iota(jnp.int32, (2 * slots, slots), 1)
    place_in = lax.rem(row, block)
    second = (place_in >= short).astype(jnp.int32)
    source = lax.div(row, block) * short + place_in - second * short
    hit = (col == source).astype(jnp.int32)
    tables = [(hit * (1 - second)).astype(F32).astype(BF16), (hit * second).astype(F32).astype(BF16)]
    width = 256
    columns = parted.shape[1]

    def cut(i, carry):
        cols = pl.multiple_of(i * width, width)
        value = jnp.dot(
            tables[0], own[pl.ds(0, slots), pl.ds(cols, width)], preferred_element_type=F32
        )
        value = value + jnp.dot(
            tables[1], own[pl.ds(0, slots), pl.ds(cols + columns, width)], preferred_element_type=F32
        )
        parted[:, pl.ds(cols, width)] = value.astype(BF16)
        return carry

    lax.fori_loop(0, columns // width, cut, 0)

    def rows_of(ref, index):
        return ref.at[pl.ds(pl.multiple_of(index * block, block), block)]

    returned = [net.start(rows_of(parted, peer[0]), rows_of(back, node), peer) for peer in peers]
    keep = pltpu.make_async_copy(rows_of(parted, node), rows_of(back, node), local_sems.at[8])
    keep.start()
    weight_tiles(6, count_tiles)
    keep.wait()
    for copies in written[-2:]:
        for copy in copies:
            copy.wait()
    for copy in share_back + returned:
        copy.wait_recv()
    net.drain()


def return_rows(routed, dense, shares, rows_x, rows_dy, parts, hidden):
    count = SIDE * CORES
    width = routed.shape[1]
    slots = routed.shape[0] // count
    tokens = dense.shape[0] // count
    nodes = SIDE * SIDE
    rows = slots + tokens
    return pl.pallas_call(
        return_kernel,
        out_shape=[
            jax.ShapeDtypeStruct((2 * slots, width // 2), BF16),
            jax.ShapeDtypeStruct((tokens, width), F32),
            jax.ShapeDtypeStruct((nodes,) + shares.shape[1:], F32),
        ]
        + [jax.ShapeDtypeStruct((width, hidden.shape[1]), BF16)] * 3,
        in_specs=[ANY, ANY, VMEM] + [ANY] * 4,
        out_specs=[VMEM] * 3 + [ANY] * 3,
        scratch_shapes=[
            pltpu.VMEM((SIDE, rows, width), BF16),
            pltpu.VMEM((SIDE, rows, width), BF16),
            pltpu.VMEM((rows, width), BF16),
            pltpu.VMEM((rows, width), BF16),
            pltpu.VMEM((rows, width), BF16),
            pltpu.VMEM((2 * slots, width // 2), BF16),
            pltpu.VMEM((count,) + shares.shape[1:], F32),
            pltpu.VMEM(shares.shape[1:], F32),
            pltpu.VMEM(rows_x.shape, BF16),
            pltpu.VMEM(rows_dy.shape, BF16),
            pltpu.VMEM(parts.shape, BF16),
            pltpu.VMEM(hidden.shape, BF16),
            pltpu.VMEM((2, TILE, 3 * hidden.shape[1]), BF16),
            pltpu.SemaphoreType.DMA((RETURN_COPIES,)),
            pltpu.SemaphoreType.DMA((RETURN_COPIES,)),
            pltpu.SemaphoreType.DMA((64,)),
        ],
        compiler_params=pltpu.CompilerParams(
            collective_id=1, has_side_effects=True, vmem_limit_bytes=60 << 20
        ),
        name="return_rows",
    )(routed, dense, shares, rows_x, rows_dy, parts, hidden)


def local(
    tokens, out_grad, gate_weights, expert_ids, dense_gate, dense_up, dense_down,
    expert_gate, expert_up, expert_down,
):
    tok_dev, width = tokens.shape
    nodes = SIDE * SIDE
    capacity = 4 * tok_dev // nodes
    block = 2 * capacity
    flat_ids = expert_ids.reshape(-1)
    pair = jnp.arange(2 * tok_dev, dtype=jnp.int32)
    earlier = (flat_ids[:, None] == flat_ids[None, :]) & (pair[None, :] < pair[:, None])
    slot_index = jnp.sum(earlier.astype(jnp.int32), axis=1)
    position = (flat_ids * block + slot_index).reshape(tok_dev, 2)
    row = jnp.arange(nodes * block, dtype=jnp.int32)[None, :, None]
    first_hit = (row == position[:, None, :]).astype(F32)
    second_hit = (row == position[:, None, :] + capacity).astype(F32)
    first_table = jnp.sum(first_hit, axis=2).astype(BF16)
    second_table = jnp.sum(second_hit, axis=2).astype(BF16)
    weight_table = jnp.sum(second_hit * gate_weights.astype(F32)[:, None, :], axis=2).astype(BF16)
    outgoing = lax.dot_general(
        jnp.concatenate([first_table, weight_table], axis=0),
        jnp.concatenate([tokens, out_grad], axis=0),
        (((0,), (0,)), ((), ())),
        preferred_element_type=F32,
    ).astype(BF16)
    (
        rows_x, rows_dy, parts, hidden, routed_input, dense_input, shares,
        dense_gate_grad, dense_up_grad, dense_down_grad,
    ) = forward(
        tokens, out_grad, outgoing, (dense_gate, dense_up, dense_down),
        (expert_gate[0], expert_up[0], expert_down[0]),
    )
    back, dense_sum, back_shares, gate_grad, up_grad, down_grad = return_rows(
        routed_input, dense_input, shares, rows_x, rows_dy, parts, hidden
    )

    picked = jnp.concatenate(
        [
            jnp.dot(first_table, back, preferred_element_type=F32),
            jnp.dot(second_table, back, preferred_element_type=F32),
        ],
        axis=1,
    )
    input_grad = (out_grad.astype(F32) + dense_sum + picked).astype(BF16)
    node, tensor = lax.axis_index("node"), lax.axis_index("tensor")
    start = lax.rem(tensor, CORES) * (nodes * capacity) + node * capacity
    mine = lax.dynamic_slice(back_shares, (0, 0, start), (nodes, 1, capacity)).reshape(1, 1, nodes, capacity)
    expert = jnp.arange(nodes, dtype=jnp.int32)[None, None, :, None]
    slot = jnp.arange(capacity, dtype=jnp.int32)[None, None, None, :]
    chosen = (expert == expert_ids[:, :, None, None]) & (
        slot == slot_index.reshape(tok_dev, 2)[:, :, None, None]
    )
    weighted = jnp.sum(jnp.where(chosen, mine, 0.0), axis=(2, 3))
    gate_weight_grad = weighted / gate_weights.astype(F32)
    return (
        input_grad,
        gate_weight_grad,
        dense_gate_grad,
        dense_up_grad,
        dense_down_grad,
        gate_grad[None],
        up_grad[None],
        down_grad[None],
    )


def solution(mesh):
    rows = P(("node", "tensor"), None)
    dense = P(None, "tensor")
    expert = P("node", None, "tensor")
    summed = P("node", "tensor")
    return jax.shard_map(
        local,
        mesh=mesh,
        in_specs=(rows,) * 4 + (dense,) * 3 + (expert,) * 3,
        out_specs=(rows, rows) + (summed,) * 3 + (expert,) * 3,
        check_vma=False,
    )
```

```python
import jax
import jax.numpy as jnp
from jax import lax
from jax.experimental import pallas as pl
from jax.experimental.pallas import tpu as pltpu
from jax.sharding import PartitionSpec as P

MESH = pl.DeviceIdType.MESH
BF16 = jnp.bfloat16
F32 = jnp.float32
SIDE = 4
CORES = 2
ANY = pl.BlockSpec(memory_space=pl.ANY)
VMEM = pl.BlockSpec(memory_space=pltpu.VMEM)


def place():
    node = lax.axis_index("node")
    tensor = lax.axis_index("tensor")
    return (
        lax.div(node, SIDE),
        lax.rem(node, SIDE),
        lax.div(tensor, CORES),
        lax.rem(tensor, CORES),
    )


def turn(position, steps):
    return lax.rem(position + steps, SIDE)


def meet(peers):
    barrier = pltpu.get_barrier_semaphore()
    for peer in peers:
        pl.semaphore_signal(barrier, inc=1, device_id=peer, device_id_type=MESH)
    pl.semaphore_wait(barrier, len(peers))


class Net:
    def __init__(self, send_sems, recv_sems):
        self.send_sems, self.recv_sems = send_sems, recv_sems
        self.copies = []

    def start(self, src, dst, peer):
        index = len(self.copies)
        copy = pltpu.make_async_remote_copy(
            src_ref=src,
            dst_ref=dst,
            send_sem=self.send_sems.at[index],
            recv_sem=self.recv_sems.at[index],
            device_id=peer,
            device_id_type=MESH,
        )
        copy.start()
        self.copies.append(copy)
        return copy

    def drain(self):
        for copy in self.copies:
            copy.wait_send()


def total(dst, sources, scale=None, slab=16):
    rows = dst.shape[-2]
    leads = [()]
    for size in dst.shape[:-2]:
        leads = [lead + (i,) for lead in leads for i in range(size)]
    for lead in leads:

        def body(i, carry, lead=lead):
            at = lead + (pl.ds(pl.multiple_of(i * slab, slab), slab), slice(None))
            value = sources[0][at].astype(F32)
            for source in sources[1:]:
                value = value + source[at].astype(F32)
            if scale is not None:
                value = value * scale
            dst[at] = value.astype(dst.dtype)
            return carry

        lax.fori_loop(0, rows // slab, body, 0)


def node_peers(x, z, tensor):
    peers = []
    for dx in range(SIDE):
        for dz in range(SIDE):
            if dx or dz:
                peers.append((turn(x, dx) * SIDE + turn(z, dz), tensor))
    return peers


class Gather:
    def __init__(self, net, node, y, core, own, whole, rows):
        self.net, self.own, self.whole, self.rows = net, own, whole, rows
        self.me = y * CORES + core
        self.right_at = turn(y, 1) * CORES + core
        self.left_at = turn(y, SIDE - 1) * CORES + core
        self.far_at = turn(y, 2) * CORES + core
        self.right = (node, self.right_at)
        self.left = (node, self.left_at)
        self.partner = (node, y * CORES + 1 - core)
        self.crossed, self.to_right, self.to_left = {}, {}, {}

    def chunk(self, half, at):
        return self.whole[half].at[pl.ds(pl.multiple_of(at * self.rows, self.rows), self.rows)]

    def pass_on(self, half, at, name):
        ref = self.chunk(half, at)
        self.crossed[name, half] = self.net.start(ref, ref, self.partner)

    def start(self, half):
        send = self.net.start
        mine, own = self.chunk(half, self.me), self.own[half]
        self.to_right[half] = send(own, mine, self.right)
        self.to_left[half] = send(own, mine, self.left)
        self.crossed["own", half] = send(own, mine, self.partner)

    def relay(self):
        send = self.net.start
        left_at, right_at = self.left_at, self.right_at
        self.to_right[0].wait_recv()
        self.relay_right = send(self.chunk(0, left_at), self.chunk(0, left_at), self.right)
        self.pass_on(0, left_at, "left")
        self.to_left[1].wait_recv()
        self.relay_left = send(self.chunk(1, right_at), self.chunk(1, right_at), self.left)
        self.pass_on(1, right_at, "right")

    def relay_rest(self):
        self.to_right[1].wait_recv()
        self.pass_on(1, self.left_at, "left")
        self.to_left[0].wait_recv()
        self.pass_on(0, self.right_at, "right")

    def relay_far(self):
        self.relay_right.wait_recv()
        self.pass_on(0, self.far_at, "far")
        self.relay_left.wait_recv()
        self.pass_on(1, self.far_at, "far")

    def arrive(self, name):
        for half in range(2):
            self.crossed[name, half].wait_recv()


class RingSum:
    def __init__(self, net, position, right, left, part, relayed, from_left, from_right):
        self.net, self.right, self.left, self.part = net, right, left, part
        self.relayed, self.from_left, self.from_right = relayed, from_left, from_right
        self.ahead, self.far, self.behind = (turn(position, k) for k in (1, 2, 3))

    def start_far(self):
        send, part = self.net.start, self.part
        self.relay_right = send(part(self.far, 0), self.relayed(0), self.right)
        self.relay_left = send(part(self.far, 1), self.relayed(1), self.left)

    def start_ahead(self):
        self.direct_right = self.net.start(self.part(self.ahead, 1), self.from_left(1), self.right)

    def start_behind(self):
        self.direct_left = self.net.start(self.part(self.behind, 0), self.from_right(0), self.left)

    def middle(self):
        send, part = self.net.start, self.part
        self.relay_right.wait_recv()
        mine = part(self.ahead, 0)
        total(mine, [mine, self.relayed(0)])
        self.sum_right = send(mine, self.from_left(0), self.right)
        self.relay_left.wait_recv()
        mine = part(self.behind, 1)
        total(mine, [mine, self.relayed(1)])
        self.sum_left = send(mine, self.from_right(1), self.left)

    def finish(self):
        for copy in (self.direct_right, self.direct_left, self.sum_right, self.sum_left):
            copy.wait_recv()


NT = (((1,), (1,)), ((), ()))
TN = (((0,), (0,)), ((), ()))
TILE = 512
HALF_TILE = 256
FORWARD_COPIES = 2 * 14 + 2 * 15 + 24


def silu_parts(pre_gate):
    sigma = jax.nn.sigmoid(pre_gate)
    return (pre_gate * sigma, sigma * (1.0 + pre_gate * (1.0 - sigma)))


def unit_grads(rows_x, rows_dy, w_both, w_down, parts, hidden_out):
    hid = w_down.shape[1]
    pre = jnp.dot(rows_x[...], w_both[...], preferred_element_type=F32)
    hidden_grad = jnp.dot(rows_dy[...], w_down[...], preferred_element_type=F32)
    pre_up = pre[:, hid:]
    activated, derivative = silu_parts(pre[:, :hid])
    hidden = activated * pre_up
    parts[:, pl.ds(0, hid)] = (hidden_grad * pre_up * derivative).astype(BF16)
    parts[:, pl.ds(hid, hid)] = (hidden_grad * activated).astype(BF16)
    hidden_out[...] = hidden.astype(BF16)
    return hidden * hidden_grad


def input_term(parts, w_both, out):
    def body(i, carry):
        cols = pl.ds(pl.multiple_of(i * TILE, TILE), TILE)
        out[:, cols] = lax.dot_general(
            parts[...], w_both[cols], NT, preferred_element_type=F32
        ).astype(BF16)
        return carry

    lax.fori_loop(0, out.shape[1] // TILE, body, 0)


def lane_sums(value):
    high = value.astype(BF16)
    low = (value - high.astype(F32)).astype(BF16)
    ones = jnp.ones((8, value.shape[1]), BF16)
    return lax.dot_general(ones, high, NT, preferred_element_type=F32) + lax.dot_general(
        ones, low, NT, preferred_element_type=F32
    )


class WeightSums:
    def __init__(self, net, x, z, tensor, grads, first_bufs, second_bufs):
        self.net, self.x, self.z, self.grads = net, x, z, grads
        self.half = half = grads.shape[2] // 2
        self.first_bufs, self.second_bufs = first_bufs, second_bufs
        pairs = SIDE // 2

        def at(xx, zz):
            return (xx * SIDE + zz, tensor)

        self.around_x = (at(turn(x, 1), z), at(turn(x, 3), z))
        self.around_z = (at(x, turn(z, 1)), at(x, turn(z, 3)))

        def x_part(position, h):
            return grads.at[position, pl.ds(h * pairs, pairs), pl.ds(0, half)]

        def z_part(position, h):
            return grads.at[pl.ds(h * pairs, pairs), position, pl.ds(half, half)]

        def slot(ref, index):
            return lambda h: ref.at[index, pl.ds(h * pairs, pairs)]

        self.rings = [
            RingSum(net, x, *self.around_x, x_part, *(slot(ref, 0) for ref in first_bufs)),
            RingSum(net, z, *self.around_z, z_part, *(slot(ref, 1) for ref in first_bufs)),
        ]

    def middle(self):
        for ring in self.rings:
            ring.middle()

    def second(self):
        half = self.half
        cut = (0, half // 32 * 16 + 16, half)
        unused, from_left, from_right = self.first_bufs

        def rows_half(h):
            return pl.ds(cut[h], cut[h + 1] - cut[h])

        def summed(index):
            return lambda position, h: from_left.at[index, position, rows_half(h)]

        def slot(ref, index):
            return lambda h: ref.at[index, rows_half(h)]

        later = [
            RingSum(self.net, self.z, *self.around_z, summed(0), *(slot(r, 0) for r in self.second_bufs)),
            RingSum(self.net, self.x, *self.around_x, summed(1), *(slot(r, 1) for r in self.second_bufs)),
        ]
        for ring in self.rings:
            ring.finish()
        for steps in (2, 1, 3, 0):
            for index, ring in enumerate(later):
                other = turn((self.z, self.x)[index], steps)
                if index == 0:
                    mine = self.grads.at[self.x, other, pl.ds(0, half)]
                else:
                    mine = self.grads.at[other, self.z, pl.ds(half, half)]
                left, right = from_left.at[index, other], from_right.at[index, other]
                total(left, [mine, left, right])
                if steps == 2:
                    ring.start_far()
                elif steps == 1:
                    ring.start_ahead()
                elif steps == 3:
                    ring.start_behind()
        self.rings = later

    def finish(self, outs):
        half = self.half
        from_left = self.first_bufs[1]
        unused, from_left2, from_right2 = self.second_bufs
        for index, ring in enumerate(self.rings):
            ring.finish()
            own = from_left.at[index, (self.z, self.x)[index]]
            for block, ref in enumerate(outs):
                cols = pl.ds(block * ref.shape[1], ref.shape[1])
                total(
                    ref.at[pl.ds(index * half, half)],
                    [own.at[:, cols], from_left2.at[index, :, cols], from_right2.at[index, :, cols]],
                    scale=1.0 / (SIDE * SIDE),
                )


def forward_kernel(
    tok, grad, first_table, second_table, first_weight, second_weight,
    dense_gate, dense_up, dense_down, expert_gate, expert_up, expert_down,
    out_x, out_dy, out_parts, out_hidden, out_routed, out_dense, shares, out_gate, out_up, out_down,
    tok_all, grad_all, rows_x, rows_dy, outgoing, landed, w_both, w_down, dense_parts, dense_hidden,
    dense_term, parts, hidden, term, grads, relayed, from_left, from_right,
    relayed2, from_left2, from_right2, send_sems, recv_sems, local_sems,
):
    x, z, y, core = place()
    node, tensor = x * SIDE + z, y * CORES + core
    net = Net(send_sems, recv_sems)
    peers = node_peers(x, z, tensor)
    local_rows, depth = tok.shape
    hid = w_down.shape[1]
    columns = landed.shape[2]
    block = landed.shape[1] // (SIDE * SIDE)
    slots = landed.shape[1] // 2
    started = []

    def fetch(src, dst):
        copy = pltpu.make_async_copy(src, dst, local_sems.at[len(started)])
        copy.start()
        started.append(copy)
        return copy

    dense = Gather(net, node, y, core, (tok, grad), (tok_all, grad_all), local_rows)
    routed = Gather(net, node, y, core, None, (rows_x, rows_dy), slots)
    routed.own = [routed.chunk(h, tensor) for h in range(2)]
    sums = WeightSums(
        net, x, z, tensor, grads, (relayed, from_left, from_right),
        (relayed2, from_left2, from_right2),
    )
    meet(peers + [dense.right, dense.left, dense.partner])

    def rows_of(ref, index):
        return ref.at[pl.ds(pl.multiple_of(index * block, block), block)]

    def fetch_weights(gate, up, down):
        return [
            fetch(gate, w_both.at[:, pl.ds(0, hid)]),
            fetch(up, w_both.at[:, pl.ds(hid, hid)]),
            fetch(down, w_down),
        ]

    dense.start(0)
    dense.start(1)
    exchanged = []
    for h, (source, left, right) in enumerate(
        ((tok, first_table, second_table), (grad, first_weight, second_weight))
    ):
        out, into = outgoing.at[h], landed.at[h]
        for first in range(0, columns, 2 * HALF_TILE):
            width = min(2 * HALF_TILE, columns - first)
            value = lax.dot_general(
                left[...], source[:, pl.ds(first, width)], TN, preferred_element_type=F32
            ) + lax.dot_general(
                right[...], source[:, pl.ds(columns + first, width)], TN, preferred_element_type=F32
            )
            out[:, pl.ds(first, width)] = value.astype(BF16)
        exchanged.append(
            [net.start(rows_of(out, peer[0]), rows_of(into, node), peer) for peer in peers]
            + [fetch(rows_of(out, node), rows_of(into, node))]
        )
    kept = [
        fetch(tok, dense.chunk(0, tensor)),
        fetch(grad, dense.chunk(1, tensor)),
    ] + fetch_weights(dense_gate, dense_up, dense_down)
    row = lax.broadcasted_iota(jnp.int32, (slots, 2 * slots), 0)
    col = lax.broadcasted_iota(jnp.int32, (slots, 2 * slots), 1)
    half = block // 2
    origin = lax.div(row, half) * block + lax.rem(row, half)
    tables = [(col == origin + k * half).astype(F32).astype(BF16) for k in range(2)]

    def join(h):
        for copy in exchanged[h][:-1]:
            copy.wait_recv()
        exchanged[h][-1].wait()
        own, into = routed.own[h], landed.at[h]
        for first in range(0, columns, 2 * HALF_TILE):
            width = min(2 * HALF_TILE, columns - first)
            cols = pl.ds(first, width)
            for k in range(2):
                own[:, pl.ds(k * columns + first, width)] = jnp.dot(
                    tables[k], into[:, cols], preferred_element_type=F32
                ).astype(BF16)

    dense.relay()
    dense.relay_rest()
    join(0)
    routed.start(0)
    dense.relay_far()
    join(1)
    routed.start(1)

    for name in ("own", "left", "right", "far"):
        dense.arrive(name)
    for copy in kept:
        copy.wait()
    unit_grads(tok_all, grad_all, w_both, w_down, dense_parts, dense_hidden)
    input_term(dense_parts, w_both, dense_term)
    leaving = [fetch(dense_term, out_dense)]
    weights = fetch_weights(expert_gate, expert_up, expert_down)
    band = depth // SIDE
    x_ring, z_ring = sums.rings
    for steps in (2, 1, 3, 0):
        other = turn(x, steps)
        cols = pl.ds(pl.multiple_of(other * band, band), band)
        value = lax.dot_general(
            tok_all[:, cols], dense_parts[...], TN, preferred_element_type=F32
        ).astype(BF16)
        grads[other, :, :, pl.ds(0, 2 * hid)] = value.reshape(SIDE, band // SIDE, 2 * hid)
        value = lax.dot_general(
            grad_all[:, cols], dense_hidden[...], TN, preferred_element_type=F32
        ).astype(BF16)
        grads[other, :, :, pl.ds(2 * hid, hid)] = value.reshape(SIDE, band // SIDE, hid)
        if steps == 2:
            x_ring.start_far()
        elif steps == 1:
            x_ring.start_ahead()
        elif steps == 3:
            x_ring.start_behind()
    z_ring.start_far()
    z_ring.start_ahead()
    z_ring.start_behind()
    for copy in weights:
        copy.wait()

    pair = CORES * slots
    held = [None, None]

    def expert_rows(which, at):
        rows = pl.ds(pl.multiple_of(at * pair, pair), pair)
        leaving.append(fetch(rows_x.at[rows], out_x.at[rows]))
        leaving.append(fetch(rows_dy.at[rows], out_dy.at[rows]))
        product = unit_grads(
            rows_x.at[rows], rows_dy.at[rows], w_both, w_down, parts.at[rows], hidden.at[rows]
        )
        shares[at] = lane_sums(product)
        if held[which] is not None:
            held[which].wait()
        input_term(parts.at[rows], w_both, term.at[which])
        held[which] = fetch(term.at[which], out_routed.at[rows])

    routed.arrive("own")
    expert_rows(0, y)
    routed.relay()
    routed.relay_rest()
    sums.middle()
    routed.arrive("left")
    expert_rows(1, turn(y, 3))
    routed.arrive("right")
    sums.second()
    expert_rows(0, turn(y, 1))
    routed.relay_far()
    sums.middle()
    routed.arrive("far")
    expert_rows(1, turn(y, 2))
    sums.finish((out_gate, out_up, out_down))
    leaving += [fetch(parts, out_parts), fetch(hidden, out_hidden)] + held
    for copy in leaving:
        copy.wait()
    net.drain()


def forward(tokens, out_grad, tables, dense, expert):
    rows, depth = tokens.shape
    hid = dense[0].shape[1]
    count = SIDE * CORES
    slots = tables[0].shape[1] // 2
    node_rows, slot_rows = count * rows, count * slots
    own = depth // (SIDE * SIDE)
    bands = (2, SIDE, own // 2, 3 * hid)
    shape = jax.ShapeDtypeStruct
    return pl.pallas_call(
        forward_kernel,
        out_shape=[
            shape((slot_rows, depth), BF16),
            shape((slot_rows, depth), BF16),
            shape((slot_rows, 2 * hid), BF16),
            shape((slot_rows, hid), BF16),
            shape((slot_rows, depth), BF16),
            shape((node_rows, depth), BF16),
            shape((SIDE, 8, CORES * slots), F32),
        ]
        + [shape((own, hid), BF16)] * 3,
        in_specs=[VMEM] * 6 + [ANY] * 6,
        out_specs=[ANY] * 6 + [VMEM] * 4,
        scratch_shapes=[
            pltpu.VMEM((node_rows, depth), BF16),
            pltpu.VMEM((node_rows, depth), BF16),
            pltpu.VMEM((slot_rows, depth), BF16),
            pltpu.VMEM((slot_rows, depth), BF16),
            pltpu.VMEM((2, 2 * slots, depth // 2), BF16),
            pltpu.VMEM((2, 2 * slots, depth // 2), BF16),
            pltpu.VMEM((depth, 2 * hid), BF16),
            pltpu.VMEM((depth, hid), BF16),
            pltpu.VMEM((node_rows, 2 * hid), BF16),
            pltpu.VMEM((node_rows, hid), BF16),
            pltpu.VMEM((node_rows, depth), BF16),
            pltpu.VMEM((slot_rows, 2 * hid), BF16),
            pltpu.VMEM((slot_rows, hid), BF16),
            pltpu.VMEM((2, CORES * slots, depth), BF16),
            pltpu.VMEM((SIDE, SIDE, own, 3 * hid), BF16),
        ]
        + [pltpu.VMEM(bands, BF16)] * 3
        + [pltpu.VMEM((2,) + bands[2:], BF16)] * 3
        + [
            pltpu.SemaphoreType.DMA((FORWARD_COPIES,)),
            pltpu.SemaphoreType.DMA((FORWARD_COPIES,)),
            pltpu.SemaphoreType.DMA((32,)),
        ],
        compiler_params=pltpu.CompilerParams(
            collective_id=0, has_side_effects=True, vmem_limit_bytes=62 << 20
        ),
        name="forward",
    )(tokens, out_grad, *tables, *dense, *expert)


RETURN_COPIES = 8 + 6 + 15 + 7 + 15


def return_kernel(
    routed, dense, shares, in_x, in_dy, in_parts, in_hidden,
    back, dense_sum, back_shares, gate_grad, up_grad, down_grad,
    partial, from_core, relayed, from_left, from_right, parted, share_in, share_sum,
    rows_x, rows_dy, parts, hidden, tiles, send_sems, recv_sems, local_sems,
):
    x, z, y, core = place()
    node, tensor = x * SIDE + z, y * CORES + core
    net = Net(send_sems, recv_sems)
    peers = node_peers(x, z, tensor)
    count = SIDE * CORES
    mates = [(node, lax.rem(tensor + k, count)) for k in range(1, count)]
    partner = (node, y * CORES + 1 - core)
    right = (node, turn(y, 1) * CORES + core)
    left = (node, turn(y, 3) * CORES + core)
    slots = routed.shape[0] // count
    tokens = dense.shape[0] // count
    rows = slots + tokens
    meet(peers + mates)

    def routed_chunk(at):
        return routed.at[pl.ds(pl.multiple_of(at * slots, slots), slots)]

    def dense_chunk(at):
        return dense.at[pl.ds(pl.multiple_of(at * tokens, tokens), tokens)]

    order = [turn(y, k) for k in (2, 1, 3, 0)]
    crossed = []
    mine = []
    used = [9]

    def fetch(src, dst):
        copy = pltpu.make_async_copy(src, dst, local_sems.at[used[0]])
        copy.start()
        used[0] += 1
        return copy

    for k, other in enumerate(order):
        theirs = other * CORES + 1 - core
        crossed.append(
            (
                net.start(routed_chunk(theirs), from_core.at[other, pl.ds(0, slots)], partner),
                net.start(dense_chunk(theirs), from_core.at[other, pl.ds(slots, tokens)], partner),
            )
        )
        ours = other * CORES + core
        mine.append(
            (
                pltpu.make_async_copy(
                    routed_chunk(ours), partial.at[other, pl.ds(0, slots)], local_sems.at[2 * k]
                ),
                pltpu.make_async_copy(
                    dense_chunk(ours),
                    partial.at[other, pl.ds(slots, tokens)],
                    local_sems.at[2 * k + 1],
                ),
            )
        )
        for copy in mine[-1]:
            copy.start()
    share_copies = [
        net.start(shares.at[lax.div(mate[1], CORES)], share_in.at[tensor], mate) for mate in mates
    ]
    count_tiles = routed.shape[1] // TILE
    hid = hidden.shape[1]
    loads = [[fetch(in_parts, parts), fetch(in_hidden, hidden)]]
    for i in range(count_tiles):
        cols = pl.ds(i * TILE, TILE)
        loads.append(
            [fetch(in_x.at[:, cols], rows_x.at[:, cols]), fetch(in_dy.at[:, cols], rows_dy.at[:, cols])]
        )
    written = []

    def weight_tiles(first, last):
        for i in range(first, last):
            for copy in (loads[0] if i == 0 else []) + loads[i + 1]:
                copy.wait()
            if i >= 2:
                for copy in written[i - 2]:
                    copy.wait()
            cols, tile = pl.ds(i * TILE, TILE), tiles.at[i % 2]
            tile[:, pl.ds(0, 2 * hid)] = lax.dot_general(
                rows_x[:, cols], parts[...], TN, preferred_element_type=F32
            ).astype(BF16)
            tile[:, pl.ds(2 * hid, hid)] = lax.dot_general(
                rows_dy[:, cols], hidden[...], TN, preferred_element_type=F32
            ).astype(BF16)
            written.append(
                [
                    fetch(tile.at[:, pl.ds(k * hid, hid)], out.at[cols])
                    for k, out in enumerate((gate_grad, up_grad, down_grad))
                ]
            )

    half = rows // 2

    def in_half(ref):
        return lambda h: ref.at[pl.ds(h * half, half)]

    def part(position, h):
        return partial.at[position, pl.ds(h * half, half)]

    ring = RingSum(net, y, right, left, part, in_half(relayed), in_half(from_left), in_half(from_right))
    for k, other in enumerate(order):
        for copy in mine[k]:
            copy.wait()
        for copy in crossed[k]:
            copy.wait_recv()
        total(partial.at[other], [partial.at[other], from_core.at[other]])
        (ring.start_far, ring.start_ahead, ring.start_behind, lambda: None)[k]()
    weight_tiles(0, 1)
    for copy in share_copies:
        copy.wait_recv()
    value = shares[y]
    for k in range(1, count):
        value = value + share_in[lax.rem(tensor + k, count)]
    share_sum[...] = value
    back_shares[node] = value
    share_back = [net.start(share_sum, back_shares.at[node], peer) for peer in peers]
    weight_tiles(1, 4)
    ring.middle()
    weight_tiles(4, 6)
    ring.finish()
    own = partial.at[y]
    total(dense_sum, [r.at[pl.ds(slots, tokens)] for r in (own, from_left, from_right)])
    total(own.at[pl.ds(0, slots)], [r.at[pl.ds(0, slots)] for r in (own, from_left, from_right)])
    block = 2 * slots // (SIDE * SIDE)
    short = block // 2
    row = lax.broadcasted_iota(jnp.int32, (2 * slots, slots), 0)
    col = lax.broadcasted_iota(jnp.int32, (2 * slots, slots), 1)
    place_in = lax.rem(row, block)
    second = (place_in >= short).astype(jnp.int32)
    source = lax.div(row, block) * short + place_in - second * short
    hit = (col == source).astype(jnp.int32)
    tables = [(hit * (1 - second)).astype(F32).astype(BF16), (hit * second).astype(F32).astype(BF16)]
    width = 256
    columns = parted.shape[1]

    def cut(i, carry):
        cols = pl.multiple_of(i * width, width)
        value = jnp.dot(
            tables[0], own[pl.ds(0, slots), pl.ds(cols, width)], preferred_element_type=F32
        )
        value = value + jnp.dot(
            tables[1], own[pl.ds(0, slots), pl.ds(cols + columns, width)], preferred_element_type=F32
        )
        parted[:, pl.ds(cols, width)] = value.astype(BF16)
        return carry

    lax.fori_loop(0, columns // width, cut, 0)

    def rows_of(ref, index):
        return ref.at[pl.ds(pl.multiple_of(index * block, block), block)]

    returned = [net.start(rows_of(parted, peer[0]), rows_of(back, node), peer) for peer in peers]
    keep = pltpu.make_async_copy(rows_of(parted, node), rows_of(back, node), local_sems.at[8])
    keep.start()
    weight_tiles(6, count_tiles)
    keep.wait()
    for copies in written[-2:]:
        for copy in copies:
            copy.wait()
    for copy in share_back + returned:
        copy.wait_recv()
    net.drain()


def return_rows(routed, dense, shares, rows_x, rows_dy, parts, hidden):
    count = SIDE * CORES
    width = routed.shape[1]
    slots = routed.shape[0] // count
    tokens = dense.shape[0] // count
    nodes = SIDE * SIDE
    rows = slots + tokens
    return pl.pallas_call(
        return_kernel,
        out_shape=[
            jax.ShapeDtypeStruct((2 * slots, width // 2), BF16),
            jax.ShapeDtypeStruct((tokens, width), F32),
            jax.ShapeDtypeStruct((nodes,) + shares.shape[1:], F32),
        ]
        + [jax.ShapeDtypeStruct((width, hidden.shape[1]), BF16)] * 3,
        in_specs=[ANY, ANY, VMEM] + [ANY] * 4,
        out_specs=[VMEM] * 3 + [ANY] * 3,
        scratch_shapes=[
            pltpu.VMEM((SIDE, rows, width), BF16),
            pltpu.VMEM((SIDE, rows, width), BF16),
            pltpu.VMEM((rows, width), BF16),
            pltpu.VMEM((rows, width), BF16),
            pltpu.VMEM((rows, width), BF16),
            pltpu.VMEM((2 * slots, width // 2), BF16),
            pltpu.VMEM((count,) + shares.shape[1:], F32),
            pltpu.VMEM(shares.shape[1:], F32),
            pltpu.VMEM(rows_x.shape, BF16),
            pltpu.VMEM(rows_dy.shape, BF16),
            pltpu.VMEM(parts.shape, BF16),
            pltpu.VMEM(hidden.shape, BF16),
            pltpu.VMEM((2, TILE, 3 * hidden.shape[1]), BF16),
            pltpu.SemaphoreType.DMA((RETURN_COPIES,)),
            pltpu.SemaphoreType.DMA((RETURN_COPIES,)),
            pltpu.SemaphoreType.DMA((64,)),
        ],
        compiler_params=pltpu.CompilerParams(
            collective_id=1, has_side_effects=True, vmem_limit_bytes=60 << 20
        ),
        name="return_rows",
    )(routed, dense, shares, rows_x, rows_dy, parts, hidden)


def finish_kernel(out_grad, dense_sum, back, first_table, second_table, *rest):
    sources, input_grad, results, sems = rest[:6], rest[6], rest[7:13], rest[13]
    copies = []
    for source, result in zip(sources, results):
        pieces = 1 if source.shape[0] < 1024 else 7
        rows = source.shape[0] // pieces
        for i in range(pieces):
            at = pl.ds(i * rows, rows)
            copies.append(
                pltpu.make_async_copy(source.at[at], result.at[at], sems.at[len(copies)])
            )
            copies[-1].start()
    columns = back.shape[1]
    for k, table in enumerate((first_table, second_table)):
        cols = pl.ds(k * columns, columns)
        picked = jnp.dot(table[...], back[...], preferred_element_type=F32)
        input_grad[:, cols] = (
            out_grad[:, cols].astype(F32) + dense_sum[:, cols] + picked
        ).astype(BF16)
    for copy in copies:
        copy.wait()


def finish(out_grad, dense_sum, back, first_table, second_table, grads):
    return pl.pallas_call(
        finish_kernel,
        out_shape=[jax.ShapeDtypeStruct(out_grad.shape, BF16)]
        + [jax.ShapeDtypeStruct(grad.shape, BF16) for grad in grads],
        in_specs=[VMEM] * 5 + [ANY] * 6,
        out_specs=[VMEM] + [ANY] * 6,
        scratch_shapes=[pltpu.SemaphoreType.DMA((24,))],
        compiler_params=pltpu.CompilerParams(vmem_limit_bytes=24 << 20),
        name="finish",
    )(out_grad, dense_sum, back, first_table, second_table, *grads)


def local(
    tokens, out_grad, gate_weights, expert_ids, dense_gate, dense_up, dense_down,
    expert_gate, expert_up, expert_down,
):
    tok_dev, width = tokens.shape
    nodes = SIDE * SIDE
    capacity = 4 * tok_dev // nodes
    block = 2 * capacity
    flat_ids = expert_ids.reshape(-1)
    pair = jnp.arange(2 * tok_dev, dtype=jnp.int32)
    earlier = (flat_ids[:, None] == flat_ids[None, :]) & (pair[None, :] < pair[:, None])
    slot_index = jnp.sum(earlier.astype(jnp.int32), axis=1)
    position = (flat_ids * block + slot_index).reshape(tok_dev, 2)
    row = jnp.arange(nodes * block, dtype=jnp.int32)[None, :, None]
    first_hit = (row == position[:, None, :]).astype(F32)
    second_hit = (row == position[:, None, :] + capacity).astype(F32)
    first_table = jnp.sum(first_hit, axis=2).astype(BF16)
    second_table = jnp.sum(second_hit, axis=2).astype(BF16)
    weights = gate_weights.astype(F32)[:, None, :]
    first_weight = jnp.sum(first_hit * weights, axis=2).astype(BF16)
    second_weight = jnp.sum(second_hit * weights, axis=2).astype(BF16)
    (
        rows_x, rows_dy, parts, hidden, routed_input, dense_input, shares,
        dense_gate_grad, dense_up_grad, dense_down_grad,
    ) = forward(
        tokens, out_grad, (first_table, second_table, first_weight, second_weight),
        (dense_gate, dense_up, dense_down),
        (expert_gate[0], expert_up[0], expert_down[0]),
    )
    back, dense_sum, back_shares, gate_grad, up_grad, down_grad = return_rows(
        routed_input, dense_input, shares, rows_x, rows_dy, parts, hidden
    )

    input_grad, *weight_grads = finish(
        out_grad, dense_sum, back, first_table, second_table,
        (dense_gate_grad, dense_up_grad, dense_down_grad, gate_grad, up_grad, down_grad),
    )
    node, tensor = lax.axis_index("node"), lax.axis_index("tensor")
    start = lax.rem(tensor, CORES) * (nodes * capacity) + node * capacity
    mine = lax.dynamic_slice(back_shares, (0, 0, start), (nodes, 1, capacity)).reshape(1, 1, nodes, capacity)
    expert = jnp.arange(nodes, dtype=jnp.int32)[None, None, :, None]
    slot = jnp.arange(capacity, dtype=jnp.int32)[None, None, None, :]
    chosen = (expert == expert_ids[:, :, None, None]) & (
        slot == slot_index.reshape(tok_dev, 2)[:, :, None, None]
    )
    weighted = jnp.sum(jnp.where(chosen, mine, 0.0), axis=(2, 3))
    gate_weight_grad = weighted / gate_weights.astype(F32)
    return (
        input_grad,
        gate_weight_grad,
        *weight_grads[:3],
        *(value[None] for value in weight_grads[3:]),
    )


def solution(mesh):
    rows = P(("node", "tensor"), None)
    dense = P(None, "tensor")
    expert = P("node", None, "tensor")
    summed = P("node", "tensor")
    return jax.shard_map(
        local,
        mesh=mesh,
        in_specs=(rows,) * 4 + (dense,) * 3 + (expert,) * 3,
        out_specs=(rows, rows) + (summed,) * 3 + (expert,) * 3,
        check_vma=False,
    )
```

```python
import jax
import jax.numpy as jnp
from jax import lax
from jax.experimental import pallas as pl
from jax.experimental.pallas import tpu as pltpu
from jax.sharding import PartitionSpec as P

MESH = pl.DeviceIdType.MESH
BF16 = jnp.bfloat16
F32 = jnp.float32
SIDE = 4
CORES = 2
ANY = pl.BlockSpec(memory_space=pl.ANY)
VMEM = pl.BlockSpec(memory_space=pltpu.VMEM)


def place():
    node = lax.axis_index("node")
    tensor = lax.axis_index("tensor")
    return (
        lax.div(node, SIDE),
        lax.rem(node, SIDE),
        lax.div(tensor, CORES),
        lax.rem(tensor, CORES),
    )


def turn(position, steps):
    return lax.rem(position + steps, SIDE)


def meet(peers):
    barrier = pltpu.get_barrier_semaphore()
    for peer in peers:
        pl.semaphore_signal(barrier, inc=1, device_id=peer, device_id_type=MESH)
    pl.semaphore_wait(barrier, len(peers))


class Net:
    def __init__(self, send_sems, recv_sems):
        self.send_sems, self.recv_sems = send_sems, recv_sems
        self.copies = []
        self.pending = []

    def start(self, src, dst, peer, keep=True):
        index = len(self.copies)
        copy = pltpu.make_async_remote_copy(
            src_ref=src,
            dst_ref=dst,
            send_sem=self.send_sems.at[index],
            recv_sem=self.recv_sems.at[index],
            device_id=peer,
            device_id_type=MESH,
        )
        copy.start()
        self.copies.append(copy)
        if keep:
            self.pending.append(copy)
        return copy

    def drain(self):
        for copy in self.pending:
            copy.wait_send()


def total(dst, sources, scale=None, slab=16):
    rows = dst.shape[-2]
    leads = [()]
    for size in dst.shape[:-2]:
        leads = [lead + (i,) for lead in leads for i in range(size)]
    for lead in leads:

        def body(i, carry, lead=lead):
            at = lead + (pl.ds(pl.multiple_of(i * slab, slab), slab), slice(None))
            value = sources[0][at].astype(F32)
            for source in sources[1:]:
                value = value + source[at].astype(F32)
            if scale is not None:
                value = value * scale
            dst[at] = value.astype(dst.dtype)
            return carry

        lax.fori_loop(0, rows // slab, body, 0)


def node_peers(x, z, tensor):
    peers = []
    for dx in range(SIDE):
        for dz in range(SIDE):
            if dx or dz:
                peers.append((turn(x, dx) * SIDE + turn(z, dz), tensor))
    return peers


class Gather:
    def __init__(self, net, node, y, core, own, whole, rows):
        self.net, self.own, self.whole, self.rows = net, own, whole, rows
        self.me = y * CORES + core
        self.right_at = turn(y, 1) * CORES + core
        self.left_at = turn(y, SIDE - 1) * CORES + core
        self.far_at = turn(y, 2) * CORES + core
        self.right = (node, self.right_at)
        self.left = (node, self.left_at)
        self.partner = (node, y * CORES + 1 - core)
        self.crossed, self.to_right, self.to_left = {}, {}, {}

    def chunk(self, half, at):
        return self.whole[half].at[pl.ds(pl.multiple_of(at * self.rows, self.rows), self.rows)]

    def pass_on(self, half, at, name):
        ref = self.chunk(half, at)
        self.crossed[name, half] = self.net.start(ref, ref, self.partner)

    def start(self, half):
        send = self.net.start
        mine, own = self.chunk(half, self.me), self.own[half]
        self.to_right[half] = send(own, mine, self.right)
        self.to_left[half] = send(own, mine, self.left)
        self.crossed["own", half] = send(own, mine, self.partner)

    def relay(self):
        send = self.net.start
        left_at, right_at = self.left_at, self.right_at
        self.to_right[0].wait_recv()
        self.relay_right = send(self.chunk(0, left_at), self.chunk(0, left_at), self.right)
        self.pass_on(0, left_at, "left")
        self.to_left[1].wait_recv()
        self.relay_left = send(self.chunk(1, right_at), self.chunk(1, right_at), self.left)
        self.pass_on(1, right_at, "right")

    def relay_rest(self):
        self.to_right[1].wait_recv()
        self.pass_on(1, self.left_at, "left")
        self.to_left[0].wait_recv()
        self.pass_on(0, self.right_at, "right")

    def relay_far(self):
        self.relay_right.wait_recv()
        self.pass_on(0, self.far_at, "far")
        self.relay_left.wait_recv()
        self.pass_on(1, self.far_at, "far")

    def arrive(self, name):
        for half in range(2):
            self.crossed[name, half].wait_recv()


class RingSum:
    def __init__(self, net, position, right, left, part, relayed, from_left, from_right):
        self.net, self.right, self.left, self.part = net, right, left, part
        self.relayed, self.from_left, self.from_right = relayed, from_left, from_right
        self.ahead, self.far, self.behind = (turn(position, k) for k in (1, 2, 3))

    def start_far(self):
        send, part = self.net.start, self.part
        self.relay_right = send(part(self.far, 0), self.relayed(0), self.right)
        self.relay_left = send(part(self.far, 1), self.relayed(1), self.left)

    def start_ahead(self):
        self.direct_right = self.net.start(self.part(self.ahead, 1), self.from_left(1), self.right)

    def start_behind(self):
        self.direct_left = self.net.start(self.part(self.behind, 0), self.from_right(0), self.left)

    def middle(self):
        self.absorb()
        self.send_sums()

    def absorb(self):
        self.relay_right.wait_recv()
        mine = self.part(self.ahead, 0)
        total(mine, [mine, self.relayed(0)])
        self.relay_left.wait_recv()
        mine = self.part(self.behind, 1)
        total(mine, [mine, self.relayed(1)])

    def send_sums(self):
        send, part = self.net.start, self.part
        self.sum_right = send(part(self.ahead, 0), self.from_left(0), self.right)
        self.sum_left = send(part(self.behind, 1), self.from_right(1), self.left)

    def finish(self):
        for copy in (self.direct_right, self.direct_left, self.sum_right, self.sum_left):
            copy.wait_recv()


NT = (((1,), (1,)), ((), ()))
TN = (((0,), (0,)), ((), ()))
TILE = 512
HALF_TILE = 256
VMEM_BYTES = 63 << 20
LAYER_COPIES = 2 * 14 + 2 * 15 + 24 + 8 + 12 + 7 + 15 + 2 * 15


def silu_parts(pre_gate):
    sigma = jax.nn.sigmoid(pre_gate)
    return (pre_gate * sigma, sigma * (1.0 + pre_gate * (1.0 - sigma)))


def unit_grads(rows_x, rows_dy, w_both, w_down, parts, hidden_out):
    hid = w_down.shape[1]
    pre = jnp.dot(rows_x[...], w_both[...], preferred_element_type=F32)
    hidden_grad = jnp.dot(rows_dy[...], w_down[...], preferred_element_type=F32)
    pre_up = pre[:, hid:]
    activated, derivative = silu_parts(pre[:, :hid])
    hidden = activated * pre_up
    parts[:, pl.ds(0, hid)] = (hidden_grad * pre_up * derivative).astype(BF16)
    parts[:, pl.ds(hid, hid)] = (hidden_grad * activated).astype(BF16)
    hidden_out[...] = hidden.astype(BF16)
    return hidden * hidden_grad


def input_term(parts, w_both, first, columns, store):
    def body(i, carry):
        at = pl.multiple_of(i * HALF_TILE, HALF_TILE)
        value = lax.dot_general(
            parts[...], w_both[pl.ds(first + at, HALF_TILE)], NT, preferred_element_type=F32
        )
        store(pl.ds(at, HALF_TILE), value.astype(BF16))
        return carry

    lax.fori_loop(0, columns // HALF_TILE, body, 0)


def lane_sums(value):
    high = value.astype(BF16)
    low = (value - high.astype(F32)).astype(BF16)
    ones = jnp.ones((8, value.shape[1]), BF16)
    return lax.dot_general(ones, high, NT, preferred_element_type=F32) + lax.dot_general(
        ones, low, NT, preferred_element_type=F32
    )


class WeightSums:
    def __init__(self, net, x, z, tensor, grads, first_bufs):
        self.net, self.x, self.z, self.grads = net, x, z, grads
        self.half = half = grads.shape[2] // 2
        self.first_bufs = first_bufs
        pairs = SIDE // 2

        def at(xx, zz):
            return (xx * SIDE + zz, tensor)

        self.around_x = (at(turn(x, 1), z), at(turn(x, 3), z))
        self.around_z = (at(x, turn(z, 1)), at(x, turn(z, 3)))

        def x_part(position, h):
            return grads.at[position, pl.ds(h * pairs, pairs), pl.ds(0, half)]

        def z_part(position, h):
            return grads.at[pl.ds(h * pairs, pairs), position, pl.ds(half, half)]

        def slot(ref, index):
            return lambda h: ref.at[index, pl.ds(h * pairs, pairs)]

        self.rings = [
            RingSum(net, x, *self.around_x, x_part, *(slot(ref, 0) for ref in first_bufs)),
            RingSum(net, z, *self.around_z, z_part, *(slot(ref, 1) for ref in first_bufs)),
        ]

    def middle(self):
        for ring in self.rings:
            ring.absorb()
        for ring in self.rings:
            ring.send_sums()

    def second(self):
        half = self.half
        cut = (0, half // 32 * 16 + 16, half)
        relayed, from_left, from_right = self.first_bufs

        def rows_half(h):
            return pl.ds(cut[h], cut[h + 1] - cut[h])

        def summed(index):
            return lambda position, h: from_left.at[index, position, rows_half(h)]

        def slot(index, k):
            return lambda h: relayed.at[index, k, rows_half(h)]

        later = [
            RingSum(self.net, self.z, *self.around_z, summed(0), *(slot(0, k) for k in range(3))),
            RingSum(self.net, self.x, *self.around_x, summed(1), *(slot(1, k) for k in range(3))),
        ]
        for ring in self.rings:
            ring.finish()
        for steps in (2, 1, 3, 0):
            for index, ring in enumerate(later):
                other = turn((self.z, self.x)[index], steps)
                if index == 0:
                    mine = self.grads.at[self.x, other, pl.ds(0, half)]
                else:
                    mine = self.grads.at[other, self.z, pl.ds(half, half)]
                left, right = from_left.at[index, other], from_right.at[index, other]
                total(left, [mine, left, right])
                if steps == 2:
                    ring.start_far()
                elif steps == 1:
                    ring.start_ahead()
                elif steps == 3:
                    ring.start_behind()
        self.rings = later

    def finish(self, outs):
        half = self.half
        relayed, from_left, unused = self.first_bufs
        for index, ring in enumerate(self.rings):
            ring.finish()
            own = from_left.at[index, (self.z, self.x)[index]]
            for block, ref in enumerate(outs):
                cols = pl.ds(block * ref.shape[1], ref.shape[1])
                total(
                    ref.at[pl.ds(index * half, half)],
                    [own.at[:, cols]] + [relayed.at[index, k, :, cols] for k in (1, 2)],
                    scale=1.0 / (SIDE * SIDE),
                )


def layer_kernel(
    tok, grad, first_table, second_table, first_weight, second_weight,
    dense_gate, dense_up, dense_down, expert_gate, expert_up, expert_down,
    back, dense_sum, back_shares, out_gate, out_up, out_down, gate_grad, up_grad, down_grad,
    tok_all, grad_all, rows_x, rows_dy, exchange, w_both, w_down, dense_parts, dense_hidden,
    parts, hidden, grads, relayed, from_left, from_right,
    terms, core_rest, y_relayed, y_left, y_right, shares, share_in, share_sum,
    send_sems, recv_sems, local_sems,
):
    x, z, y, core = place()
    node, tensor = x * SIDE + z, y * CORES + core
    net = Net(send_sems, recv_sems)
    peers = node_peers(x, z, tensor)
    count = SIDE * CORES
    mates = [(node, lax.rem(tensor + k, count)) for k in range(1, count)]
    local_rows, depth = tok.shape
    hid = w_down.shape[1]
    columns = exchange.shape[1]
    stack = exchange.shape[0] // 4
    outgoing = [exchange.at[pl.ds(h * stack, stack)] for h in range(2)]
    landed = [exchange.at[pl.ds((2 + h) * stack, stack)] for h in range(2)]
    block = stack // (SIDE * SIDE)
    slots = stack // 2
    started = []

    def fetch(src, dst):
        copy = pltpu.make_async_copy(src, dst, local_sems.at[len(started)])
        copy.start()
        started.append(copy)
        return copy

    dense = Gather(net, node, y, core, (tok, grad), (tok_all, grad_all), local_rows)
    routed = Gather(net, node, y, core, None, (rows_x, rows_dy), slots)
    routed.own = [routed.chunk(h, tensor) for h in range(2)]
    sums = WeightSums(net, x, z, tensor, grads, (relayed, from_left, from_right))
    meet(peers + mates)

    def rows_of(ref, index):
        return ref.at[pl.ds(pl.multiple_of(index * block, block), block)]

    def fetch_weights(gate, up, down):
        return [
            fetch(gate, w_both.at[:, pl.ds(0, hid)]),
            fetch(up, w_both.at[:, pl.ds(hid, hid)]),
            fetch(down, w_down),
        ]

    dense.start(0)
    dense.start(1)
    exchanged = []
    for h, (source, left, right) in enumerate(
        ((tok, first_table, second_table), (grad, first_weight, second_weight))
    ):
        out, into = outgoing[h], landed[h]
        for first in range(0, columns, 2 * HALF_TILE):
            width = min(2 * HALF_TILE, columns - first)
            value = lax.dot_general(
                left[...], source[:, pl.ds(first, width)], TN, preferred_element_type=F32
            ) + lax.dot_general(
                right[...], source[:, pl.ds(columns + first, width)], TN, preferred_element_type=F32
            )
            out[:, pl.ds(first, width)] = value.astype(BF16)
        exchanged.append(
            [net.start(rows_of(out, peer[0]), rows_of(into, node), peer, False) for peer in peers]
            + [fetch(rows_of(out, node), rows_of(into, node))]
        )
    kept = [
        fetch(tok, dense.chunk(0, tensor)),
        fetch(grad, dense.chunk(1, tensor)),
    ] + fetch_weights(dense_gate, dense_up, dense_down)
    row = lax.broadcasted_iota(jnp.int32, (slots, 2 * slots), 0)
    col = lax.broadcasted_iota(jnp.int32, (slots, 2 * slots), 1)
    half = block // 2
    origin = lax.div(row, half) * block + lax.rem(row, half)
    tables = [(col == origin + k * half).astype(F32).astype(BF16) for k in range(2)]
    row = lax.broadcasted_iota(jnp.int32, (2 * slots, slots), 0)
    col = lax.broadcasted_iota(jnp.int32, (2 * slots, slots), 1)
    origin = lax.div(row, block) * half + lax.rem(row, block)
    back_tables = [
        (jnp.logical_and(col == origin - k * half, lax.div(lax.rem(row, block), half) == k))
        .astype(F32)
        .astype(BF16)
        for k in range(2)
    ]

    def join(h):
        for copy in exchanged[h][:-1]:
            copy.wait()
        exchanged[h][-1].wait()
        own, into = routed.own[h], landed[h]
        for first in range(0, columns, 2 * HALF_TILE):
            width = min(2 * HALF_TILE, columns - first)
            cols = pl.ds(first, width)
            for k in range(2):
                own[:, pl.ds(k * columns + first, width)] = jnp.dot(
                    tables[k], into[:, cols], preferred_element_type=F32
                ).astype(BF16)

    dense.relay()
    dense.relay_rest()
    join(0)
    routed.start(0)
    dense.relay_far()
    join(1)
    routed.start(1)

    for name in ("own", "left", "right", "far"):
        dense.arrive(name)
    for copy in kept:
        copy.wait()
    unit_grads(tok_all, grad_all, w_both, w_down, dense_parts, dense_hidden)

    def side(other_core):
        return lax.rem(core + other_core, CORES)

    for c in range(2):

        def keep_dense(cols, value, c=c):
            for at in range(SIDE):
                for k in range(CORES):
                    first = (at * CORES + k) * local_rows
                    terms[c, side(k), at, pl.ds(slots, local_rows), cols] = value[
                        first : first + local_rows
                    ]

        input_term(dense_parts, w_both, c * columns, columns, keep_dense)
    weights = fetch_weights(expert_gate, expert_up, expert_down)
    band = depth // SIDE
    x_ring, z_ring = sums.rings
    for steps in (2, 1, 3, 0):
        other = turn(x, steps)
        cols = pl.ds(pl.multiple_of(other * band, band), band)
        value = lax.dot_general(
            tok_all[:, cols], dense_parts[...], TN, preferred_element_type=F32
        ).astype(BF16)
        grads[other, :, :, pl.ds(0, 2 * hid)] = value.reshape(SIDE, band // SIDE, 2 * hid)
        value = lax.dot_general(
            grad_all[:, cols], dense_hidden[...], TN, preferred_element_type=F32
        ).astype(BF16)
        grads[other, :, :, pl.ds(2 * hid, hid)] = value.reshape(SIDE, band // SIDE, hid)
        if steps == 2:
            x_ring.start_far()
        elif steps == 1:
            x_ring.start_ahead()
        elif steps == 3:
            x_ring.start_behind()
    z_ring.start_far()
    z_ring.start_ahead()
    z_ring.start_behind()
    for copy in weights:
        copy.wait()

    pair = CORES * slots
    crossed = {}

    def from_core(step, c):
        index, rows = 2 * step + c, slots + local_rows
        fit = exchange.shape[0] // rows
        if index < fit:
            return exchange.at[pl.ds(index * rows, rows)]
        return core_rest.at[index - fit]

    def expert_rows(step, at):
        rows = pl.ds(pl.multiple_of(at * pair, pair), pair)
        product = unit_grads(
            rows_x.at[rows], rows_dy.at[rows], w_both, w_down, parts.at[rows], hidden.at[rows]
        )
        shares[at] = lane_sums(product)
        for c in range(2):

            def keep_routed(cols, value, c=c):
                for k in range(CORES):
                    terms[c, side(k), at, pl.ds(0, slots), cols] = value[k * slots : (k + 1) * slots]

            input_term(parts.at[rows], w_both, c * columns, columns, keep_routed)
            crossed[step, c] = net.start(
                terms.at[c, 1, at], from_core(step, c), routed.partner
            )

    def absorb(step, at, c):
        crossed[step, c].wait_recv()
        mine = terms.at[c, 0, at]
        total(mine, [mine, from_core(step, c)])

    def half_rows(ref, *lead):
        half = ref.shape[-2] // 2
        return lambda h: ref.at[(*lead, pl.ds(h * half, half))]

    y_rings = [
        RingSum(
            net, y, routed.right, routed.left,
            lambda position, h, c=c: half_rows(terms, c, 0, position)(h),
            half_rows(y_relayed, c), half_rows(y_left, c), half_rows(y_right, c),
        )
        for c in range(2)
    ]
    routed.arrive("own")
    expert_rows(0, y)
    routed.relay()
    routed.relay_rest()
    sums.middle()
    routed.arrive("left")
    expert_rows(1, turn(y, 3))
    routed.arrive("right")
    sums.second()
    expert_rows(2, turn(y, 1))
    for c in range(2):
        absorb(1, turn(y, 3), c)
        absorb(2, turn(y, 1), c)
    routed.relay_far()
    for ring in y_rings:
        ring.start_ahead()
        ring.start_behind()
    routed.arrive("far")
    expert_rows(3, turn(y, 2))
    for c in range(2):
        absorb(3, turn(y, 2), c)
        y_rings[c].start_far()
    share_copies = [
        net.start(shares.at[lax.div(mate[1], CORES)], share_in.at[tensor], mate) for mate in mates
    ]
    sums.middle()
    for c in range(2):
        absorb(0, y, c)

    written = []

    def weight_tiles(first, last):
        for i in range(first, last):
            cols = pl.ds(i * TILE, TILE)
            w_both[cols] = lax.dot_general(
                rows_x[:, cols], parts[...], TN, preferred_element_type=F32
            ).astype(BF16)
            w_down[cols] = lax.dot_general(
                rows_dy[:, cols], hidden[...], TN, preferred_element_type=F32
            ).astype(BF16)
            written.append(fetch(w_both.at[cols, pl.ds(0, hid)], gate_grad.at[cols]))
            written.append(fetch(w_both.at[cols, pl.ds(hid, hid)], up_grad.at[cols]))
            written.append(fetch(w_down.at[cols], down_grad.at[cols]))

    weight_tiles(0, 2)
    for copy in share_copies:
        copy.wait_recv()
    value = shares[y]
    for k in range(1, count):
        value = value + share_in[lax.rem(tensor + k, count)]
    share_sum[...] = value
    back_shares[node] = value
    returned = [net.start(share_sum, back_shares.at[node], peer) for peer in peers]
    weight_tiles(2, 3)
    y_rings[0].middle()
    weight_tiles(3, 5)
    y_rings[1].middle()
    sums.finish((out_gate, out_up, out_down))
    count_tiles = depth // TILE
    short = columns // 2
    for c in range(2):
        if c == 0:
            weight_tiles(5, 6)
        y_rings[c].finish()
        own, left, right = terms.at[c, 0, y], y_left.at[c], y_right.at[c]
        landed_rows = [ref.at[pl.ds(0, slots)] for ref in (own, left, right)]
        total(own.at[pl.ds(0, slots)], landed_rows)
        for first in range(0, short, HALF_TILE):
            width = min(HALF_TILE, short - first)
            value = jnp.dot(
                back_tables[0], own[pl.ds(0, slots), pl.ds(first, width)], preferred_element_type=F32
            ) + jnp.dot(
                back_tables[1],
                own[pl.ds(0, slots), pl.ds(short + first, width)],
                preferred_element_type=F32,
            )
            for k in range(2):
                y_relayed[c, pl.ds(0, slots), pl.ds(k * short + first, width)] = value[
                    k * slots : (k + 1) * slots
                ].astype(BF16)

        def parted(index, c=c):
            each = slots // block
            rows = pl.multiple_of(lax.rem(index, each) * block, block)
            cols = pl.multiple_of(lax.div(index, each) * short, 128)
            return y_relayed.at[c, pl.ds(rows, block), pl.ds(cols, short)]

        returned += [net.start(parted(peer[0]), rows_of(back.at[c], node), peer) for peer in peers]
        written.append(fetch(parted(node), rows_of(back.at[c], node)))
        total(
            dense_sum.at[:, pl.ds(c * columns, columns)],
            [ref.at[pl.ds(slots, local_rows)] for ref in (own, left, right)],
        )
    weight_tiles(6, count_tiles)
    for copy in returned:
        copy.wait_recv()
    for copy in written:
        copy.wait()
    net.drain()


def layer(tokens, out_grad, tables, dense, expert):
    rows, depth = tokens.shape
    hid = dense[0].shape[1]
    count = SIDE * CORES
    nodes = SIDE * SIDE
    slots = tables[0].shape[1] // 2
    node_rows, slot_rows = count * rows, count * slots
    own = depth // nodes
    half = depth // 2
    bands = (2, SIDE, own // 2, 3 * hid)
    shape = jax.ShapeDtypeStruct
    share = (8, CORES * slots)
    return pl.pallas_call(
        layer_kernel,
        out_shape=[
            shape((2, 2 * slots, half // 2), BF16),
            shape((rows, depth), F32),
            shape((nodes,) + share, F32),
        ]
        + [shape((own, hid), BF16)] * 3
        + [shape((depth, hid), BF16)] * 3,
        in_specs=[VMEM] * 6 + [ANY] * 6,
        out_specs=[ANY] + [VMEM] * 5 + [ANY] * 3,
        scratch_shapes=[
            pltpu.VMEM((node_rows, depth), BF16),
            pltpu.VMEM((node_rows, depth), BF16),
            pltpu.VMEM((slot_rows, depth), BF16),
            pltpu.VMEM((slot_rows, depth), BF16),
            pltpu.VMEM((8 * slots, half), BF16),
            pltpu.VMEM((depth, 2 * hid), BF16),
            pltpu.VMEM((depth, hid), BF16),
            pltpu.VMEM((node_rows, 2 * hid), BF16),
            pltpu.VMEM((node_rows, hid), BF16),
            pltpu.VMEM((slot_rows, 2 * hid), BF16),
            pltpu.VMEM((slot_rows, hid), BF16),
            pltpu.VMEM((SIDE, SIDE, own, 3 * hid), BF16),
        ]
        + [pltpu.VMEM(bands, BF16)] * 3
        + [
            pltpu.VMEM((2, CORES, SIDE, slots + rows, half), BF16),
            pltpu.VMEM((2 * SIDE - 8 * slots // (slots + rows), slots + rows, half), BF16),
        ]
        + [pltpu.VMEM((2, slots + rows, half), BF16)] * 3
        + [
            pltpu.VMEM((SIDE,) + share, F32),
            pltpu.VMEM((count,) + share, F32),
            pltpu.VMEM(share, F32),
            pltpu.SemaphoreType.DMA((LAYER_COPIES,)),
            pltpu.SemaphoreType.DMA((LAYER_COPIES,)),
            pltpu.SemaphoreType.DMA((36,)),
        ],
        compiler_params=pltpu.CompilerParams(
            collective_id=0, has_side_effects=True, vmem_limit_bytes=VMEM_BYTES
        ),
        name="layer",
    )(tokens, out_grad, *tables, *dense, *expert)


def finish_kernel(out_grad, dense_sum, back, first_table, second_table, *rest):
    sources, input_grad, results, sems = rest[:6], rest[6], rest[7:13], rest[13]
    copies = []
    for source, result in zip(sources, results):
        pieces = 1 if source.shape[0] < 1024 else 7
        rows = source.shape[0] // pieces
        for i in range(pieces):
            at = pl.ds(i * rows, rows)
            copies.append(
                pltpu.make_async_copy(source.at[at], result.at[at], sems.at[len(copies)])
            )
            copies[-1].start()
    columns = back.shape[2]
    for k in range(4):
        cols = pl.ds(k * columns, columns)
        table = (first_table, second_table)[k % 2]
        picked = jnp.dot(table[...], back[k // 2], preferred_element_type=F32)
        input_grad[:, cols] = (
            out_grad[:, cols].astype(F32) + dense_sum[:, cols] + picked
        ).astype(BF16)
    for copy in copies:
        copy.wait()


def finish(out_grad, dense_sum, back, first_table, second_table, grads):
    return pl.pallas_call(
        finish_kernel,
        out_shape=[jax.ShapeDtypeStruct(out_grad.shape, BF16)]
        + [jax.ShapeDtypeStruct(grad.shape, BF16) for grad in grads],
        in_specs=[VMEM] * 5 + [ANY] * 6,
        out_specs=[VMEM] + [ANY] * 6,
        scratch_shapes=[pltpu.SemaphoreType.DMA((24,))],
        compiler_params=pltpu.CompilerParams(vmem_limit_bytes=60 << 20),
        name="finish",
    )(out_grad, dense_sum, back, first_table, second_table, *grads)


def local(
    tokens, out_grad, gate_weights, expert_ids, dense_gate, dense_up, dense_down,
    expert_gate, expert_up, expert_down,
):
    tok_dev, width = tokens.shape
    nodes = SIDE * SIDE
    capacity = 4 * tok_dev // nodes
    block = 2 * capacity
    flat_ids = expert_ids.reshape(-1)
    pair = jnp.arange(2 * tok_dev, dtype=jnp.int32)
    earlier = (flat_ids[:, None] == flat_ids[None, :]) & (pair[None, :] < pair[:, None])
    slot_index = jnp.sum(earlier.astype(jnp.int32), axis=1)
    position = (flat_ids * block + slot_index).reshape(tok_dev, 2)
    row = jnp.arange(nodes * block, dtype=jnp.int32)[None, :, None]
    first_hit = (row == position[:, None, :]).astype(F32)
    second_hit = (row == position[:, None, :] + capacity).astype(F32)
    first_table = jnp.sum(first_hit, axis=2).astype(BF16)
    second_table = jnp.sum(second_hit, axis=2).astype(BF16)
    weights = gate_weights.astype(F32)[:, None, :]
    first_weight = jnp.sum(first_hit * weights, axis=2).astype(BF16)
    second_weight = jnp.sum(second_hit * weights, axis=2).astype(BF16)
    back, dense_sum, back_shares, *sums = layer(
        tokens, out_grad, (first_table, second_table, first_weight, second_weight),
        (dense_gate, dense_up, dense_down), (expert_gate[0], expert_up[0], expert_down[0]),
    )
    input_grad, *weight_grads = finish(
        out_grad, dense_sum, back, first_table, second_table, sums
    )
    node, tensor = lax.axis_index("node"), lax.axis_index("tensor")
    start = lax.rem(tensor, CORES) * (nodes * capacity) + node * capacity
    mine = lax.dynamic_slice(back_shares, (0, 0, start), (nodes, 1, capacity)).reshape(1, 1, nodes, capacity)
    expert = jnp.arange(nodes, dtype=jnp.int32)[None, None, :, None]
    slot = jnp.arange(capacity, dtype=jnp.int32)[None, None, None, :]
    chosen = (expert == expert_ids[:, :, None, None]) & (
        slot == slot_index.reshape(tok_dev, 2)[:, :, None, None]
    )
    weighted = jnp.sum(jnp.where(chosen, mine, 0.0), axis=(2, 3))
    gate_weight_grad = weighted / gate_weights.astype(F32)
    return (
        input_grad,
        gate_weight_grad,
        *weight_grads[:3],
        *(value[None] for value in weight_grads[3:]),
    )


def solution(mesh):
    rows = P(("node", "tensor"), None)
    dense = P(None, "tensor")
    expert = P("node", None, "tensor")
    summed = P("node", "tensor")
    return jax.shard_map(
        local,
        mesh=mesh,
        in_specs=(rows,) * 4 + (dense,) * 3 + (expert,) * 3,
        out_specs=(rows, rows) + (summed,) * 3 + (expert,) * 3,
        check_vma=False,
    )
```

```python
import jax
import jax.numpy as jnp
from jax import lax
from jax.experimental import pallas as pl
from jax.experimental.pallas import tpu as pltpu
from jax.sharding import PartitionSpec as P

MESH = pl.DeviceIdType.MESH
BF16 = jnp.bfloat16
F32 = jnp.float32
SIDE = 4
CORES = 2
ANY = pl.BlockSpec(memory_space=pl.ANY)
VMEM = pl.BlockSpec(memory_space=pltpu.VMEM)


def place():
    node = lax.axis_index("node")
    tensor = lax.axis_index("tensor")
    return (
        lax.div(node, SIDE),
        lax.rem(node, SIDE),
        lax.div(tensor, CORES),
        lax.rem(tensor, CORES),
    )


def turn(position, steps):
    return lax.rem(position + steps, SIDE)


def meet(peers):
    barrier = pltpu.get_barrier_semaphore()
    for peer in peers:
        pl.semaphore_signal(barrier, inc=1, device_id=peer, device_id_type=MESH)
    pl.semaphore_wait(barrier, len(peers))


class Net:
    def __init__(self, send_sems, recv_sems):
        self.send_sems, self.recv_sems = send_sems, recv_sems
        self.copies = []
        self.pending = []

    def start(self, src, dst, peer, keep=True):
        index = len(self.copies)
        copy = pltpu.make_async_remote_copy(
            src_ref=src,
            dst_ref=dst,
            send_sem=self.send_sems.at[index],
            recv_sem=self.recv_sems.at[index],
            device_id=peer,
            device_id_type=MESH,
        )
        copy.start()
        self.copies.append(copy)
        if keep:
            self.pending.append(copy)
        return copy

    def drain(self):
        for copy in self.pending:
            copy.wait_send()


def total(dst, sources, scale=None, slab=16):
    rows = dst.shape[-2]
    leads = [()]
    for size in dst.shape[:-2]:
        leads = [lead + (i,) for lead in leads for i in range(size)]
    for lead in leads:

        def body(i, carry, lead=lead):
            at = lead + (pl.ds(pl.multiple_of(i * slab, slab), slab), slice(None))
            value = sources[0][at].astype(F32)
            for source in sources[1:]:
                value = value + source[at].astype(F32)
            if scale is not None:
                value = value * scale
            dst[at] = value.astype(dst.dtype)
            return carry

        lax.fori_loop(0, rows // slab, body, 0)


def node_peers(x, z, tensor):
    peers = []
    for dx in range(SIDE):
        for dz in range(SIDE):
            if dx or dz:
                peers.append((turn(x, dx) * SIDE + turn(z, dz), tensor))
    return peers


class Gather:
    def __init__(self, net, node, y, core, own, whole, rows):
        self.net, self.own, self.whole, self.rows = net, own, whole, rows
        self.me = y * CORES + core
        self.right_at = turn(y, 1) * CORES + core
        self.left_at = turn(y, SIDE - 1) * CORES + core
        self.far_at = turn(y, 2) * CORES + core
        self.right = (node, self.right_at)
        self.left = (node, self.left_at)
        self.partner = (node, y * CORES + 1 - core)
        self.crossed, self.to_right, self.to_left = {}, {}, {}

    def chunk(self, half, at):
        return self.whole[half].at[pl.ds(pl.multiple_of(at * self.rows, self.rows), self.rows)]

    def pass_on(self, half, at, name):
        ref = self.chunk(half, at)
        self.crossed[name, half] = self.net.start(ref, ref, self.partner)

    def start(self, half):
        send = self.net.start
        mine, own = self.chunk(half, self.me), self.own[half]
        self.to_right[half] = send(own, mine, self.right)
        self.to_left[half] = send(own, mine, self.left)
        self.crossed["own", half] = send(own, mine, self.partner)

    def relay(self):
        send = self.net.start
        left_at, right_at = self.left_at, self.right_at
        self.to_right[0].wait_recv()
        self.relay_right = send(self.chunk(0, left_at), self.chunk(0, left_at), self.right)
        self.pass_on(0, left_at, "left")
        self.to_left[1].wait_recv()
        self.relay_left = send(self.chunk(1, right_at), self.chunk(1, right_at), self.left)
        self.pass_on(1, right_at, "right")

    def relay_rest(self):
        self.to_right[1].wait_recv()
        self.pass_on(1, self.left_at, "left")
        self.to_left[0].wait_recv()
        self.pass_on(0, self.right_at, "right")

    def take(self, half):
        self.to_right[half].wait_recv()
        self.pass_on(half, self.left_at, "left")
        self.to_left[half].wait_recv()
        self.pass_on(half, self.right_at, "right")

    def relay_far(self):
        self.relay_right.wait_recv()
        self.pass_on(0, self.far_at, "far")
        self.relay_left.wait_recv()
        self.pass_on(1, self.far_at, "far")

    def arrive(self, name):
        for half in range(2):
            self.crossed[name, half].wait_recv()


class RingSum:
    def __init__(self, net, position, right, left, part, relayed, from_left, from_right):
        self.net, self.right, self.left, self.part = net, right, left, part
        self.relayed, self.from_left, self.from_right = relayed, from_left, from_right
        self.ahead, self.far, self.behind = (turn(position, k) for k in (1, 2, 3))

    def start_far(self):
        send, part = self.net.start, self.part
        self.relay_right = send(part(self.far, 0), self.relayed(0), self.right)
        self.relay_left = send(part(self.far, 1), self.relayed(1), self.left)

    def start_ahead(self):
        self.direct_right = self.net.start(self.part(self.ahead, 1), self.from_left(1), self.right)

    def start_behind(self):
        self.direct_left = self.net.start(self.part(self.behind, 0), self.from_right(0), self.left)

    def middle(self):
        self.absorb()
        self.send_sums()

    def absorb(self):
        self.relay_right.wait_recv()
        mine = self.part(self.ahead, 0)
        total(mine, [mine, self.relayed(0)])
        self.relay_left.wait_recv()
        mine = self.part(self.behind, 1)
        total(mine, [mine, self.relayed(1)])

    def send_sums(self):
        send, part = self.net.start, self.part
        self.sum_right = send(part(self.ahead, 0), self.from_left(0), self.right)
        self.sum_left = send(part(self.behind, 1), self.from_right(1), self.left)

    def finish(self):
        for copy in (self.direct_right, self.direct_left, self.sum_right, self.sum_left):
            copy.wait_recv()


NT = (((1,), (1,)), ((), ()))
TN = (((0,), (0,)), ((), ()))
TILE = 512
HALF_TILE = 256
VMEM_BYTES = 63 << 20
LAYER_COPIES = 14 + 12 + 1 + 3 * 15 + 24 + 8 + 12 + 7 + 15 + 2 * 15


def silu_parts(pre_gate):
    sigma = jax.nn.sigmoid(pre_gate)
    return (pre_gate * sigma, sigma * (1.0 + pre_gate * (1.0 - sigma)))


def unit_grads(rows_x, rows_dy, w_both, w_down, parts, hidden_out):
    hid = w_down.shape[1]
    pre = jnp.dot(rows_x[...], w_both[...], preferred_element_type=F32)
    hidden_grad = jnp.dot(rows_dy[...], w_down[...], preferred_element_type=F32)
    pre_up = pre[:, hid:]
    activated, derivative = silu_parts(pre[:, :hid])
    hidden = activated * pre_up
    parts[:, pl.ds(0, hid)] = (hidden_grad * pre_up * derivative).astype(BF16)
    parts[:, pl.ds(hid, hid)] = (hidden_grad * activated).astype(BF16)
    hidden_out[...] = hidden.astype(BF16)
    return hidden * hidden_grad


def input_term(parts, w_both, first, columns, store):
    def body(i, carry):
        at = pl.multiple_of(i * HALF_TILE, HALF_TILE)
        value = lax.dot_general(
            parts[...], w_both[pl.ds(first + at, HALF_TILE)], NT, preferred_element_type=F32
        )
        store(pl.ds(at, HALF_TILE), value.astype(BF16))
        return carry

    lax.fori_loop(0, columns // HALF_TILE, body, 0)


def lane_sums(value):
    high = value.astype(BF16)
    low = (value - high.astype(F32)).astype(BF16)
    ones = jnp.ones((8, value.shape[1]), BF16)
    return lax.dot_general(ones, high, NT, preferred_element_type=F32) + lax.dot_general(
        ones, low, NT, preferred_element_type=F32
    )


class WeightSums:
    def __init__(self, net, x, z, tensor, grads, first_bufs):
        self.net, self.x, self.z, self.grads = net, x, z, grads
        self.half = half = grads.shape[2] // 2
        self.first_bufs = first_bufs
        pairs = SIDE // 2

        def at(xx, zz):
            return (xx * SIDE + zz, tensor)

        self.around_x = (at(turn(x, 1), z), at(turn(x, 3), z))
        self.around_z = (at(x, turn(z, 1)), at(x, turn(z, 3)))

        def x_part(position, h):
            return grads.at[position, pl.ds(h * pairs, pairs), pl.ds(0, half)]

        def z_part(position, h):
            return grads.at[pl.ds(h * pairs, pairs), position, pl.ds(half, half)]

        def slot(ref, index):
            return lambda h: ref.at[index, pl.ds(h * pairs, pairs)]

        self.rings = [
            RingSum(net, x, *self.around_x, x_part, *(slot(ref, 0) for ref in first_bufs)),
            RingSum(net, z, *self.around_z, z_part, *(slot(ref, 1) for ref in first_bufs)),
        ]

    def middle(self):
        for ring in self.rings:
            ring.absorb()
        for ring in self.rings:
            ring.send_sums()

    def second(self):
        half = self.half
        cut = (0, half // 32 * 16 + 16, half)
        relayed, from_left, from_right = self.first_bufs

        def rows_half(h):
            return pl.ds(cut[h], cut[h + 1] - cut[h])

        def summed(index):
            return lambda position, h: from_left.at[index, position, rows_half(h)]

        def slot(index, k):
            return lambda h: relayed.at[index, k, rows_half(h)]

        later = [
            RingSum(self.net, self.z, *self.around_z, summed(0), *(slot(0, k) for k in range(3))),
            RingSum(self.net, self.x, *self.around_x, summed(1), *(slot(1, k) for k in range(3))),
        ]
        for ring in self.rings:
            ring.finish()
        for steps in (2, 1, 3, 0):
            for index, ring in enumerate(later):
                other = turn((self.z, self.x)[index], steps)
                if index == 0:
                    mine = self.grads.at[self.x, other, pl.ds(0, half)]
                else:
                    mine = self.grads.at[other, self.z, pl.ds(half, half)]
                left, right = from_left.at[index, other], from_right.at[index, other]
                total(left, [mine, left, right])
                if steps == 2:
                    ring.start_far()
                elif steps == 1:
                    ring.start_ahead()
                elif steps == 3:
                    ring.start_behind()
        self.rings = later

    def finish(self, outs):
        half = self.half
        relayed, from_left, unused = self.first_bufs
        for index, ring in enumerate(self.rings):
            ring.finish()
            own = from_left.at[index, (self.z, self.x)[index]]
            for block, ref in enumerate(outs):
                cols = pl.ds(block * ref.shape[1], ref.shape[1])
                total(
                    ref.at[pl.ds(index * half, half)],
                    [own.at[:, cols]] + [relayed.at[index, k, :, cols] for k in (1, 2)],
                    scale=1.0 / (SIDE * SIDE),
                )


def layer_kernel(
    tok, grad, tables, dense_gate, dense_up, dense_down, expert_gate, expert_up, expert_down,
    back, dense_sum, back_shares, out_gate, out_up, out_down, gate_grad, up_grad, down_grad,
    tok_all, grad_all, rows_x, rows_dy, exchange, w_both, w_down, dense_parts, dense_hidden,
    parts, hidden, grads, relayed, from_left, from_right,
    terms, core_rest, y_relayed, y_left, y_right, far_tables,
    shares, share_in, share_sum,
    send_sems, recv_sems, local_sems,
):
    x, z, y, core = place()
    node, tensor = x * SIDE + z, y * CORES + core
    net = Net(send_sems, recv_sems)
    peers = node_peers(x, z, tensor)
    count = SIDE * CORES
    mates = [(node, lax.rem(tensor + k, count)) for k in range(1, count)]
    local_rows, depth = tok.shape
    hid = w_down.shape[1]
    columns = exchange.shape[1]
    stack = exchange.shape[0] // 4
    outgoing = [exchange.at[pl.ds(h * stack, stack)] for h in range(2)]
    landed = [exchange.at[pl.ds((2 + h) * stack, stack)] for h in range(2)]
    block = stack // (SIDE * SIDE)
    slots = stack // 2
    started = []

    def fetch(src, dst):
        copy = pltpu.make_async_copy(src, dst, local_sems.at[len(started)])
        copy.start()
        started.append(copy)
        return copy

    dense = Gather(net, node, y, core, (tok, grad), (tok_all, grad_all), local_rows)
    routed = Gather(net, node, y, core, None, (rows_x, rows_dy), slots)
    routed.own = [routed.chunk(h, tensor) for h in range(2)]
    sums = WeightSums(net, x, z, tensor, grads, (relayed, from_left, from_right))
    meet(peers + mates)

    def rows_of(ref, index):
        return ref.at[pl.ds(pl.multiple_of(index * block, block), block)]

    def fetch_weights(gate, up, down):
        return [
            fetch(gate, w_both.at[:, pl.ds(0, hid)]),
            fetch(up, w_both.at[:, pl.ds(hid, hid)]),
            fetch(down, w_down),
        ]

    dense.start(0)
    dense.start(1)
    exchanged = []
    far = (node, dense.far_at)
    tables_sent = net.start(tables, far_tables, far)
    for h, source in enumerate((tok, grad)):
        out, into = outgoing[h], landed[h]
        left, right = tables.at[2 * h], tables.at[2 * h + 1]
        for first in range(0, columns, 2 * HALF_TILE):
            width = min(2 * HALF_TILE, columns - first)
            value = lax.dot_general(
                left[...], source[:, pl.ds(first, width)], TN, preferred_element_type=F32
            ) + lax.dot_general(
                right[...], source[:, pl.ds(columns + first, width)], TN, preferred_element_type=F32
            )
            out[:, pl.ds(first, width)] = value.astype(BF16)
        exchanged.append(
            [net.start(rows_of(out, peer[0]), rows_of(into, node), peer, False) for peer in peers]
            + [fetch(rows_of(out, node), rows_of(into, node))]
        )
    kept = [
        fetch(tok, dense.chunk(0, tensor)),
        fetch(grad, dense.chunk(1, tensor)),
    ] + fetch_weights(dense_gate, dense_up, dense_down)
    row = lax.broadcasted_iota(jnp.int32, (slots, 2 * slots), 0)
    col = lax.broadcasted_iota(jnp.int32, (slots, 2 * slots), 1)
    half = block // 2
    origin = lax.div(row, half) * block + lax.rem(row, half)
    join_tables = [(col == origin + k * half).astype(F32).astype(BF16) for k in range(2)]
    row = lax.broadcasted_iota(jnp.int32, (2 * slots, slots), 0)
    col = lax.broadcasted_iota(jnp.int32, (2 * slots, slots), 1)
    origin = lax.div(row, block) * half + lax.rem(row, block)
    back_tables = [
        (jnp.logical_and(col == origin - k * half, lax.div(lax.rem(row, block), half) == k))
        .astype(F32)
        .astype(BF16)
        for k in range(2)
    ]

    def join(h):
        for copy in exchanged[h][:-1]:
            copy.wait()
        exchanged[h][-1].wait()
        own, into = routed.own[h], landed[h]
        for first in range(0, columns, 2 * HALF_TILE):
            width = min(2 * HALF_TILE, columns - first)
            cols = pl.ds(first, width)
            for k in range(2):
                own[:, pl.ds(k * columns + first, width)] = jnp.dot(
                    join_tables[k], into[:, cols], preferred_element_type=F32
                ).astype(BF16)

    dense.relay()
    dense.relay_rest()
    join(0)
    routed.start(0)
    dense.relay_far()
    tables_sent.wait_recv()
    quarter = columns // 2
    far_rows = pl.ds(pl.multiple_of(dense.far_at * local_rows, local_rows), local_rows)
    for h, source in enumerate((tok_all, grad_all)):
        for k in range(2):
            value = lax.dot_general(
                far_tables[2 * h], source[far_rows, pl.ds(2 * k * quarter, quarter)], TN,
                preferred_element_type=F32,
            ) + lax.dot_general(
                far_tables[2 * h + 1], source[far_rows, pl.ds((2 * k + 1) * quarter, quarter)], TN,
                preferred_element_type=F32,
            )
            grads[:, :, pl.ds((2 * h + k) * block, block), pl.ds(0, quarter)] = value.astype(
                BF16
            ).reshape(SIDE, SIDE, block, quarter)

    def far_block(ref, index, first):
        at = (lax.div(index, SIDE), lax.rem(index, SIDE), pl.ds(first, 4 * block), pl.ds(0, quarter))
        return ref.at[at]

    far_copies = [
        net.start(far_block(grads, peer[0], 0), far_block(grads, node, 4 * block), peer, False)
        for peer in peers
    ]
    far_kept = fetch(far_block(grads, node, 0), far_block(grads, node, 4 * block))

    def join_far():
        for copy in far_copies:
            copy.wait()
        far_kept.wait()
        for h in range(2):
            into = routed.chunk(h, routed.far_at)
            for k in range(2):
                value = grads[:, :, pl.ds((4 + 2 * h + k) * block, block), pl.ds(0, quarter)]
                value = value.reshape(SIDE * SIDE * block, quarter)
                for q in range(2):
                    into[:, pl.ds((2 * k + q) * quarter, quarter)] = jnp.dot(
                        join_tables[q], value, preferred_element_type=F32
                    ).astype(BF16)
            routed.pass_on(h, routed.far_at, "far")

    join(1)
    routed.start(1)

    for name in ("own", "left", "right", "far"):
        dense.arrive(name)
    for copy in kept:
        copy.wait()
    unit_grads(tok_all, grad_all, w_both, w_down, dense_parts, dense_hidden)

    def side(other_core):
        return lax.rem(core + other_core, CORES)

    for c in range(2):

        def keep_dense(cols, value, c=c):
            for at in range(SIDE):
                for k in range(CORES):
                    first = (at * CORES + k) * local_rows
                    terms[c, side(k), at, pl.ds(slots, local_rows), cols] = value[
                        first : first + local_rows
                    ]

        input_term(dense_parts, w_both, c * columns, columns, keep_dense)
    weights = fetch_weights(expert_gate, expert_up, expert_down)
    for copy in weights:
        copy.wait()

    pair = CORES * slots
    crossed = {}

    def from_core(step, c):
        index, rows = 2 * step + c, slots + local_rows
        fit = exchange.shape[0] // rows
        if index < fit:
            return exchange.at[pl.ds(index * rows, rows)]
        return core_rest.at[index - fit]

    def expert_rows(step, at):
        rows = pl.ds(pl.multiple_of(at * pair, pair), pair)
        product = unit_grads(
            rows_x.at[rows], rows_dy.at[rows], w_both, w_down, parts.at[rows], hidden.at[rows]
        )
        shares[at] = lane_sums(product)
        for c in range(2):

            def keep_routed(cols, value, c=c):
                for k in range(CORES):
                    terms[c, side(k), at, pl.ds(0, slots), cols] = value[k * slots : (k + 1) * slots]

            input_term(parts.at[rows], w_both, c * columns, columns, keep_routed)
            crossed[step, c] = net.start(
                terms.at[c, 1, at], from_core(step, c), routed.partner
            )

    def absorb(step, at, c):
        crossed[step, c].wait_recv()
        mine = terms.at[c, 0, at]
        total(mine, [mine, from_core(step, c)])

    def half_rows(ref, *lead):
        half = ref.shape[-2] // 2
        return lambda h: ref.at[(*lead, pl.ds(h * half, half))]

    y_rings = [
        RingSum(
            net, y, routed.right, routed.left,
            lambda position, h, c=c: half_rows(terms, c, 0, position)(h),
            half_rows(y_relayed, c), half_rows(y_left, c), half_rows(y_right, c),
        )
        for c in range(2)
    ]
    routed.arrive("own")
    expert_rows(0, y)
    routed.take(0)
    routed.take(1)
    routed.arrive("left")
    expert_rows(1, turn(y, 3))
    routed.arrive("right")
    expert_rows(2, turn(y, 1))
    for c in range(2):
        absorb(1, turn(y, 3), c)
        y_rings[c].start_behind()
        absorb(2, turn(y, 1), c)
        y_rings[c].start_ahead()
    join_far()
    band = depth // SIDE
    x_ring, z_ring = sums.rings
    for steps in (2, 1, 3, 0):
        other = turn(x, steps)
        cols = pl.ds(pl.multiple_of(other * band, band), band)
        value = lax.dot_general(
            tok_all[:, cols], dense_parts[...], TN, preferred_element_type=F32
        ).astype(BF16)
        grads[other, :, :, pl.ds(0, 2 * hid)] = value.reshape(SIDE, band // SIDE, 2 * hid)
        value = lax.dot_general(
            grad_all[:, cols], dense_hidden[...], TN, preferred_element_type=F32
        ).astype(BF16)
        grads[other, :, :, pl.ds(2 * hid, hid)] = value.reshape(SIDE, band // SIDE, hid)
        if steps == 2:
            x_ring.start_far()
        elif steps == 1:
            x_ring.start_ahead()
        elif steps == 3:
            x_ring.start_behind()
    z_ring.start_far()
    z_ring.start_ahead()
    z_ring.start_behind()
    routed.arrive("far")
    expert_rows(3, turn(y, 2))
    for c in range(2):
        absorb(3, turn(y, 2), c)
        y_rings[c].start_far()
    share_copies = [
        net.start(shares.at[lax.div(mate[1], CORES)], share_in.at[tensor], mate) for mate in mates
    ]
    for c in range(2):
        absorb(0, y, c)

    written = []

    def weight_tiles(first, last):
        for i in range(first, last):
            cols = pl.ds(i * TILE, TILE)
            w_both[cols] = lax.dot_general(
                rows_x[:, cols], parts[...], TN, preferred_element_type=F32
            ).astype(BF16)
            w_down[cols] = lax.dot_general(
                rows_dy[:, cols], hidden[...], TN, preferred_element_type=F32
            ).astype(BF16)
            written.append(fetch(w_both.at[cols, pl.ds(0, hid)], gate_grad.at[cols]))
            written.append(fetch(w_both.at[cols, pl.ds(hid, hid)], up_grad.at[cols]))
            written.append(fetch(w_down.at[cols], down_grad.at[cols]))

    weight_tiles(0, 2)
    for copy in share_copies:
        copy.wait_recv()
    value = shares[y]
    for k in range(1, count):
        value = value + share_in[lax.rem(tensor + k, count)]
    share_sum[...] = value
    back_shares[node] = value
    returned = [net.start(share_sum, back_shares.at[node], peer) for peer in peers]
    weight_tiles(2, 3)
    y_rings[0].middle()
    weight_tiles(3, 5)
    y_rings[1].middle()
    sums.middle()
    count_tiles = depth // TILE
    short = columns // 2
    for c in range(2):
        weight_tiles(5 + c, 6 + c)
        y_rings[c].finish()
        own, left, right = terms.at[c, 0, y], y_left.at[c], y_right.at[c]
        landed_rows = [ref.at[pl.ds(0, slots)] for ref in (own, left, right)]
        total(own.at[pl.ds(0, slots)], landed_rows)
        for first in range(0, short, HALF_TILE):
            width = min(HALF_TILE, short - first)
            value = jnp.dot(
                back_tables[0], own[pl.ds(0, slots), pl.ds(first, width)], preferred_element_type=F32
            ) + jnp.dot(
                back_tables[1],
                own[pl.ds(0, slots), pl.ds(short + first, width)],
                preferred_element_type=F32,
            )
            for k in range(2):
                y_relayed[c, pl.ds(0, slots), pl.ds(k * short + first, width)] = value[
                    k * slots : (k + 1) * slots
                ].astype(BF16)

        def parted(index, c=c):
            each = slots // block
            rows = pl.multiple_of(lax.rem(index, each) * block, block)
            cols = pl.multiple_of(lax.div(index, each) * short, 128)
            return y_relayed.at[c, pl.ds(rows, block), pl.ds(cols, short)]

        returned += [net.start(parted(peer[0]), rows_of(back.at[c], node), peer) for peer in peers]
        written.append(fetch(parted(node), rows_of(back.at[c], node)))
        total(
            dense_sum.at[:, pl.ds(c * columns, columns)],
            [ref.at[pl.ds(slots, local_rows)] for ref in (own, left, right)],
        )
        if c == 0:
            sums.second()
    sums.middle()
    weight_tiles(7, count_tiles)
    sums.finish((out_gate, out_up, out_down))
    for copy in returned:
        copy.wait_recv()
    for copy in written:
        copy.wait()
    net.drain()


def layer(tokens, out_grad, tables, dense, expert):
    rows, depth = tokens.shape
    hid = dense[0].shape[1]
    count = SIDE * CORES
    nodes = SIDE * SIDE
    slots = tables.shape[2] // 2
    node_rows, slot_rows = count * rows, count * slots
    own = depth // nodes
    half = depth // 2
    bands = (2, SIDE, own // 2, 3 * hid)
    shape = jax.ShapeDtypeStruct
    share = (8, CORES * slots)
    return pl.pallas_call(
        layer_kernel,
        out_shape=[
            shape((2, 2 * slots, half // 2), BF16),
            shape((rows, depth), F32),
            shape((nodes,) + share, F32),
        ]
        + [shape((own, hid), BF16)] * 3
        + [shape((depth, hid), BF16)] * 3,
        in_specs=[VMEM] * 3 + [ANY] * 6,
        out_specs=[ANY] + [VMEM] * 5 + [ANY] * 3,
        scratch_shapes=[
            pltpu.VMEM((node_rows, depth), BF16),
            pltpu.VMEM((node_rows, depth), BF16),
            pltpu.VMEM((slot_rows, depth), BF16),
            pltpu.VMEM((slot_rows, depth), BF16),
            pltpu.VMEM((8 * slots, half), BF16),
            pltpu.VMEM((depth, 2 * hid), BF16),
            pltpu.VMEM((depth, hid), BF16),
            pltpu.VMEM((node_rows, 2 * hid), BF16),
            pltpu.VMEM((node_rows, hid), BF16),
            pltpu.VMEM((slot_rows, 2 * hid), BF16),
            pltpu.VMEM((slot_rows, hid), BF16),
            pltpu.VMEM((SIDE, SIDE, own, 3 * hid), BF16),
        ]
        + [pltpu.VMEM(bands, BF16)] * 3
        + [
            pltpu.VMEM((2, CORES, SIDE, slots + rows, half), BF16),
            pltpu.VMEM((2 * SIDE - 8 * slots // (slots + rows), slots + rows, half), BF16),
        ]
        + [pltpu.VMEM((2, slots + rows, half), BF16)] * 3
        + [
            pltpu.VMEM(tables.shape, BF16),
            pltpu.VMEM((SIDE,) + share, F32),
            pltpu.VMEM((count,) + share, F32),
            pltpu.VMEM(share, F32),
            pltpu.SemaphoreType.DMA((LAYER_COPIES,)),
            pltpu.SemaphoreType.DMA((LAYER_COPIES,)),
            pltpu.SemaphoreType.DMA((36,)),
        ],
        compiler_params=pltpu.CompilerParams(
            collective_id=0, has_side_effects=True, vmem_limit_bytes=VMEM_BYTES
        ),
        name="layer",
    )(tokens, out_grad, tables, *dense, *expert)


def finish_kernel(out_grad, dense_sum, back, tables, *rest):
    sources, input_grad, results = rest[:6], rest[6], rest[7:13]
    buffers, in_sems, out_sems = rest[13:19], rest[19], rest[20]
    loads, stores = [], []
    for source, buffer, result in zip(sources, buffers, results):
        pieces = 1 if source.shape[0] < 1024 else 7
        rows = source.shape[0] // pieces
        for i in range(pieces):
            at = pl.ds(i * rows, rows)
            k = len(loads)
            loads.append(pltpu.make_async_copy(source.at[at], buffer.at[at], in_sems.at[k]))
            stores.append(pltpu.make_async_copy(buffer.at[at], result.at[at], out_sems.at[k]))
            loads[k].start()
    columns = back.shape[2]
    for k in range(4):
        cols = pl.ds(k * columns, columns)
        picked = jnp.dot(tables[k % 2], back[k // 2], preferred_element_type=F32)
        input_grad[:, cols] = (
            out_grad[:, cols].astype(F32) + dense_sum[:, cols] + picked
        ).astype(BF16)
        for load, store in list(zip(loads, stores))[k::4]:
            load.wait()
            store.start()
    for store in stores:
        store.wait()


def finish(out_grad, dense_sum, back, tables, grads):
    return pl.pallas_call(
        finish_kernel,
        out_shape=[jax.ShapeDtypeStruct(out_grad.shape, BF16)]
        + [jax.ShapeDtypeStruct(grad.shape, BF16) for grad in grads],
        in_specs=[VMEM] * 4 + [ANY] * 6,
        out_specs=[VMEM] + [ANY] * 6,
        scratch_shapes=[pltpu.VMEM(grad.shape, BF16) for grad in grads]
        + [pltpu.SemaphoreType.DMA((24,))] * 2,
        compiler_params=pltpu.CompilerParams(vmem_limit_bytes=60 << 20),
        name="finish",
    )(out_grad, dense_sum, back, tables, *grads)


def local(
    tokens, out_grad, gate_weights, expert_ids, dense_gate, dense_up, dense_down,
    expert_gate, expert_up, expert_down,
):
    tok_dev, width = tokens.shape
    nodes = SIDE * SIDE
    capacity = 4 * tok_dev // nodes
    block = 2 * capacity
    flat_ids = expert_ids.reshape(-1)
    pair = jnp.arange(2 * tok_dev, dtype=jnp.int32)
    earlier = (flat_ids[:, None] == flat_ids[None, :]) & (pair[None, :] < pair[:, None])
    slot_index = jnp.sum(earlier.astype(jnp.int32), axis=1)
    position = (flat_ids * block + slot_index).reshape(tok_dev, 2)
    row = jnp.arange(nodes * block, dtype=jnp.int32)[None, :, None]
    offset = jnp.array([0, capacity, 0, capacity], jnp.int32)[:, None, None, None]
    hit = (row == position[:, None, :] + offset).astype(F32)
    weights = jnp.stack([jnp.ones_like(gate_weights), gate_weights]).astype(F32)
    weights = jnp.repeat(weights, 2, axis=0)[:, :, None, :]
    tables = jnp.sum(hit * weights, axis=3).astype(BF16)
    back, dense_sum, back_shares, *sums = layer(
        tokens, out_grad, tables,
        (dense_gate, dense_up, dense_down), (expert_gate[0], expert_up[0], expert_down[0]),
    )
    input_grad, *weight_grads = finish(out_grad, dense_sum, back, tables, sums)
    node, tensor = lax.axis_index("node"), lax.axis_index("tensor")
    start = lax.rem(tensor, CORES) * (nodes * capacity) + node * capacity
    mine = lax.dynamic_slice(back_shares, (0, 0, start), (nodes, 1, capacity)).reshape(1, 1, nodes, capacity)
    expert = jnp.arange(nodes, dtype=jnp.int32)[None, None, :, None]
    slot = jnp.arange(capacity, dtype=jnp.int32)[None, None, None, :]
    chosen = (expert == expert_ids[:, :, None, None]) & (
        slot == slot_index.reshape(tok_dev, 2)[:, :, None, None]
    )
    weighted = jnp.sum(jnp.where(chosen, mine, 0.0), axis=(2, 3))
    gate_weight_grad = weighted / gate_weights.astype(F32)
    return (
        input_grad,
        gate_weight_grad,
        *weight_grads[:3],
        *(value[None] for value in weight_grads[3:]),
    )


def solution(mesh):
    rows = P(("node", "tensor"), None)
    dense = P(None, "tensor")
    expert = P("node", None, "tensor")
    summed = P("node", "tensor")
    return jax.shard_map(
        local,
        mesh=mesh,
        in_specs=(rows,) * 4 + (dense,) * 3 + (expert,) * 3,
        out_specs=(rows, rows) + (summed,) * 3 + (expert,) * 3,
        check_vma=False,
    )
```

```python
import jax
import jax.numpy as jnp
from jax import lax
from jax.experimental import pallas as pl
from jax.experimental.pallas import tpu as pltpu
from jax.sharding import PartitionSpec as P

MESH = pl.DeviceIdType.MESH
BF16 = jnp.bfloat16
F32 = jnp.float32
SIDE = 4
CORES = 2
ANY = pl.BlockSpec(memory_space=pl.ANY)
VMEM = pl.BlockSpec(memory_space=pltpu.VMEM)


def place():
    node = lax.axis_index("node")
    tensor = lax.axis_index("tensor")
    return (
        lax.div(node, SIDE),
        lax.rem(node, SIDE),
        lax.div(tensor, CORES),
        lax.rem(tensor, CORES),
    )


def turn(position, steps):
    return lax.rem(position + steps, SIDE)


def meet(peers):
    barrier = pltpu.get_barrier_semaphore()
    for peer in peers:
        pl.semaphore_signal(barrier, inc=1, device_id=peer, device_id_type=MESH)
    pl.semaphore_wait(barrier, len(peers))


class Net:
    def __init__(self, send_sems, recv_sems):
        self.send_sems, self.recv_sems = send_sems, recv_sems
        self.copies = []
        self.pending = []

    def start(self, src, dst, peer, keep=True):
        index = len(self.copies)
        copy = pltpu.make_async_remote_copy(
            src_ref=src,
            dst_ref=dst,
            send_sem=self.send_sems.at[index],
            recv_sem=self.recv_sems.at[index],
            device_id=peer,
            device_id_type=MESH,
        )
        copy.start()
        self.copies.append(copy)
        if keep:
            self.pending.append(copy)
        return copy

    def drain(self):
        for copy in self.pending:
            copy.wait_send()


def total(dst, sources, scale=None, slab=16):
    rows = dst.shape[-2]
    leads = [()]
    for size in dst.shape[:-2]:
        leads = [lead + (i,) for lead in leads for i in range(size)]
    for lead in leads:

        def body(i, carry, lead=lead):
            at = lead + (pl.ds(pl.multiple_of(i * slab, slab), slab), slice(None))
            value = sources[0][at].astype(F32)
            for source in sources[1:]:
                value = value + source[at].astype(F32)
            if scale is not None:
                value = value * scale
            dst[at] = value.astype(dst.dtype)
            return carry

        lax.fori_loop(0, rows // slab, body, 0)


def node_peers(x, z, tensor):
    peers = []
    for dx in range(SIDE):
        for dz in range(SIDE):
            if dx or dz:
                peers.append((turn(x, dx) * SIDE + turn(z, dz), tensor))
    return peers


class Gather:
    def __init__(self, net, node, y, core, own, whole, rows):
        self.net, self.own, self.whole, self.rows = net, own, whole, rows
        self.me = y * CORES + core
        self.right_at = turn(y, 1) * CORES + core
        self.left_at = turn(y, SIDE - 1) * CORES + core
        self.far_at = turn(y, 2) * CORES + core
        self.right = (node, self.right_at)
        self.left = (node, self.left_at)
        self.partner = (node, y * CORES + 1 - core)
        self.crossed, self.to_right, self.to_left = {}, {}, {}

    def chunk(self, half, at):
        return self.whole[half].at[pl.ds(pl.multiple_of(at * self.rows, self.rows), self.rows)]

    def pass_on(self, half, at, name):
        ref = self.chunk(half, at)
        self.crossed[name, half] = self.net.start(ref, ref, self.partner)

    def start(self, half):
        send = self.net.start
        mine, own = self.chunk(half, self.me), self.own[half]
        self.to_right[half] = send(own, mine, self.right)
        self.to_left[half] = send(own, mine, self.left)
        self.crossed["own", half] = send(own, mine, self.partner)

    def relay(self):
        send = self.net.start
        left_at, right_at = self.left_at, self.right_at
        self.to_right[0].wait_recv()
        self.relay_right = send(self.chunk(0, left_at), self.chunk(0, left_at), self.right)
        self.pass_on(0, left_at, "left")
        self.to_left[1].wait_recv()
        self.relay_left = send(self.chunk(1, right_at), self.chunk(1, right_at), self.left)
        self.pass_on(1, right_at, "right")

    def relay_rest(self):
        self.to_right[1].wait_recv()
        self.pass_on(1, self.left_at, "left")
        self.to_left[0].wait_recv()
        self.pass_on(0, self.right_at, "right")

    def take(self, half):
        self.to_right[half].wait_recv()
        self.pass_on(half, self.left_at, "left")
        self.to_left[half].wait_recv()
        self.pass_on(half, self.right_at, "right")

    def part_of(self, half, at, k):
        rows = self.rows // 2
        first = pl.multiple_of(at * self.rows + k * rows, rows)
        return self.whole[half].at[pl.ds(first, rows)]

    def take_and_relay(self, half):
        send = self.net.start
        self.to_right[half].wait_recv()
        ref = self.part_of(half, self.left_at, 0)
        self.relay_right = send(ref, ref, self.right)
        self.pass_on(half, self.left_at, "left")
        self.to_left[half].wait_recv()
        ref = self.part_of(half, self.right_at, 1)
        self.relay_left = send(ref, ref, self.left)
        self.pass_on(half, self.right_at, "right")

    def take_far(self, half):
        self.relay_right.wait_recv()
        self.relay_left.wait_recv()
        self.pass_on(half, self.far_at, "far")

    def relay_far(self):
        self.relay_right.wait_recv()
        self.pass_on(0, self.far_at, "far")
        self.relay_left.wait_recv()
        self.pass_on(1, self.far_at, "far")

    def arrive(self, name):
        for half in range(2):
            self.crossed[name, half].wait_recv()


class RingSum:
    def __init__(self, net, position, right, left, part, relayed, from_left, from_right):
        self.net, self.right, self.left, self.part = net, right, left, part
        self.relayed, self.from_left, self.from_right = relayed, from_left, from_right
        self.ahead, self.far, self.behind = (turn(position, k) for k in (1, 2, 3))

    def start_far(self):
        send, part = self.net.start, self.part
        self.relay_right = send(part(self.far, 0), self.relayed(0), self.right)
        self.relay_left = send(part(self.far, 1), self.relayed(1), self.left)

    def start_ahead(self):
        self.direct_right = self.net.start(self.part(self.ahead, 1), self.from_left(1), self.right)

    def start_behind(self):
        self.direct_left = self.net.start(self.part(self.behind, 0), self.from_right(0), self.left)

    def middle(self):
        self.absorb()
        self.send_sums()

    def absorb(self):
        self.relay_right.wait_recv()
        mine = self.part(self.ahead, 0)
        total(mine, [mine, self.relayed(0)])
        self.relay_left.wait_recv()
        mine = self.part(self.behind, 1)
        total(mine, [mine, self.relayed(1)])

    def send_sums(self):
        send, part = self.net.start, self.part
        self.sum_right = send(part(self.ahead, 0), self.from_left(0), self.right)
        self.sum_left = send(part(self.behind, 1), self.from_right(1), self.left)

    def finish(self):
        for copy in (self.direct_right, self.direct_left, self.sum_right, self.sum_left):
            copy.wait_recv()


NT = (((1,), (1,)), ((), ()))
TN = (((0,), (0,)), ((), ()))
TILE = 512
HALF_TILE = 256
TERM_TILE = 256
VMEM_BYTES = 63 << 20
LAYER_COPIES = 2 * 14 + 1 + 3 * 15 + 24 + 8 + 12 + 7 + 15 + 2 * 15


def silu_parts(pre_gate):
    sigma = jax.nn.sigmoid(pre_gate)
    return (pre_gate * sigma, sigma * (1.0 + pre_gate * (1.0 - sigma)))


def unit_grads(rows_x, rows_dy, w_both, w_down, parts, hidden_out):
    hid = w_down.shape[1]
    pre = jnp.dot(rows_x[...], w_both[...], preferred_element_type=F32)
    hidden_grad = jnp.dot(rows_dy[...], w_down[...], preferred_element_type=F32)
    pre_up = pre[:, hid:]
    activated, derivative = silu_parts(pre[:, :hid])
    hidden = activated * pre_up
    parts[:, pl.ds(0, hid)] = (hidden_grad * pre_up * derivative).astype(BF16)
    parts[:, pl.ds(hid, hid)] = (hidden_grad * activated).astype(BF16)
    hidden_out[...] = hidden.astype(BF16)
    return hidden * hidden_grad


def input_term(parts, w_both, first, columns, store, tile=TERM_TILE):
    def body(i, carry):
        at = pl.multiple_of(i * tile, tile)
        value = lax.dot_general(
            parts[...], w_both[pl.ds(first + at, tile)], NT, preferred_element_type=F32
        )
        store(pl.ds(at, tile), value.astype(BF16))
        return carry

    lax.fori_loop(0, columns // tile, body, 0)


def lane_sums(value):
    high = value.astype(BF16)
    low = (value - high.astype(F32)).astype(BF16)
    ones = jnp.ones((8, value.shape[1]), BF16)
    return lax.dot_general(ones, high, NT, preferred_element_type=F32) + lax.dot_general(
        ones, low, NT, preferred_element_type=F32
    )


def routing(meta, slots, tokens, block):
    experts = SIDE * SIDE
    expert = lax.broadcasted_iota(jnp.int32, (experts, tokens), 0).astype(F32)
    named = [(expert == meta[k : k + 1, :tokens]).astype(F32) for k in range(2)]
    row = lax.broadcasted_iota(jnp.int32, (tokens, tokens), 0)
    col = lax.broadcasted_iota(jnp.int32, (tokens, tokens), 1)
    earlier = jnp.dot(
        (named[0] + named[1]).astype(BF16),
        (row < col).astype(F32).astype(BF16),
        preferred_element_type=F32,
    )
    slot = [jnp.sum(earlier * hit, axis=0, keepdims=True) for hit in named]
    weight = [meta[2 + k : 3 + k, :tokens] for k in range(2)]
    return named, slot, weight


def routing_tables(meta, slots, tokens, block):
    unused, slot, weight = routing(meta, slots, tokens, block)
    row = lax.broadcasted_iota(jnp.int32, (2 * slots, tokens), 0).astype(F32)
    tables = []
    for weighted in range(2):
        for second in range(2):
            table = jnp.zeros((2 * slots, tokens), F32)
            for k in range(2):
                position = meta[k : k + 1, :tokens] * block + slot[k] + second * (block // 2)
                value = weight[k] if weighted else jnp.ones_like(weight[k])
                table = table + jnp.where(row == position, value, 0.0)
            tables.append(table.astype(BF16))
    return tables


class WeightSums:
    def __init__(self, net, x, z, tensor, grads, first_bufs):
        self.net, self.x, self.z, self.grads = net, x, z, grads
        self.half = half = grads.shape[2] // 2
        self.first_bufs = first_bufs
        pairs = SIDE // 2

        def at(xx, zz):
            return (xx * SIDE + zz, tensor)

        self.around_x = (at(turn(x, 1), z), at(turn(x, 3), z))
        self.around_z = (at(x, turn(z, 1)), at(x, turn(z, 3)))

        def x_part(position, h):
            return grads.at[position, pl.ds(h * pairs, pairs), pl.ds(0, half)]

        def z_part(position, h):
            return grads.at[pl.ds(h * pairs, pairs), position, pl.ds(half, half)]

        def slot(ref, index):
            return lambda h: ref.at[index, pl.ds(h * pairs, pairs)]

        self.rings = [
            RingSum(net, x, *self.around_x, x_part, *(slot(ref, 0) for ref in first_bufs)),
            RingSum(net, z, *self.around_z, z_part, *(slot(ref, 1) for ref in first_bufs)),
        ]

    def middle(self):
        for ring in self.rings:
            ring.absorb()
        for ring in self.rings:
            ring.send_sums()

    def second(self):
        half = self.half
        cut = (0, half // 32 * 16 + 16, half)
        relayed, from_left, from_right = self.first_bufs

        def rows_half(h):
            return pl.ds(cut[h], cut[h + 1] - cut[h])

        def summed(index):
            return lambda position, h: from_left.at[index, position, rows_half(h)]

        def slot(index, k):
            return lambda h: relayed.at[index, k, rows_half(h)]

        later = [
            RingSum(self.net, self.z, *self.around_z, summed(0), *(slot(0, k) for k in range(3))),
            RingSum(self.net, self.x, *self.around_x, summed(1), *(slot(1, k) for k in range(3))),
        ]
        for ring in self.rings:
            ring.finish()
        for steps in (2, 1, 3, 0):
            for index, ring in enumerate(later):
                other = turn((self.z, self.x)[index], steps)
                if index == 0:
                    mine = self.grads.at[self.x, other, pl.ds(0, half)]
                else:
                    mine = self.grads.at[other, self.z, pl.ds(half, half)]
                left, right = from_left.at[index, other], from_right.at[index, other]
                total(left, [mine, left, right])
                if steps == 2:
                    ring.start_far()
                elif steps == 1:
                    ring.start_ahead()
                elif steps == 3:
                    ring.start_behind()
        self.rings = later

    def finish(self, outs):
        half = self.half
        relayed, from_left, unused = self.first_bufs
        for index, ring in enumerate(self.rings):
            ring.finish()
            own = from_left.at[index, (self.z, self.x)[index]]
            for block, ref in enumerate(outs):
                cols = pl.ds(block * ref.shape[1], ref.shape[1])
                total(
                    ref.at[pl.ds(index * half, half)],
                    [own.at[:, cols]] + [relayed.at[index, k, :, cols] for k in (1, 2)],
                    scale=1.0 / (SIDE * SIDE),
                )


def layer_kernel(
    tok, grad, meta, dense_gate, dense_up, dense_down, expert_gate, expert_up, expert_down,
    back, dense_sum, back_shares, out_gate, out_up, out_down, gate_grad, up_grad, down_grad,
    tok_all, grad_all, rows_x, rows_dy, exchange, w_both, w_down, parts, hidden, grads, relayed, from_left, from_right,
    terms, core_rest, y_relayed, y_left, y_right, far_meta,
    shares, share_in, share_sum,
    send_sems, recv_sems, local_sems,
):
    x, z, y, core = place()
    node, tensor = x * SIDE + z, y * CORES + core
    net = Net(send_sems, recv_sems)
    peers = node_peers(x, z, tensor)
    count = SIDE * CORES
    mates = [(node, lax.rem(tensor + k, count)) for k in range(1, count)]
    local_rows, depth = tok.shape
    hid = w_down.shape[1]
    columns = exchange.shape[1]
    stack = exchange.shape[0] // 4
    outgoing = [exchange.at[pl.ds(h * stack, stack)] for h in range(2)]
    landed = [exchange.at[pl.ds((2 + h) * stack, stack)] for h in range(2)]
    block = stack // (SIDE * SIDE)
    slots = stack // 2
    far_pair = pl.ds(pl.multiple_of(turn(y, 2) * stack, stack), stack)
    dense_parts, dense_hidden = parts.at[far_pair], hidden.at[far_pair]
    started = []

    def fetch(src, dst):
        copy = pltpu.make_async_copy(src, dst, local_sems.at[len(started)])
        copy.start()
        started.append(copy)
        return copy

    dense = Gather(net, node, y, core, (tok, grad), (tok_all, grad_all), local_rows)
    routed = Gather(net, node, y, core, None, (rows_x, rows_dy), slots)
    routed.own = [routed.chunk(h, tensor) for h in range(2)]
    sums = WeightSums(net, x, z, tensor, grads, (relayed, from_left, from_right))
    meet(peers + mates)

    def rows_of(ref, index):
        return ref.at[pl.ds(pl.multiple_of(index * block, block), block)]

    def fetch_weights(gate, up, down):
        return [
            fetch(gate, w_both.at[:, pl.ds(0, hid)]),
            fetch(up, w_both.at[:, pl.ds(hid, hid)]),
            fetch(down, w_down),
        ]

    dense.start(0)
    dense.start(1)
    exchanged = []
    meta_sent = net.start(meta, far_meta, (node, dense.far_at))
    tables = routing_tables(meta[...], slots, local_rows, block)
    for h, source in enumerate((tok, grad)):
        out, into = outgoing[h], landed[h]
        left, right = tables[2 * h], tables[2 * h + 1]
        for first in range(0, columns, 2 * HALF_TILE):
            width = min(2 * HALF_TILE, columns - first)
            value = jnp.dot(
                left, source[:, pl.ds(first, width)], preferred_element_type=F32
            ) + jnp.dot(right, source[:, pl.ds(columns + first, width)], preferred_element_type=F32)
            out[:, pl.ds(first, width)] = value.astype(BF16)
        exchanged.append(
            [net.start(rows_of(out, peer[0]), rows_of(into, node), peer, False) for peer in peers]
            + [fetch(rows_of(out, node), rows_of(into, node))]
        )
    kept = [
        fetch(tok, dense.chunk(0, tensor)),
        fetch(grad, dense.chunk(1, tensor)),
    ] + fetch_weights(dense_gate, dense_up, dense_down)
    row = lax.broadcasted_iota(jnp.int32, (slots, 2 * slots), 0)
    col = lax.broadcasted_iota(jnp.int32, (slots, 2 * slots), 1)
    half = block // 2
    origin = lax.div(row, half) * block + lax.rem(row, half)
    join_tables = [(col == origin + k * half).astype(F32).astype(BF16) for k in range(2)]
    row = lax.broadcasted_iota(jnp.int32, (2 * slots, slots), 0)
    col = lax.broadcasted_iota(jnp.int32, (2 * slots, slots), 1)
    origin = lax.div(row, block) * half + lax.rem(row, block)
    back_tables = [
        (jnp.logical_and(col == origin - k * half, lax.div(lax.rem(row, block), half) == k))
        .astype(F32)
        .astype(BF16)
        for k in range(2)
    ]

    def join(h):
        for copy in exchanged[h][:-1]:
            copy.wait()
        exchanged[h][-1].wait()
        own, into = routed.own[h], landed[h]
        for first in range(0, columns, 2 * HALF_TILE):
            width = min(2 * HALF_TILE, columns - first)
            cols = pl.ds(first, width)
            for k in range(2):
                own[:, pl.ds(k * columns + first, width)] = jnp.dot(
                    join_tables[k], into[:, cols], preferred_element_type=F32
                ).astype(BF16)

    dense.relay()
    dense.relay_rest()
    join(0)
    routed.start(0)
    dense.relay_far()
    meta_sent.wait_recv()
    tables = routing_tables(far_meta[...], slots, local_rows, block)[:2]
    far_rows = pl.ds(pl.multiple_of(dense.far_at * local_rows, local_rows), local_rows)
    far_y = turn(y, 2)
    for first in range(0, columns, 2 * HALF_TILE):
        width = min(2 * HALF_TILE, columns - first)
        value = (
            jnp.dot(tables[0], tok_all[far_rows, pl.ds(first, width)], preferred_element_type=F32)
            + jnp.dot(
                tables[1],
                tok_all[far_rows, pl.ds(columns + first, width)],
                preferred_element_type=F32,
            )
        ).astype(BF16)
        for c in range(2):
            terms[c, 1, far_y, pl.ds(0, slots), pl.ds(first, width)] = value[
                c * slots : (c + 1) * slots
            ]
    each = SIDE * SIDE // 2

    def far_leaving(index):
        rows = pl.ds(pl.multiple_of(lax.rem(index, each) * block, block), block)
        return terms.at[lax.div(index, each), 1, far_y, rows]

    def far_landing(index):
        rows = pl.ds(pl.multiple_of(lax.rem(index, each) * block, block), block)
        return core_rest.at[lax.div(index, each), rows]

    far_copies = [
        net.start(far_leaving(peer[0]), far_landing(node), peer, False) for peer in peers
    ]
    far_kept = fetch(far_leaving(node), far_landing(node))

    def join_far():
        for copy in far_copies:
            copy.wait()
        far_kept.wait()
        for c in range(2):
            rows = pl.ds(pl.multiple_of(routed.far_at * slots + c * (slots // 2), slots // 2), slots // 2)
            for first in range(0, columns, 2 * HALF_TILE):
                width = min(2 * HALF_TILE, columns - first)
                value = core_rest[c, pl.ds(0, slots), pl.ds(first, width)]
                for k in range(2):
                    rows_x[rows, pl.ds(k * columns + first, width)] = jnp.dot(
                        join_tables[k][: slots // 2, :slots], value, preferred_element_type=F32
                    ).astype(BF16)
        routed.pass_on(0, routed.far_at, "far")

    join(1)
    routed.start(1)

    for name in ("own", "left", "right", "far"):
        dense.arrive(name)
    for copy in kept:
        copy.wait()
    unit_grads(tok_all, grad_all, w_both, w_down, dense_parts, dense_hidden)

    def side(other_core):
        return lax.rem(core + other_core, CORES)

    for c in range(2):

        def keep_dense(cols, value, c=c):
            for at in range(SIDE):
                for k in range(CORES):
                    first = (at * CORES + k) * local_rows
                    terms[c, side(k), at, pl.ds(slots, local_rows), cols] = value[
                        first : first + local_rows
                    ]

        input_term(dense_parts, w_both, c * columns, columns, keep_dense)
    weights = fetch_weights(expert_gate, expert_up, expert_down)
    band = depth // SIDE
    x_ring, z_ring = sums.rings
    for steps in (2, 1, 3, 0):
        other = turn(x, steps)
        cols = pl.ds(pl.multiple_of(other * band, band), band)
        value = lax.dot_general(
            tok_all[:, cols], dense_parts[...], TN, preferred_element_type=F32
        ).astype(BF16)
        grads[other, :, :, pl.ds(0, 2 * hid)] = value.reshape(SIDE, band // SIDE, 2 * hid)
        value = lax.dot_general(
            grad_all[:, cols], dense_hidden[...], TN, preferred_element_type=F32
        ).astype(BF16)
        grads[other, :, :, pl.ds(2 * hid, hid)] = value.reshape(SIDE, band // SIDE, hid)
        if steps == 2:
            x_ring.start_far()
        elif steps == 1:
            x_ring.start_ahead()
        elif steps == 3:
            x_ring.start_behind()
    z_ring.start_far()
    z_ring.start_ahead()
    z_ring.start_behind()
    for copy in weights:
        copy.wait()

    pair = CORES * slots
    crossed = {}

    def from_core(step, c):
        index, rows = 2 * step + c, slots + local_rows
        fit = exchange.shape[0] // rows
        if index < fit:
            return exchange.at[pl.ds(index * rows, rows)]
        return core_rest.at[index - fit]

    def expert_rows(step, at):
        rows = pl.ds(pl.multiple_of(at * pair, pair), pair)
        product = unit_grads(
            rows_x.at[rows], rows_dy.at[rows], w_both, w_down, parts.at[rows], hidden.at[rows]
        )
        shares[at] = lane_sums(product)
        for c in range(2):

            def keep_routed(cols, value, c=c):
                for k in range(CORES):
                    terms[c, side(k), at, pl.ds(0, slots), cols] = value[k * slots : (k + 1) * slots]

            input_term(parts.at[rows], w_both, c * columns, columns, keep_routed)
            crossed[step, c] = net.start(
                terms.at[c, 1, at], from_core(step, c), routed.partner
            )

    def absorb(step, at, c):
        crossed[step, c].wait_recv()
        mine = terms.at[c, 0, at]
        total(mine, [mine, from_core(step, c)])

    def half_rows(ref, *lead):
        half = ref.shape[-2] // 2
        return lambda h: ref.at[(*lead, pl.ds(h * half, half))]

    y_rings = [
        RingSum(
            net, y, routed.right, routed.left,
            lambda position, h, c=c: half_rows(terms, c, 0, position)(h),
            half_rows(y_relayed, c), half_rows(y_left, c), half_rows(y_right, c),
        )
        for c in range(2)
    ]
    routed.arrive("own")
    expert_rows(0, y)
    routed.take(0)
    join_far()
    sums.middle()
    routed.take_and_relay(1)
    routed.arrive("left")
    expert_rows(1, turn(y, 3))
    for c in range(2):
        absorb(1, turn(y, 3), c)
        y_rings[c].start_behind()
    routed.arrive("right")
    expert_rows(2, turn(y, 1))
    for c in range(2):
        absorb(2, turn(y, 1), c)
        y_rings[c].start_ahead()
    routed.take_far(1)
    routed.arrive("far")
    expert_rows(3, turn(y, 2))
    for c in range(2):
        absorb(3, turn(y, 2), c)
        y_rings[c].start_far()
    share_copies = [
        net.start(shares.at[lax.div(mate[1], CORES)], share_in.at[tensor], mate) for mate in mates
    ]
    for c in range(2):
        absorb(0, y, c)

    written = []

    def weight_tiles(first, last):
        for i in range(first, last):
            cols = pl.ds(i * TILE, TILE)
            w_both[cols] = lax.dot_general(
                rows_x[:, cols], parts[...], TN, preferred_element_type=F32
            ).astype(BF16)
            w_down[cols] = lax.dot_general(
                rows_dy[:, cols], hidden[...], TN, preferred_element_type=F32
            ).astype(BF16)
            written.append(fetch(w_both.at[cols, pl.ds(0, hid)], gate_grad.at[cols]))
            written.append(fetch(w_both.at[cols, pl.ds(hid, hid)], up_grad.at[cols]))
            written.append(fetch(w_down.at[cols], down_grad.at[cols]))

    weight_tiles(0, 2)
    for copy in share_copies:
        copy.wait_recv()
    value = shares[y]
    for k in range(1, count):
        value = value + share_in[lax.rem(tensor + k, count)]
    share_sum[...] = value
    back_shares[node] = value
    returned = [net.start(share_sum, back_shares.at[node], peer) for peer in peers]
    sums.second()
    y_rings[0].middle()
    weight_tiles(2, 4)
    y_rings[1].middle()
    weight_tiles(4, 5)
    sums.middle()
    count_tiles = depth // TILE
    short = columns // 2
    for c in range(2):
        weight_tiles(5 + c, 6 + c)
        y_rings[c].finish()
        own, left, right = terms.at[c, 0, y], y_left.at[c], y_right.at[c]
        landed_rows = [ref.at[pl.ds(0, slots)] for ref in (own, left, right)]
        total(own.at[pl.ds(0, slots)], landed_rows)
        for first in range(0, short, HALF_TILE):
            width = min(HALF_TILE, short - first)
            value = jnp.dot(
                back_tables[0], own[pl.ds(0, slots), pl.ds(first, width)], preferred_element_type=F32
            ) + jnp.dot(
                back_tables[1],
                own[pl.ds(0, slots), pl.ds(short + first, width)],
                preferred_element_type=F32,
            )
            for k in range(2):
                y_relayed[c, pl.ds(0, slots), pl.ds(k * short + first, width)] = value[
                    k * slots : (k + 1) * slots
                ].astype(BF16)

        def parted(index, c=c):
            each = slots // block
            rows = pl.multiple_of(lax.rem(index, each) * block, block)
            cols = pl.multiple_of(lax.div(index, each) * short, 128)
            return y_relayed.at[c, pl.ds(rows, block), pl.ds(cols, short)]

        returned += [net.start(parted(peer[0]), rows_of(back.at[c], node), peer) for peer in peers]
        written.append(fetch(parted(node), rows_of(back.at[c], node)))
        total(
            dense_sum.at[:, pl.ds(c * columns, columns)],
            [ref.at[pl.ds(slots, local_rows)] for ref in (own, left, right)],
        )
    weight_tiles(7, count_tiles)
    sums.finish((out_gate, out_up, out_down))
    for copy in returned:
        copy.wait_recv()
    for copy in written:
        copy.wait()
    net.drain()


def layer(tokens, out_grad, meta, slots, dense, expert):
    rows, depth = tokens.shape
    hid = dense[0].shape[1]
    count = SIDE * CORES
    nodes = SIDE * SIDE
    node_rows, slot_rows = count * rows, count * slots
    own = depth // nodes
    half = depth // 2
    bands = (2, SIDE, own // 2, 3 * hid)
    shape = jax.ShapeDtypeStruct
    share = (8, CORES * slots)
    return pl.pallas_call(
        layer_kernel,
        out_shape=[
            shape((2, 2 * slots, half // 2), BF16),
            shape((rows, depth), F32),
            shape((nodes,) + share, F32),
        ]
        + [shape((own, hid), BF16)] * 3
        + [shape((depth, hid), BF16)] * 3,
        in_specs=[VMEM] * 3 + [ANY] * 6,
        out_specs=[ANY] + [VMEM] * 5 + [ANY] * 3,
        scratch_shapes=[
            pltpu.VMEM((node_rows, depth), BF16),
            pltpu.VMEM((node_rows, depth), BF16),
            pltpu.VMEM((slot_rows, depth), BF16),
            pltpu.VMEM((slot_rows, depth), BF16),
            pltpu.VMEM((8 * slots, half), BF16),
            pltpu.VMEM((depth, 2 * hid), BF16),
            pltpu.VMEM((depth, hid), BF16),
            pltpu.VMEM((slot_rows, 2 * hid), BF16),
            pltpu.VMEM((slot_rows, hid), BF16),
            pltpu.VMEM((SIDE, SIDE, own, 3 * hid), BF16),
        ]
        + [pltpu.VMEM(bands, BF16)] * 3
        + [
            pltpu.VMEM((2, CORES, SIDE, slots + rows, half), BF16),
            pltpu.VMEM((2 * SIDE - 8 * slots // (slots + rows), slots + rows, half), BF16),
        ]
        + [pltpu.VMEM((2, slots + rows, half), BF16)] * 3
        + [
            pltpu.VMEM(meta.shape, F32),
            pltpu.VMEM((SIDE,) + share, F32),
            pltpu.VMEM((count,) + share, F32),
            pltpu.VMEM(share, F32),
            pltpu.SemaphoreType.DMA((LAYER_COPIES,)),
            pltpu.SemaphoreType.DMA((LAYER_COPIES,)),
            pltpu.SemaphoreType.DMA((36,)),
        ],
        compiler_params=pltpu.CompilerParams(
            collective_id=0, has_side_effects=True, vmem_limit_bytes=VMEM_BYTES
        ),
        name="layer",
    )(tokens, out_grad, meta, *dense, *expert)


def finish_kernel(out_grad, dense_sum, back, meta, back_shares, *rest):
    sources, input_grad, share, results = rest[:6], rest[6], rest[7], rest[8:14]
    buffers, in_sems, out_sems = rest[14:20], rest[20], rest[21]
    loads, stores = [], []
    for source, buffer, result in zip(sources, buffers, results):
        pieces = 1 if source.shape[0] < 1024 else 7
        rows = source.shape[0] // pieces
        for i in range(pieces):
            at = pl.ds(i * rows, rows)
            k = len(loads)
            loads.append(pltpu.make_async_copy(source.at[at], buffer.at[at], in_sems.at[k]))
            stores.append(pltpu.make_async_copy(buffer.at[at], result.at[at], out_sems.at[k]))
            loads[k].start()
    nodes, tokens = SIDE * SIDE, out_grad.shape[0]
    slots, columns = back.shape[1] // 2, back.shape[2]
    block = 2 * slots // nodes
    named, slot, weight = routing(meta[...], slots, tokens, block)
    first = lax.axis_index("node") * (block // 2)
    first = first + lax.rem(lax.axis_index("tensor"), CORES) * slots
    lane = lax.broadcasted_iota(jnp.int32, (block // 2, CORES * slots), 1)
    wanted = lax.broadcasted_iota(jnp.int32, (block // 2, CORES * slots), 0) + first
    wanted = (lane == wanted).astype(F32).astype(BF16)

    def split(value):
        high = value.astype(BF16)
        return high, (value - high.astype(F32)).astype(BF16)

    mine = sum(
        lax.dot_general(wanted, part, NT, preferred_element_type=F32)
        for part in split(back_shares[:, 0, :])
    )
    index = lax.broadcasted_iota(jnp.int32, (block // 2, tokens), 0).astype(F32)
    for k in range(2):
        value = sum(
            jnp.dot(part, named[k].astype(BF16), preferred_element_type=F32) for part in split(mine)
        )
        value = jnp.sum(jnp.where(index == slot[k], value, 0.0), axis=0, keepdims=True)
        share[pl.ds(k, 1), :] = value / weight[k]
    for load, store in zip(loads, stores):
        load.wait()
        store.start()
    tables = routing_tables(meta[...], slots, tokens, block)
    for k in range(4):
        cols = pl.ds(k * columns, columns)
        picked = lax.dot_general(tables[k % 2], back[k // 2], TN, preferred_element_type=F32)
        input_grad[:, cols] = (
            out_grad[:, cols].astype(F32) + dense_sum[:, cols] + picked
        ).astype(BF16)
    for store in stores:
        store.wait()


def finish(out_grad, dense_sum, back, meta, back_shares, grads):
    return pl.pallas_call(
        finish_kernel,
        out_shape=[
            jax.ShapeDtypeStruct(out_grad.shape, BF16),
            jax.ShapeDtypeStruct((2, out_grad.shape[0]), F32),
        ]
        + [jax.ShapeDtypeStruct(grad.shape, BF16) for grad in grads],
        in_specs=[VMEM] * 5 + [ANY] * 6,
        out_specs=[VMEM] * 2 + [ANY] * 6,
        scratch_shapes=[pltpu.VMEM(grad.shape, BF16) for grad in grads]
        + [pltpu.SemaphoreType.DMA((24,))] * 2,
        compiler_params=pltpu.CompilerParams(vmem_limit_bytes=60 << 20),
        name="finish",
    )(out_grad, dense_sum, back, meta, back_shares, *grads)


def local(
    tokens, out_grad, gate_weights, expert_ids, dense_gate, dense_up, dense_down,
    expert_gate, expert_up, expert_down,
):
    slots = 4 * tokens.shape[0]
    meta = jnp.concatenate([expert_ids.T.astype(F32), gate_weights.T.astype(F32)], axis=0)
    meta = jnp.pad(meta, ((0, 4), (0, 128 - meta.shape[1])))
    back, dense_sum, back_shares, *sums = layer(
        tokens, out_grad, meta, slots, (dense_gate, dense_up, dense_down),
        (expert_gate[0], expert_up[0], expert_down[0]),
    )
    input_grad, share, *sums = finish(out_grad, dense_sum, back, meta, back_shares, sums)
    return (input_grad, share.T, *sums[:3], *(value[None] for value in sums[3:]))


def solution(mesh):
    rows = P(("node", "tensor"), None)
    dense = P(None, "tensor")
    expert = P("node", None, "tensor")
    summed = P("node", "tensor")
    return jax.shard_map(
        local,
        mesh=mesh,
        in_specs=(rows,) * 4 + (dense,) * 3 + (expert,) * 3,
        out_specs=(rows, rows) + (summed,) * 3 + (expert,) * 3,
        check_vma=False,
    )
```

```python
import jax
import jax.numpy as jnp
from jax import lax
from jax.experimental import pallas as pl
from jax.experimental.pallas import tpu as pltpu
from jax.sharding import PartitionSpec as P

MESH = pl.DeviceIdType.MESH
BF16 = jnp.bfloat16
F32 = jnp.float32
SIDE = 4
CORES = 2
ANY = pl.BlockSpec(memory_space=pl.ANY)
VMEM = pl.BlockSpec(memory_space=pltpu.VMEM)


def place():
    node = lax.axis_index("node")
    tensor = lax.axis_index("tensor")
    return (
        lax.div(node, SIDE),
        lax.rem(node, SIDE),
        lax.div(tensor, CORES),
        lax.rem(tensor, CORES),
    )


def turn(position, steps):
    return lax.rem(position + steps, SIDE)


def meet(peers):
    barrier = pltpu.get_barrier_semaphore()
    for peer in peers:
        pl.semaphore_signal(barrier, inc=1, device_id=peer, device_id_type=MESH)
    pl.semaphore_wait(barrier, len(peers))


class Net:
    def __init__(self, send_sems, recv_sems):
        self.send_sems, self.recv_sems = send_sems, recv_sems
        self.copies = []
        self.pending = []

    def start(self, src, dst, peer, keep=True):
        index = len(self.copies)
        copy = pltpu.make_async_remote_copy(
            src_ref=src,
            dst_ref=dst,
            send_sem=self.send_sems.at[index],
            recv_sem=self.recv_sems.at[index],
            device_id=peer,
            device_id_type=MESH,
        )
        copy.start()
        self.copies.append(copy)
        if keep:
            self.pending.append(copy)
        return copy

    def drain(self):
        for copy in self.pending:
            copy.wait_send()


def total(dst, sources, scale=None, slab=16):
    rows = dst.shape[-2]
    leads = [()]
    for size in dst.shape[:-2]:
        leads = [lead + (i,) for lead in leads for i in range(size)]
    for lead in leads:

        def body(i, carry, lead=lead):
            at = lead + (pl.ds(pl.multiple_of(i * slab, slab), slab), slice(None))
            value = sources[0][at].astype(F32)
            for source in sources[1:]:
                value = value + source[at].astype(F32)
            if scale is not None:
                value = value * scale
            dst[at] = value.astype(dst.dtype)
            return carry

        lax.fori_loop(0, rows // slab, body, 0)


def node_peers(x, z, tensor):
    peers = []
    for dx in range(SIDE):
        for dz in range(SIDE):
            if dx or dz:
                peers.append((turn(x, dx) * SIDE + turn(z, dz), tensor))
    return peers


class Gather:
    def __init__(self, net, node, y, core, own, whole, rows):
        self.net, self.own, self.whole, self.rows = net, own, whole, rows
        self.me = y * CORES + core
        self.right_at = turn(y, 1) * CORES + core
        self.left_at = turn(y, SIDE - 1) * CORES + core
        self.far_at = turn(y, 2) * CORES + core
        self.right = (node, self.right_at)
        self.left = (node, self.left_at)
        self.partner = (node, y * CORES + 1 - core)
        self.sent = []
        self.crossed, self.to_right, self.to_left = {}, {}, {}

    def send(self, src, dst, peer):
        self.sent.append(self.net.start(src, dst, peer, False))
        return self.sent[-1]

    def flush(self):
        for copy in self.sent:
            copy.wait_send()

    def chunk(self, half, at):
        return self.whole[half].at[pl.ds(pl.multiple_of(at * self.rows, self.rows), self.rows)]

    def pass_on(self, half, at, name):
        ref = self.chunk(half, at)
        self.crossed[name, half] = self.send(ref, ref, self.partner)

    def start(self, half):
        send = self.send
        mine, own = self.chunk(half, self.me), self.own[half]
        self.to_right[half] = send(own, mine, self.right)
        self.to_left[half] = send(own, mine, self.left)
        self.crossed["own", half] = send(own, mine, self.partner)

    def relay(self):
        send = self.send
        left_at, right_at = self.left_at, self.right_at
        self.to_right[0].wait_recv()
        self.relay_right = send(self.chunk(0, left_at), self.chunk(0, left_at), self.right)
        self.pass_on(0, left_at, "left")
        self.to_left[1].wait_recv()
        self.relay_left = send(self.chunk(1, right_at), self.chunk(1, right_at), self.left)
        self.pass_on(1, right_at, "right")

    def relay_rest(self):
        self.to_right[1].wait_recv()
        self.pass_on(1, self.left_at, "left")
        self.to_left[0].wait_recv()
        self.pass_on(0, self.right_at, "right")

    def take(self, half):
        self.to_right[half].wait_recv()
        self.pass_on(half, self.left_at, "left")
        self.to_left[half].wait_recv()
        self.pass_on(half, self.right_at, "right")

    def part_of(self, half, at, k):
        rows = self.rows // 2
        first = pl.multiple_of(at * self.rows + k * rows, rows)
        return self.whole[half].at[pl.ds(first, rows)]

    def take_and_relay(self, half):
        send = self.send
        self.to_right[half].wait_recv()
        ref = self.part_of(half, self.left_at, 0)
        self.relay_right = send(ref, ref, self.right)
        self.pass_on(half, self.left_at, "left")
        self.to_left[half].wait_recv()
        ref = self.part_of(half, self.right_at, 1)
        self.relay_left = send(ref, ref, self.left)
        self.pass_on(half, self.right_at, "right")

    def take_far(self, half):
        self.relay_right.wait_recv()
        self.relay_left.wait_recv()
        self.pass_on(half, self.far_at, "far")

    def relay_far(self):
        self.relay_right.wait_recv()
        self.pass_on(0, self.far_at, "far")
        self.relay_left.wait_recv()
        self.pass_on(1, self.far_at, "far")

    def arrive(self, name, halves=(0, 1)):
        for half in halves:
            self.crossed[name, half].wait_recv()


class RingSum:
    def __init__(self, net, position, right, left, part, relayed, from_left, from_right):
        self.net, self.right, self.left, self.part = net, right, left, part
        self.relayed, self.from_left, self.from_right = relayed, from_left, from_right
        self.ahead, self.far, self.behind = (turn(position, k) for k in (1, 2, 3))

    def start_far(self):
        send, part = self.net.start, self.part
        self.relay_right = send(part(self.far, 0), self.relayed(0), self.right)
        self.relay_left = send(part(self.far, 1), self.relayed(1), self.left)

    def start_ahead(self):
        self.direct_right = self.net.start(self.part(self.ahead, 1), self.from_left(1), self.right)

    def start_behind(self):
        self.direct_left = self.net.start(self.part(self.behind, 0), self.from_right(0), self.left)

    def middle(self):
        self.absorb()
        self.send_sums()

    def absorb(self):
        self.relay_right.wait_recv()
        mine = self.part(self.ahead, 0)
        total(mine, [mine, self.relayed(0)])
        self.relay_left.wait_recv()
        mine = self.part(self.behind, 1)
        total(mine, [mine, self.relayed(1)])

    def send_sums(self):
        send, part = self.net.start, self.part
        self.sum_right = send(part(self.ahead, 0), self.from_left(0), self.right)
        self.sum_left = send(part(self.behind, 1), self.from_right(1), self.left)

    def finish(self):
        for copy in (self.direct_right, self.direct_left, self.sum_right, self.sum_left):
            copy.wait_recv()


NT = (((1,), (1,)), ((), ()))
TN = (((0,), (0,)), ((), ()))
TILE = 512
HALF_TILE = 256
TERM_TILE = 256
VMEM_BYTES = 63 << 20
LAYER_COPIES = 2 * 14 + 1 + 3 * 15 + 24 + 8 + 12 + 7 + 15 + 2 * 15


def silu_parts(pre_gate):
    sigma = jax.nn.sigmoid(pre_gate)
    return (pre_gate * sigma, sigma * (1.0 + pre_gate * (1.0 - sigma)))


def unit_grads(rows_x, rows_dy, w_both, w_down, parts, hidden_out, pre=None):
    hid = w_down.shape[1]
    if pre is None:
        pre = jnp.dot(rows_x[...], w_both[...], preferred_element_type=F32)
    hidden_grad = jnp.dot(rows_dy[...], w_down[...], preferred_element_type=F32)
    pre_up = pre[:, hid:]
    activated, derivative = silu_parts(pre[:, :hid])
    hidden = activated * pre_up
    parts[:, pl.ds(0, hid)] = (hidden_grad * pre_up * derivative).astype(BF16)
    parts[:, pl.ds(hid, hid)] = (hidden_grad * activated).astype(BF16)
    hidden_out[...] = hidden.astype(BF16)
    return hidden * hidden_grad


def input_term(parts, w_both, first, columns, store, tile=TERM_TILE):
    def body(i, carry):
        at = pl.multiple_of(i * tile, tile)
        value = lax.dot_general(
            parts[...], w_both[pl.ds(first + at, tile)], NT, preferred_element_type=F32
        )
        store(pl.ds(at, tile), value.astype(BF16))
        return carry

    lax.fori_loop(0, columns // tile, body, 0)


def lane_sums(value):
    high = value.astype(BF16)
    low = (value - high.astype(F32)).astype(BF16)
    ones = jnp.ones((8, value.shape[1]), BF16)
    return lax.dot_general(ones, high, NT, preferred_element_type=F32) + lax.dot_general(
        ones, low, NT, preferred_element_type=F32
    )


def routing(meta, slots, tokens, block):
    experts = SIDE * SIDE
    expert = lax.broadcasted_iota(jnp.int32, (experts, tokens), 0).astype(F32)
    named = [(expert == meta[k : k + 1, :tokens]).astype(F32) for k in range(2)]
    row = lax.broadcasted_iota(jnp.int32, (tokens, tokens), 0)
    col = lax.broadcasted_iota(jnp.int32, (tokens, tokens), 1)
    earlier = jnp.dot(
        (named[0] + named[1]).astype(BF16),
        (row < col).astype(F32).astype(BF16),
        preferred_element_type=F32,
    )
    slot = [jnp.sum(earlier * hit, axis=0, keepdims=True) for hit in named]
    weight = [meta[2 + k : 3 + k, :tokens] for k in range(2)]
    return named, slot, weight


def routing_tables(meta, slots, tokens, block):
    unused, slot, weight = routing(meta, slots, tokens, block)
    row = lax.broadcasted_iota(jnp.int32, (2 * slots, tokens), 0).astype(F32)
    tables = []
    for weighted in range(2):
        for second in range(2):
            table = jnp.zeros((2 * slots, tokens), F32)
            for k in range(2):
                position = meta[k : k + 1, :tokens] * block + slot[k] + second * (block // 2)
                value = weight[k] if weighted else jnp.ones_like(weight[k])
                table = table + jnp.where(row == position, value, 0.0)
            tables.append(table.astype(BF16))
    return tables


def fill(meta, ids, weights):
    tokens = ids.shape[1]
    meta[...] = jnp.zeros_like(meta)
    meta[pl.ds(0, 2), pl.ds(0, tokens)] = ids[...].astype(F32)
    meta[pl.ds(2, 2), pl.ds(0, tokens)] = weights[...].astype(F32)


class WeightSums:
    def __init__(self, net, x, z, tensor, grads, first_bufs):
        self.net, self.x, self.z, self.grads = net, x, z, grads
        self.half = half = grads.shape[2] // 2
        self.first_bufs = first_bufs
        pairs = SIDE // 2

        def at(xx, zz):
            return (xx * SIDE + zz, tensor)

        self.around_x = (at(turn(x, 1), z), at(turn(x, 3), z))
        self.around_z = (at(x, turn(z, 1)), at(x, turn(z, 3)))

        def x_part(position, h):
            return grads.at[position, pl.ds(h * pairs, pairs), pl.ds(0, half)]

        def z_part(position, h):
            return grads.at[pl.ds(h * pairs, pairs), position, pl.ds(half, half)]

        def slot(ref, index):
            return lambda h: ref.at[index, pl.ds(h * pairs, pairs)]

        self.rings = [
            RingSum(net, x, *self.around_x, x_part, *(slot(ref, 0) for ref in first_bufs)),
            RingSum(net, z, *self.around_z, z_part, *(slot(ref, 1) for ref in first_bufs)),
        ]

    def middle(self):
        for ring in self.rings:
            ring.absorb()
        for ring in self.rings:
            ring.send_sums()

    def second(self):
        half = self.half
        cut = (0, half // 32 * 16 + 16, half)
        relayed, from_left, from_right = self.first_bufs

        def rows_half(h):
            return pl.ds(cut[h], cut[h + 1] - cut[h])

        def summed(index):
            return lambda position, h: from_left.at[index, position, rows_half(h)]

        def slot(index, k):
            return lambda h: relayed.at[index, k, rows_half(h)]

        later = [
            RingSum(self.net, self.z, *self.around_z, summed(0), *(slot(0, k) for k in range(3))),
            RingSum(self.net, self.x, *self.around_x, summed(1), *(slot(1, k) for k in range(3))),
        ]
        for ring in self.rings:
            ring.finish()
        for steps in (2, 1, 3, 0):
            for index, ring in enumerate(later):
                other = turn((self.z, self.x)[index], steps)
                if index == 0:
                    mine = self.grads.at[self.x, other, pl.ds(0, half)]
                else:
                    mine = self.grads.at[other, self.z, pl.ds(half, half)]
                left, right = from_left.at[index, other], from_right.at[index, other]
                total(left, [mine, left, right])
                if steps == 2:
                    ring.start_far()
                elif steps == 1:
                    ring.start_ahead()
                elif steps == 3:
                    ring.start_behind()
        self.rings = later

    def finish(self, outs):
        half = self.half
        relayed, from_left, unused = self.first_bufs
        for index, ring in enumerate(self.rings):
            ring.finish()
            own = from_left.at[index, (self.z, self.x)[index]]
            for block, ref in enumerate(outs):
                cols = pl.ds(block * ref.shape[1], ref.shape[1])
                total(
                    ref.at[pl.ds(index * half, half)],
                    [own.at[:, cols]] + [relayed.at[index, k, :, cols] for k in (1, 2)],
                    scale=1.0 / (SIDE * SIDE),
                )


def layer_kernel(
    tok, grad, ids, gates, dense_gate, dense_up, dense_down, expert_gate, expert_up, expert_down,
    back, dense_sum, back_shares, out_gate, out_up, out_down, gate_grad, up_grad, down_grad,
    tok_all, grad_all, rows_x, rows_dy, exchange, w_both, w_down, parts, hidden, grads, relayed, from_left, from_right,
    terms, core_rest, y_relayed, y_left, y_right, meta, far_meta,
    shares, share_in, share_sum,
    send_sems, recv_sems, local_sems,
):
    x, z, y, core = place()
    node, tensor = x * SIDE + z, y * CORES + core
    net = Net(send_sems, recv_sems)
    peers = node_peers(x, z, tensor)
    count = SIDE * CORES
    mates = [(node, lax.rem(tensor + k, count)) for k in range(1, count)]
    local_rows, depth = tok.shape
    hid = w_down.shape[1]
    columns = exchange.shape[1]
    stack = exchange.shape[0] // 4
    outgoing = [exchange.at[pl.ds(h * stack, stack)] for h in range(2)]
    landed = [exchange.at[pl.ds((2 + h) * stack, stack)] for h in range(2)]
    block = stack // (SIDE * SIDE)
    slots = stack // 2
    far_pair = pl.ds(pl.multiple_of(turn(y, 2) * stack, stack), stack)
    dense_parts, dense_hidden = parts.at[far_pair], hidden.at[far_pair]
    started = []

    def fetch(src, dst):
        copy = pltpu.make_async_copy(src, dst, local_sems.at[len(started)])
        copy.start()
        started.append(copy)
        return copy

    dense = Gather(net, node, y, core, (tok, grad), (tok_all, grad_all), local_rows)
    routed = Gather(net, node, y, core, None, (rows_x, rows_dy), slots)
    routed.own = [routed.chunk(h, tensor) for h in range(2)]
    sums = WeightSums(net, x, z, tensor, grads, (relayed, from_left, from_right))
    meet(peers + mates)

    def rows_of(ref, index):
        return ref.at[pl.ds(pl.multiple_of(index * block, block), block)]

    def fetch_weights(gate, up, down):
        return [
            fetch(gate, w_both.at[:, pl.ds(0, hid)]),
            fetch(up, w_both.at[:, pl.ds(hid, hid)]),
            fetch(down, w_down),
        ]

    dense.start(0)
    dense.start(1)
    exchanged = []
    fill(meta, ids, gates)
    meta_sent = net.start(meta, far_meta, (node, dense.far_at))
    tables = routing_tables(meta[...], slots, local_rows, block)
    for h, source in enumerate((tok, grad)):
        out, into = outgoing[h], landed[h]
        left, right = tables[2 * h], tables[2 * h + 1]
        for first in range(0, columns, 2 * HALF_TILE):
            width = min(2 * HALF_TILE, columns - first)
            value = jnp.dot(
                left, source[:, pl.ds(first, width)], preferred_element_type=F32
            ) + jnp.dot(right, source[:, pl.ds(columns + first, width)], preferred_element_type=F32)
            out[:, pl.ds(first, width)] = value.astype(BF16)
        exchanged.append(
            [net.start(rows_of(out, peer[0]), rows_of(into, node), peer, False) for peer in peers]
            + [fetch(rows_of(out, node), rows_of(into, node))]
        )
    kept = [
        fetch(tok, dense.chunk(0, tensor)),
        fetch(grad, dense.chunk(1, tensor)),
    ] + fetch_weights(dense_gate, dense_up, dense_down)
    row = lax.broadcasted_iota(jnp.int32, (slots, 2 * slots), 0)
    col = lax.broadcasted_iota(jnp.int32, (slots, 2 * slots), 1)
    half = block // 2
    origin = lax.div(row, half) * block + lax.rem(row, half)
    join_tables = [(col == origin + k * half).astype(F32).astype(BF16) for k in range(2)]
    row = lax.broadcasted_iota(jnp.int32, (2 * slots, slots), 0)
    col = lax.broadcasted_iota(jnp.int32, (2 * slots, slots), 1)
    origin = lax.div(row, block) * half + lax.rem(row, block)
    back_tables = [
        (jnp.logical_and(col == origin - k * half, lax.div(lax.rem(row, block), half) == k))
        .astype(F32)
        .astype(BF16)
        for k in range(2)
    ]

    def join(h):
        for copy in exchanged[h][:-1]:
            copy.wait()
        exchanged[h][-1].wait()
        own, into = routed.own[h], landed[h]
        for first in range(0, columns, 2 * HALF_TILE):
            width = min(2 * HALF_TILE, columns - first)
            cols = pl.ds(first, width)
            for k in range(2):
                own[:, pl.ds(k * columns + first, width)] = jnp.dot(
                    join_tables[k], into[:, cols], preferred_element_type=F32
                ).astype(BF16)

    dense.relay()
    dense.relay_rest()
    join(0)
    routed.start(0)
    dense.relay_far()
    meta_sent.wait_recv()
    tables = routing_tables(far_meta[...], slots, local_rows, block)[:2]
    far_rows = pl.ds(pl.multiple_of(dense.far_at * local_rows, local_rows), local_rows)
    far_y = turn(y, 2)
    for first in range(0, columns, 2 * HALF_TILE):
        width = min(2 * HALF_TILE, columns - first)
        value = (
            jnp.dot(tables[0], tok_all[far_rows, pl.ds(first, width)], preferred_element_type=F32)
            + jnp.dot(
                tables[1],
                tok_all[far_rows, pl.ds(columns + first, width)],
                preferred_element_type=F32,
            )
        ).astype(BF16)
        for c in range(2):
            terms[c, 1, far_y, pl.ds(0, slots), pl.ds(first, width)] = value[
                c * slots : (c + 1) * slots
            ]
    each = SIDE * SIDE // 2

    def far_leaving(index):
        rows = pl.ds(pl.multiple_of(lax.rem(index, each) * block, block), block)
        return terms.at[lax.div(index, each), 1, far_y, rows]

    def far_landing(index):
        rows = pl.ds(pl.multiple_of(lax.rem(index, each) * block, block), block)
        return core_rest.at[lax.div(index, each), rows]

    far_copies = [
        net.start(far_leaving(peer[0]), far_landing(node), peer, False) for peer in peers
    ]
    far_kept = fetch(far_leaving(node), far_landing(node))

    def join_far():
        for copy in far_copies:
            copy.wait()
        far_kept.wait()
        for c in range(2):
            rows = pl.ds(pl.multiple_of(routed.far_at * slots + c * (slots // 2), slots // 2), slots // 2)
            for first in range(0, columns, 2 * HALF_TILE):
                width = min(2 * HALF_TILE, columns - first)
                value = core_rest[c, pl.ds(0, slots), pl.ds(first, width)]
                for k in range(2):
                    rows_x[rows, pl.ds(k * columns + first, width)] = jnp.dot(
                        join_tables[k][: slots // 2, :slots], value, preferred_element_type=F32
                    ).astype(BF16)
        routed.pass_on(0, routed.far_at, "far")

    join(1)
    routed.start(1)

    for name in ("own", "left", "right", "far"):
        dense.arrive(name)
    for copy in kept:
        copy.wait()
    unit_grads(tok_all, grad_all, w_both, w_down, dense_parts, dense_hidden)

    def side(other_core):
        return lax.rem(core + other_core, CORES)

    for c in range(2):

        def keep_dense(cols, value, c=c):
            for at in range(SIDE):
                for k in range(CORES):
                    first = (at * CORES + k) * local_rows
                    terms[c, side(k), at, pl.ds(slots, local_rows), cols] = value[
                        first : first + local_rows
                    ]

        input_term(dense_parts, w_both, c * columns, columns, keep_dense)
    weights = fetch_weights(expert_gate, expert_up, expert_down)
    band = depth // SIDE
    x_ring, z_ring = sums.rings
    for steps in (2, 1, 3, 0):
        other = turn(x, steps)
        cols = pl.ds(pl.multiple_of(other * band, band), band)
        value = lax.dot_general(
            tok_all[:, cols], dense_parts[...], TN, preferred_element_type=F32
        ).astype(BF16)
        grads[other, :, :, pl.ds(0, 2 * hid)] = value.reshape(SIDE, band // SIDE, 2 * hid)
        value = lax.dot_general(
            grad_all[:, cols], dense_hidden[...], TN, preferred_element_type=F32
        ).astype(BF16)
        grads[other, :, :, pl.ds(2 * hid, hid)] = value.reshape(SIDE, band // SIDE, hid)
        if steps == 2:
            x_ring.start_far()
        elif steps == 1:
            x_ring.start_ahead()
        elif steps == 3:
            x_ring.start_behind()
    z_ring.start_far()
    z_ring.start_ahead()
    z_ring.start_behind()
    for copy in weights:
        copy.wait()

    pair = CORES * slots
    crossed = {}

    def from_core(step, c):
        index, rows = 2 * step + c, slots + local_rows
        fit = exchange.shape[0] // rows
        if index < fit:
            return exchange.at[pl.ds(index * rows, rows)]
        return core_rest.at[index - fit]

    def early_place(step):
        ref, first = ((tok_all, 0), (tok_all, 4 * hid), (grad_all, 0))[step - 1]
        return [ref.at[:, pl.ds(first + k * 2 * hid, 2 * hid)] for k in range(2)]

    def early_rows(step, at):
        rows = pl.ds(pl.multiple_of(at * pair, pair), pair)
        pre = jnp.dot(rows_x[rows], w_both[...], preferred_element_type=F32)
        high, low = early_place(step)
        rounded = pre.astype(BF16)
        high[...] = rounded
        low[...] = (pre - rounded.astype(F32)).astype(BF16)

    def expert_rows(step, at):
        rows = pl.ds(pl.multiple_of(at * pair, pair), pair)
        pre = None
        if step:
            high, low = early_place(step)
            pre = high[...].astype(F32) + low[...].astype(F32)
        product = unit_grads(
            rows_x.at[rows], rows_dy.at[rows], w_both, w_down, parts.at[rows], hidden.at[rows], pre
        )
        shares[at] = lane_sums(product)
        for c in range(2):

            def keep_routed(cols, value, c=c):
                for k in range(CORES):
                    terms[c, side(k), at, pl.ds(0, slots), cols] = value[k * slots : (k + 1) * slots]

            input_term(parts.at[rows], w_both, c * columns, columns, keep_routed)
            crossed[step, c] = net.start(
                terms.at[c, 1, at], from_core(step, c), routed.partner
            )

    def absorb(step, at, c):
        crossed[step, c].wait_recv()
        mine = terms.at[c, 0, at]
        total(mine, [mine, from_core(step, c)])

    def half_rows(ref, *lead):
        half = ref.shape[-2] // 2
        return lambda h: ref.at[(*lead, pl.ds(h * half, half))]

    y_rings = [
        RingSum(
            net, y, routed.right, routed.left,
            lambda position, h, c=c: half_rows(terms, c, 0, position)(h),
            half_rows(y_relayed, c), half_rows(y_left, c), half_rows(y_right, c),
        )
        for c in range(2)
    ]
    routed.arrive("own")
    expert_rows(0, y)
    routed.take(0)
    join_far()
    dense.flush()
    for step, (name, at) in enumerate((("left", 3), ("right", 1), ("far", 2))):
        routed.arrive(name, (0,))
        early_rows(step + 1, turn(y, at))
    routed.take_and_relay(1)
    sums.middle()
    routed.arrive("left", (1,))
    expert_rows(1, turn(y, 3))
    for c in range(2):
        absorb(1, turn(y, 3), c)
        y_rings[c].start_behind()
    routed.arrive("right", (1,))
    expert_rows(2, turn(y, 1))
    for c in range(2):
        absorb(2, turn(y, 1), c)
        y_rings[c].start_ahead()
    routed.take_far(1)
    routed.arrive("far", (1,))
    expert_rows(3, turn(y, 2))
    for c in range(2):
        absorb(3, turn(y, 2), c)
        y_rings[c].start_far()
    sums.second()
    share_copies = [
        net.start(shares.at[lax.div(mate[1], CORES)], share_in.at[tensor], mate) for mate in mates
    ]
    for c in range(2):
        absorb(0, y, c)

    written = []

    def weight_tiles(first, last):
        for i in range(first, last):
            cols = pl.ds(i * TILE, TILE)
            w_both[cols] = lax.dot_general(
                rows_x[:, cols], parts[...], TN, preferred_element_type=F32
            ).astype(BF16)
            w_down[cols] = lax.dot_general(
                rows_dy[:, cols], hidden[...], TN, preferred_element_type=F32
            ).astype(BF16)
            written.append(fetch(w_both.at[cols, pl.ds(0, hid)], gate_grad.at[cols]))
            written.append(fetch(w_both.at[cols, pl.ds(hid, hid)], up_grad.at[cols]))
            written.append(fetch(w_down.at[cols], down_grad.at[cols]))

    weight_tiles(0, 2)
    for copy in share_copies:
        copy.wait_recv()
    value = shares[y]
    for k in range(1, count):
        value = value + share_in[lax.rem(tensor + k, count)]
    share_sum[...] = value
    back_shares[node] = value
    returned = [net.start(share_sum, back_shares.at[node], peer) for peer in peers]
    y_rings[0].middle()
    weight_tiles(2, 4)
    y_rings[1].middle()
    weight_tiles(4, 5)
    sums.middle()
    count_tiles = depth // TILE
    short = columns // 2
    for c in range(2):
        weight_tiles(5 + c, 6 + c)
        y_rings[c].finish()
        own, left, right = terms.at[c, 0, y], y_left.at[c], y_right.at[c]
        landed_rows = [ref.at[pl.ds(0, slots)] for ref in (own, left, right)]
        total(own.at[pl.ds(0, slots)], landed_rows)
        for first in range(0, short, HALF_TILE):
            width = min(HALF_TILE, short - first)
            value = jnp.dot(
                back_tables[0], own[pl.ds(0, slots), pl.ds(first, width)], preferred_element_type=F32
            ) + jnp.dot(
                back_tables[1],
                own[pl.ds(0, slots), pl.ds(short + first, width)],
                preferred_element_type=F32,
            )
            for k in range(2):
                y_relayed[c, pl.ds(0, slots), pl.ds(k * short + first, width)] = value[
                    k * slots : (k + 1) * slots
                ].astype(BF16)

        def parted(index, c=c):
            each = slots // block
            rows = pl.multiple_of(lax.rem(index, each) * block, block)
            cols = pl.multiple_of(lax.div(index, each) * short, 128)
            return y_relayed.at[c, pl.ds(rows, block), pl.ds(cols, short)]

        returned += [net.start(parted(peer[0]), rows_of(back.at[c], node), peer) for peer in peers]
        written.append(fetch(parted(node), rows_of(back.at[c], node)))
        total(
            dense_sum.at[:, pl.ds(c * columns, columns)],
            [ref.at[pl.ds(slots, local_rows)] for ref in (own, left, right)],
        )
    weight_tiles(7, count_tiles)
    sums.finish((out_gate, out_up, out_down))
    for copy in returned:
        copy.wait_recv()
    for copy in written:
        copy.wait()
    routed.flush()
    net.drain()


def layer(tokens, out_grad, ids, gates, slots, dense, expert):
    rows, depth = tokens.shape
    hid = dense[0].shape[1]
    count = SIDE * CORES
    nodes = SIDE * SIDE
    node_rows, slot_rows = count * rows, count * slots
    own = depth // nodes
    half = depth // 2
    bands = (2, SIDE, own // 2, 3 * hid)
    shape = jax.ShapeDtypeStruct
    share = (8, CORES * slots)
    return pl.pallas_call(
        layer_kernel,
        out_shape=[
            shape((2, 2 * slots, half // 2), BF16),
            shape((rows, depth), F32),
            shape((nodes,) + share, F32),
        ]
        + [shape((own, hid), BF16)] * 3
        + [shape((depth, hid), BF16)] * 3,
        in_specs=[VMEM] * 4 + [ANY] * 6,
        out_specs=[ANY] + [VMEM] * 5 + [ANY] * 3,
        scratch_shapes=[
            pltpu.VMEM((node_rows, depth), BF16),
            pltpu.VMEM((node_rows, depth), BF16),
            pltpu.VMEM((slot_rows, depth), BF16),
            pltpu.VMEM((slot_rows, depth), BF16),
            pltpu.VMEM((8 * slots, half), BF16),
            pltpu.VMEM((depth, 2 * hid), BF16),
            pltpu.VMEM((depth, hid), BF16),
            pltpu.VMEM((slot_rows, 2 * hid), BF16),
            pltpu.VMEM((slot_rows, hid), BF16),
            pltpu.VMEM((SIDE, SIDE, own, 3 * hid), BF16),
        ]
        + [pltpu.VMEM(bands, BF16)] * 3
        + [
            pltpu.VMEM((2, CORES, SIDE, slots + rows, half), BF16),
            pltpu.VMEM((2 * SIDE - 8 * slots // (slots + rows), slots + rows, half), BF16),
        ]
        + [pltpu.VMEM((2, slots + rows, half), BF16)] * 3
        + [
            pltpu.VMEM((8, 128), F32),
            pltpu.VMEM((8, 128), F32),
            pltpu.VMEM((SIDE,) + share, F32),
            pltpu.VMEM((count,) + share, F32),
            pltpu.VMEM(share, F32),
            pltpu.SemaphoreType.DMA((LAYER_COPIES,)),
            pltpu.SemaphoreType.DMA((LAYER_COPIES,)),
            pltpu.SemaphoreType.DMA((36,)),
        ],
        compiler_params=pltpu.CompilerParams(
            collective_id=0, has_side_effects=True, vmem_limit_bytes=VMEM_BYTES
        ),
        name="layer",
    )(tokens, out_grad, ids, gates, *dense, *expert)


def finish_kernel(out_grad, dense_sum, back, ids, gates, back_shares, *rest):
    sources, input_grad, share, results = rest[:6], rest[6], rest[7], rest[8:14]
    buffers, in_sems, out_sems, meta = rest[14:20], rest[20], rest[21], rest[22]
    loads, stores = [], []
    for source, buffer, result in zip(sources, buffers, results):
        pieces = 1 if source.shape[0] < 1024 else 7
        rows = source.shape[0] // pieces
        for i in range(pieces):
            at = pl.ds(i * rows, rows)
            k = len(loads)
            loads.append(pltpu.make_async_copy(source.at[at], buffer.at[at], in_sems.at[k]))
            stores.append(pltpu.make_async_copy(buffer.at[at], result.at[at], out_sems.at[k]))
            loads[k].start()
    nodes, tokens = SIDE * SIDE, out_grad.shape[0]
    slots, columns = back.shape[1] // 2, back.shape[2]
    block = 2 * slots // nodes
    fill(meta, ids, gates)
    named, slot, weight = routing(meta[...], slots, tokens, block)
    first = lax.axis_index("node") * (block // 2)
    first = first + lax.rem(lax.axis_index("tensor"), CORES) * slots
    lane = lax.broadcasted_iota(jnp.int32, (block // 2, CORES * slots), 1)
    wanted = lax.broadcasted_iota(jnp.int32, (block // 2, CORES * slots), 0) + first
    wanted = (lane == wanted).astype(F32).astype(BF16)

    def split(value):
        high = value.astype(BF16)
        return high, (value - high.astype(F32)).astype(BF16)

    mine = sum(
        lax.dot_general(wanted, part, NT, preferred_element_type=F32)
        for part in split(back_shares[:, 0, :])
    )
    index = lax.broadcasted_iota(jnp.int32, (block // 2, tokens), 0).astype(F32)
    for k in range(2):
        value = sum(
            jnp.dot(part, named[k].astype(BF16), preferred_element_type=F32) for part in split(mine)
        )
        value = jnp.sum(jnp.where(index == slot[k], value, 0.0), axis=0, keepdims=True)
        share[pl.ds(k, 1), :] = value / weight[k]
    for load, store in zip(loads, stores):
        load.wait()
        store.start()
    tables = routing_tables(meta[...], slots, tokens, block)
    for k in range(4):
        cols = pl.ds(k * columns, columns)
        picked = lax.dot_general(tables[k % 2], back[k // 2], TN, preferred_element_type=F32)
        input_grad[:, cols] = (
            out_grad[:, cols].astype(F32) + dense_sum[:, cols] + picked
        ).astype(BF16)
    for store in stores:
        store.wait()


def finish(out_grad, dense_sum, back, ids, gates, back_shares, grads):
    return pl.pallas_call(
        finish_kernel,
        out_shape=[
            jax.ShapeDtypeStruct(out_grad.shape, BF16),
            jax.ShapeDtypeStruct((2, out_grad.shape[0]), F32),
        ]
        + [jax.ShapeDtypeStruct(grad.shape, BF16) for grad in grads],
        in_specs=[VMEM] * 6 + [ANY] * 6,
        out_specs=[VMEM] * 2 + [ANY] * 6,
        scratch_shapes=[pltpu.VMEM(grad.shape, BF16) for grad in grads]
        + [pltpu.SemaphoreType.DMA((24,))] * 2
        + [pltpu.VMEM((8, 128), F32)],
        compiler_params=pltpu.CompilerParams(vmem_limit_bytes=60 << 20),
        name="finish",
    )(out_grad, dense_sum, back, ids, gates, back_shares, *grads)


def local(
    tokens, out_grad, gate_weights, expert_ids, dense_gate, dense_up, dense_down,
    expert_gate, expert_up, expert_down,
):
    slots = 4 * tokens.shape[0]
    ids, gates = expert_ids.T, gate_weights.T
    back, dense_sum, back_shares, *sums = layer(
        tokens, out_grad, ids, gates, slots, (dense_gate, dense_up, dense_down),
        (expert_gate[0], expert_up[0], expert_down[0]),
    )
    input_grad, share, *sums = finish(out_grad, dense_sum, back, ids, gates, back_shares, sums)
    return (input_grad, share.T, *sums[:3], *(value[None] for value in sums[3:]))


def solution(mesh):
    rows = P(("node", "tensor"), None)
    dense = P(None, "tensor")
    expert = P("node", None, "tensor")
    summed = P("node", "tensor")
    return jax.shard_map(
        local,
        mesh=mesh,
        in_specs=(rows,) * 4 + (dense,) * 3 + (expert,) * 3,
        out_specs=(rows, rows) + (summed,) * 3 + (expert,) * 3,
        check_vma=False,
    )
```

```python
import jax
import jax.numpy as jnp
from jax import lax
from jax.experimental import pallas as pl
from jax.experimental.pallas import tpu as pltpu
from jax.sharding import PartitionSpec as P

MESH = pl.DeviceIdType.MESH
BF16 = jnp.bfloat16
F32 = jnp.float32
SIDE = 4
CORES = 2
ANY = pl.BlockSpec(memory_space=pl.ANY)
VMEM = pl.BlockSpec(memory_space=pltpu.VMEM)


def place():
    node = lax.axis_index("node")
    tensor = lax.axis_index("tensor")
    return (
        lax.div(node, SIDE),
        lax.rem(node, SIDE),
        lax.div(tensor, CORES),
        lax.rem(tensor, CORES),
    )


def turn(position, steps):
    return lax.rem(position + steps, SIDE)


def meet(peers):
    barrier = pltpu.get_barrier_semaphore()
    for peer in peers:
        pl.semaphore_signal(barrier, inc=1, device_id=peer, device_id_type=MESH)
    pl.semaphore_wait(barrier, len(peers))


class Net:
    def __init__(self, send_sems, recv_sems):
        self.send_sems, self.recv_sems = send_sems, recv_sems
        self.copies = []
        self.pending = []

    def start(self, src, dst, peer, keep=True):
        index = len(self.copies)
        copy = pltpu.make_async_remote_copy(
            src_ref=src,
            dst_ref=dst,
            send_sem=self.send_sems.at[index],
            recv_sem=self.recv_sems.at[index],
            device_id=peer,
            device_id_type=MESH,
        )
        copy.start()
        self.copies.append(copy)
        if keep:
            self.pending.append(copy)
        return copy

    def drain(self):
        for copy in self.pending:
            copy.wait_send()


def total(dst, sources, scale=None, slab=16):
    rows = dst.shape[-2]
    leads = [()]
    for size in dst.shape[:-2]:
        leads = [lead + (i,) for lead in leads for i in range(size)]
    for lead in leads:

        def body(i, carry, lead=lead):
            at = lead + (pl.ds(pl.multiple_of(i * slab, slab), slab), slice(None))
            value = sources[0][at].astype(F32)
            for source in sources[1:]:
                value = value + source[at].astype(F32)
            if scale is not None:
                value = value * scale
            dst[at] = value.astype(dst.dtype)
            return carry

        lax.fori_loop(0, rows // slab, body, 0)


def node_peers(x, z, tensor):
    peers = []
    for dx in range(SIDE):
        for dz in range(SIDE):
            if dx or dz:
                peers.append((turn(x, dx) * SIDE + turn(z, dz), tensor))
    return peers


class Gather:
    def __init__(self, net, node, y, core, own, whole, rows):
        self.net, self.own, self.whole, self.rows = net, own, whole, rows
        self.me = y * CORES + core
        self.right_at = turn(y, 1) * CORES + core
        self.left_at = turn(y, SIDE - 1) * CORES + core
        self.far_at = turn(y, 2) * CORES + core
        self.right = (node, self.right_at)
        self.left = (node, self.left_at)
        self.partner = (node, y * CORES + 1 - core)
        self.sent = []
        self.crossed, self.to_right, self.to_left = {}, {}, {}

    def send(self, src, dst, peer):
        self.sent.append(self.net.start(src, dst, peer, False))
        return self.sent[-1]

    def flush(self):
        for copy in self.sent:
            copy.wait_send()

    def chunk(self, half, at):
        return self.whole[half].at[pl.ds(pl.multiple_of(at * self.rows, self.rows), self.rows)]

    def pass_on(self, half, at, name):
        ref = self.chunk(half, at)
        self.crossed[name, half] = self.send(ref, ref, self.partner)

    def start(self, half):
        send = self.send
        mine, own = self.chunk(half, self.me), self.own[half]
        self.to_right[half] = send(own, mine, self.right)
        self.to_left[half] = send(own, mine, self.left)
        self.crossed["own", half] = send(own, mine, self.partner)

    def relay(self):
        send = self.send
        left_at, right_at = self.left_at, self.right_at
        self.to_right[0].wait_recv()
        self.relay_right = send(self.chunk(0, left_at), self.chunk(0, left_at), self.right)
        self.pass_on(0, left_at, "left")
        self.to_left[1].wait_recv()
        self.relay_left = send(self.chunk(1, right_at), self.chunk(1, right_at), self.left)
        self.pass_on(1, right_at, "right")

    def relay_rest(self):
        self.to_right[1].wait_recv()
        self.pass_on(1, self.left_at, "left")
        self.to_left[0].wait_recv()
        self.pass_on(0, self.right_at, "right")

    def take(self, half):
        self.to_right[half].wait_recv()
        self.pass_on(half, self.left_at, "left")
        self.to_left[half].wait_recv()
        self.pass_on(half, self.right_at, "right")

    def part_of(self, half, at, k):
        rows = self.rows // 2
        first = pl.multiple_of(at * self.rows + k * rows, rows)
        return self.whole[half].at[pl.ds(first, rows)]

    def take_and_relay(self, half):
        send = self.send
        self.to_right[half].wait_recv()
        ref = self.part_of(half, self.left_at, 0)
        self.relay_right = send(ref, ref, self.right)
        self.pass_on(half, self.left_at, "left")
        self.to_left[half].wait_recv()
        ref = self.part_of(half, self.right_at, 1)
        self.relay_left = send(ref, ref, self.left)
        self.pass_on(half, self.right_at, "right")

    def take_far(self, half):
        self.relay_right.wait_recv()
        self.relay_left.wait_recv()
        self.pass_on(half, self.far_at, "far")

    def relay_far(self):
        self.relay_right.wait_recv()
        self.pass_on(0, self.far_at, "far")
        self.relay_left.wait_recv()
        self.pass_on(1, self.far_at, "far")

    def arrive(self, name, halves=(0, 1)):
        for half in halves:
            self.crossed[name, half].wait_recv()


class RingSum:
    def __init__(self, net, position, right, left, part, relayed, from_left, from_right):
        self.net, self.right, self.left, self.part = net, right, left, part
        self.relayed, self.from_left, self.from_right = relayed, from_left, from_right
        self.ahead, self.far, self.behind = (turn(position, k) for k in (1, 2, 3))

    def start_far(self):
        send, part = self.net.start, self.part
        self.relay_right = send(part(self.far, 0), self.relayed(0), self.right)
        self.relay_left = send(part(self.far, 1), self.relayed(1), self.left)

    def start_ahead(self):
        self.direct_right = self.net.start(self.part(self.ahead, 1), self.from_left(1), self.right)

    def start_behind(self):
        self.direct_left = self.net.start(self.part(self.behind, 0), self.from_right(0), self.left)

    def middle(self):
        self.absorb()
        self.send_sums()

    def absorb(self):
        self.relay_right.wait_recv()
        mine = self.part(self.ahead, 0)
        total(mine, [mine, self.relayed(0)])
        self.relay_left.wait_recv()
        mine = self.part(self.behind, 1)
        total(mine, [mine, self.relayed(1)])

    def send_sums(self):
        send, part = self.net.start, self.part
        self.sum_right = send(part(self.ahead, 0), self.from_left(0), self.right)
        self.sum_left = send(part(self.behind, 1), self.from_right(1), self.left)

    def finish(self):
        for copy in (self.direct_right, self.direct_left, self.sum_right, self.sum_left):
            copy.wait_recv()


NT = (((1,), (1,)), ((), ()))
TN = (((0,), (0,)), ((), ()))
TILE = 512
HALF_TILE = 256
TERM_TILE = 256
VMEM_BYTES = 63 << 20
LAYER_COPIES = 2 * 14 + 1 + 3 * 15 + 24 + 8 + 12 + 7 + 15 + 2 * 15


def silu_parts(pre_gate):
    sigma = jax.nn.sigmoid(pre_gate)
    return (pre_gate * sigma, sigma * (1.0 + pre_gate * (1.0 - sigma)))


def unit_grads(rows_x, rows_dy, w_both, w_down, parts, hidden_out, pre=None):
    hid = w_down.shape[1]
    if pre is None:
        pre = jnp.dot(rows_x[...], w_both[...], preferred_element_type=F32)
    hidden_grad = jnp.dot(rows_dy[...], w_down[...], preferred_element_type=F32)
    pre_up = pre[:, hid:]
    activated, derivative = silu_parts(pre[:, :hid])
    hidden = activated * pre_up
    parts[:, pl.ds(0, hid)] = (hidden_grad * pre_up * derivative).astype(BF16)
    parts[:, pl.ds(hid, hid)] = (hidden_grad * activated).astype(BF16)
    hidden_out[...] = hidden.astype(BF16)
    return hidden * hidden_grad


def input_term(parts, w_both, first, columns, store, tile=TERM_TILE):
    def body(i, carry):
        at = pl.multiple_of(i * tile, tile)
        value = lax.dot_general(
            parts[...], w_both[pl.ds(first + at, tile)], NT, preferred_element_type=F32
        )
        store(pl.ds(at, tile), value.astype(BF16))
        return carry

    lax.fori_loop(0, columns // tile, body, 0)


def lane_sums(value):
    high = value.astype(BF16)
    low = (value - high.astype(F32)).astype(BF16)
    ones = jnp.ones((8, value.shape[1]), BF16)
    return lax.dot_general(ones, high, NT, preferred_element_type=F32) + lax.dot_general(
        ones, low, NT, preferred_element_type=F32
    )


def routing(meta, slots, tokens, block):
    experts = SIDE * SIDE
    expert = lax.broadcasted_iota(jnp.int32, (experts, tokens), 0).astype(F32)
    named = [(expert == meta[k : k + 1, :tokens]).astype(F32) for k in range(2)]
    row = lax.broadcasted_iota(jnp.int32, (tokens, tokens), 0)
    col = lax.broadcasted_iota(jnp.int32, (tokens, tokens), 1)
    earlier = jnp.dot(
        (named[0] + named[1]).astype(BF16),
        (row < col).astype(F32).astype(BF16),
        preferred_element_type=F32,
    )
    slot = [jnp.sum(earlier * hit, axis=0, keepdims=True) for hit in named]
    weight = [meta[2 + k : 3 + k, :tokens] for k in range(2)]
    return named, slot, weight


def routing_tables(meta, slots, tokens, block):
    unused, slot, weight = routing(meta, slots, tokens, block)
    row = lax.broadcasted_iota(jnp.int32, (2 * slots, tokens), 0).astype(F32)
    tables = []
    for weighted in range(2):
        for second in range(2):
            table = jnp.zeros((2 * slots, tokens), F32)
            for k in range(2):
                position = meta[k : k + 1, :tokens] * block + slot[k] + second * (block // 2)
                value = weight[k] if weighted else jnp.ones_like(weight[k])
                table = table + jnp.where(row == position, value, 0.0)
            tables.append(table.astype(BF16))
    return tables


def fill(meta, ids, weights):
    tokens = ids.shape[1]
    meta[...] = jnp.zeros_like(meta)
    meta[pl.ds(0, 2), pl.ds(0, tokens)] = ids[...].astype(F32)
    meta[pl.ds(2, 2), pl.ds(0, tokens)] = weights[...].astype(F32)


class WeightSums:
    def __init__(self, net, x, z, tensor, grads, first_bufs):
        self.net, self.x, self.z, self.grads = net, x, z, grads
        self.half = half = grads.shape[2] // 2
        self.first_bufs = first_bufs
        pairs = SIDE // 2

        def at(xx, zz):
            return (xx * SIDE + zz, tensor)

        self.around_x = (at(turn(x, 1), z), at(turn(x, 3), z))
        self.around_z = (at(x, turn(z, 1)), at(x, turn(z, 3)))

        def x_part(position, h):
            return grads.at[position, pl.ds(h * pairs, pairs), pl.ds(0, half)]

        def z_part(position, h):
            return grads.at[pl.ds(h * pairs, pairs), position, pl.ds(half, half)]

        def slot(ref, index):
            return lambda h: ref.at[index, pl.ds(h * pairs, pairs)]

        self.rings = [
            RingSum(net, x, *self.around_x, x_part, *(slot(ref, 0) for ref in first_bufs)),
            RingSum(net, z, *self.around_z, z_part, *(slot(ref, 1) for ref in first_bufs)),
        ]

    def middle(self):
        for ring in self.rings:
            ring.absorb()
        for ring in self.rings:
            ring.send_sums()

    def second(self):
        half = self.half
        cut = (0, half // 32 * 16 + 16, half)
        relayed, from_left, from_right = self.first_bufs

        def rows_half(h):
            return pl.ds(cut[h], cut[h + 1] - cut[h])

        def summed(index):
            return lambda position, h: from_left.at[index, position, rows_half(h)]

        def slot(index, k):
            return lambda h: relayed.at[index, k, rows_half(h)]

        later = [
            RingSum(self.net, self.z, *self.around_z, summed(0), *(slot(0, k) for k in range(3))),
            RingSum(self.net, self.x, *self.around_x, summed(1), *(slot(1, k) for k in range(3))),
        ]
        for ring in self.rings:
            ring.finish()
        for steps in (2, 1, 3, 0):
            for index, ring in enumerate(later):
                other = turn((self.z, self.x)[index], steps)
                if index == 0:
                    mine = self.grads.at[self.x, other, pl.ds(0, half)]
                else:
                    mine = self.grads.at[other, self.z, pl.ds(half, half)]
                left, right = from_left.at[index, other], from_right.at[index, other]
                total(left, [mine, left, right])
                if steps == 2:
                    ring.start_far()
                elif steps == 1:
                    ring.start_ahead()
                elif steps == 3:
                    ring.start_behind()
        self.rings = later

    def finish(self, outs):
        half = self.half
        relayed, from_left, unused = self.first_bufs
        for index, ring in enumerate(self.rings):
            ring.finish()
            own = from_left.at[index, (self.z, self.x)[index]]
            for block, ref in enumerate(outs):
                cols = pl.ds(block * ref.shape[1], ref.shape[1])
                total(
                    ref.at[pl.ds(index * half, half)],
                    [own.at[:, cols]] + [relayed.at[index, k, :, cols] for k in (1, 2)],
                    scale=1.0 / (SIDE * SIDE),
                )


def layer_kernel(
    tok, grad, ids, gates, dense_gate, dense_up, dense_down, expert_gate, expert_up, expert_down,
    back, dense_sum, back_shares, out_gate, out_up, out_down, gate_grad, up_grad, down_grad,
    tok_all, grad_all, rows_x, rows_dy, exchange, w_both, w_down, parts, hidden, grads, relayed, from_left, from_right,
    terms, core_rest, y_relayed, y_left, y_right, meta, far_meta,
    shares, share_in, share_sum,
    send_sems, recv_sems, local_sems,
):
    x, z, y, core = place()
    node, tensor = x * SIDE + z, y * CORES + core
    net = Net(send_sems, recv_sems)
    peers = node_peers(x, z, tensor)
    count = SIDE * CORES
    mates = [(node, lax.rem(tensor + k, count)) for k in range(1, count)]
    local_rows, depth = tok.shape
    hid = w_down.shape[1]
    columns = exchange.shape[1]
    stack = exchange.shape[0] // 4
    outgoing = [exchange.at[pl.ds(h * stack, stack)] for h in range(2)]
    landed = [exchange.at[pl.ds((2 + h) * stack, stack)] for h in range(2)]
    block = stack // (SIDE * SIDE)
    slots = stack // 2
    far_pair = pl.ds(pl.multiple_of(turn(y, 2) * stack, stack), stack)
    dense_parts, dense_hidden = parts.at[far_pair], hidden.at[far_pair]
    started = []

    def fetch(src, dst):
        copy = pltpu.make_async_copy(src, dst, local_sems.at[len(started)])
        copy.start()
        started.append(copy)
        return copy

    dense = Gather(net, node, y, core, (tok, grad), (tok_all, grad_all), local_rows)
    routed = Gather(net, node, y, core, None, (rows_x, rows_dy), slots)
    routed.own = [routed.chunk(h, tensor) for h in range(2)]
    sums = WeightSums(net, x, z, tensor, grads, (relayed, from_left, from_right))
    meet(peers + mates)

    def rows_of(ref, index):
        return ref.at[pl.ds(pl.multiple_of(index * block, block), block)]

    def fetch_weights(gate, up, down):
        return [
            fetch(gate, w_both.at[:, pl.ds(0, hid)]),
            fetch(up, w_both.at[:, pl.ds(hid, hid)]),
            fetch(down, w_down),
        ]

    dense.start(0)
    dense.start(1)
    exchanged = []
    fill(meta, ids, gates)
    meta_sent = net.start(meta, far_meta, (node, dense.far_at))
    tables = routing_tables(meta[...], slots, local_rows, block)
    for h, source in enumerate((tok, grad)):
        out, into = outgoing[h], landed[h]
        left, right = tables[2 * h], tables[2 * h + 1]
        for first in range(0, columns, 2 * HALF_TILE):
            width = min(2 * HALF_TILE, columns - first)
            value = jnp.dot(
                left, source[:, pl.ds(first, width)], preferred_element_type=F32
            ) + jnp.dot(right, source[:, pl.ds(columns + first, width)], preferred_element_type=F32)
            out[:, pl.ds(first, width)] = value.astype(BF16)
        exchanged.append(
            [net.start(rows_of(out, peer[0]), rows_of(into, node), peer, False) for peer in peers]
            + [fetch(rows_of(out, node), rows_of(into, node))]
        )
    kept = [
        fetch(tok, dense.chunk(0, tensor)),
        fetch(grad, dense.chunk(1, tensor)),
    ] + fetch_weights(dense_gate, dense_up, dense_down)
    row = lax.broadcasted_iota(jnp.int32, (slots, 2 * slots), 0)
    col = lax.broadcasted_iota(jnp.int32, (slots, 2 * slots), 1)
    half = block // 2
    origin = lax.div(row, half) * block + lax.rem(row, half)
    join_tables = [(col == origin + k * half).astype(F32).astype(BF16) for k in range(2)]
    row = lax.broadcasted_iota(jnp.int32, (2 * slots, slots), 0)
    col = lax.broadcasted_iota(jnp.int32, (2 * slots, slots), 1)
    origin = lax.div(row, block) * half + lax.rem(row, block)
    back_tables = [
        (jnp.logical_and(col == origin - k * half, lax.div(lax.rem(row, block), half) == k))
        .astype(F32)
        .astype(BF16)
        for k in range(2)
    ]

    def join(h):
        for copy in exchanged[h][:-1]:
            copy.wait()
        exchanged[h][-1].wait()
        own, into = routed.own[h], landed[h]
        for first in range(0, columns, 2 * HALF_TILE):
            width = min(2 * HALF_TILE, columns - first)
            cols = pl.ds(first, width)
            for k in range(2):
                own[:, pl.ds(k * columns + first, width)] = jnp.dot(
                    join_tables[k], into[:, cols], preferred_element_type=F32
                ).astype(BF16)

    dense.relay()
    dense.relay_rest()
    join(0)
    routed.start(0)
    dense.relay_far()
    meta_sent.wait_recv()
    tables = routing_tables(far_meta[...], slots, local_rows, block)[:2]
    far_rows = pl.ds(pl.multiple_of(dense.far_at * local_rows, local_rows), local_rows)
    far_y = turn(y, 2)
    for first in range(0, columns, 2 * HALF_TILE):
        width = min(2 * HALF_TILE, columns - first)
        value = (
            jnp.dot(tables[0], tok_all[far_rows, pl.ds(first, width)], preferred_element_type=F32)
            + jnp.dot(
                tables[1],
                tok_all[far_rows, pl.ds(columns + first, width)],
                preferred_element_type=F32,
            )
        ).astype(BF16)
        for c in range(2):
            terms[c, 1, far_y, pl.ds(0, slots), pl.ds(first, width)] = value[
                c * slots : (c + 1) * slots
            ]
    each = SIDE * SIDE // 2

    def far_leaving(index):
        rows = pl.ds(pl.multiple_of(lax.rem(index, each) * block, block), block)
        return terms.at[lax.div(index, each), 1, far_y, rows]

    def far_landing(index):
        rows = pl.ds(pl.multiple_of(lax.rem(index, each) * block, block), block)
        return core_rest.at[lax.div(index, each), rows]

    far_copies = [
        net.start(far_leaving(peer[0]), far_landing(node), peer, False) for peer in peers
    ]
    far_kept = fetch(far_leaving(node), far_landing(node))

    def join_far():
        for copy in far_copies:
            copy.wait()
        far_kept.wait()
        for c in range(2):
            rows = pl.ds(pl.multiple_of(routed.far_at * slots + c * (slots // 2), slots // 2), slots // 2)
            for first in range(0, columns, 2 * HALF_TILE):
                width = min(2 * HALF_TILE, columns - first)
                value = core_rest[c, pl.ds(0, slots), pl.ds(first, width)]
                for k in range(2):
                    rows_x[rows, pl.ds(k * columns + first, width)] = jnp.dot(
                        join_tables[k][: slots // 2, :slots], value, preferred_element_type=F32
                    ).astype(BF16)
        routed.pass_on(0, routed.far_at, "far")

    join(1)
    routed.start(1)

    for name in ("own", "left", "right", "far"):
        dense.arrive(name)
    for copy in kept:
        copy.wait()
    unit_grads(tok_all, grad_all, w_both, w_down, dense_parts, dense_hidden)

    def side(other_core):
        return lax.rem(core + other_core, CORES)

    for c in range(2):

        def keep_dense(cols, value, c=c):
            for at in range(SIDE):
                for k in range(CORES):
                    first = (at * CORES + k) * local_rows
                    terms[c, side(k), at, pl.ds(slots, local_rows), cols] = value[
                        first : first + local_rows
                    ]

        input_term(dense_parts, w_both, c * columns, columns, keep_dense)
    weights = fetch_weights(expert_gate, expert_up, expert_down)
    band = depth // SIDE
    x_ring, z_ring = sums.rings
    for steps in (2, 1, 3, 0):
        other = turn(x, steps)
        cols = pl.ds(pl.multiple_of(other * band, band), band)
        value = lax.dot_general(
            tok_all[:, cols], dense_parts[...], TN, preferred_element_type=F32
        ).astype(BF16)
        grads[other, :, :, pl.ds(0, 2 * hid)] = value.reshape(SIDE, band // SIDE, 2 * hid)
        value = lax.dot_general(
            grad_all[:, cols], dense_hidden[...], TN, preferred_element_type=F32
        ).astype(BF16)
        grads[other, :, :, pl.ds(2 * hid, hid)] = value.reshape(SIDE, band // SIDE, hid)
        if steps == 2:
            x_ring.start_far()
        elif steps == 1:
            x_ring.start_ahead()
        elif steps == 3:
            x_ring.start_behind()
    z_ring.start_far()
    z_ring.start_ahead()
    z_ring.start_behind()
    for copy in weights:
        copy.wait()

    pair = CORES * slots
    crossed = {}

    def from_core(step, c):
        index, rows = 2 * step + c, slots + local_rows
        fit = exchange.shape[0] // rows
        if index < fit:
            return exchange.at[pl.ds(index * rows, rows)]
        return core_rest.at[index - fit]

    def early_place(step):
        ref, first = ((tok_all, 0), (tok_all, 4 * hid), (grad_all, 0))[step - 1]
        return [ref.at[:, pl.ds(first + k * 2 * hid, 2 * hid)] for k in range(2)]

    def early_rows(step, at):
        rows = pl.ds(pl.multiple_of(at * pair, pair), pair)
        pre = jnp.dot(rows_x[rows], w_both[...], preferred_element_type=F32)
        high, low = early_place(step)
        rounded = pre.astype(BF16)
        high[...] = rounded
        low[...] = (pre - rounded.astype(F32)).astype(BF16)

    def expert_rows(step, at):
        rows = pl.ds(pl.multiple_of(at * pair, pair), pair)
        pre = None
        if step:
            high, low = early_place(step)
            pre = high[...].astype(F32) + low[...].astype(F32)
        product = unit_grads(
            rows_x.at[rows], rows_dy.at[rows], w_both, w_down, parts.at[rows], hidden.at[rows], pre
        )
        shares[at] = lane_sums(product)
        for c in range(2):

            def keep_routed(cols, value, c=c):
                for k in range(CORES):
                    terms[c, side(k), at, pl.ds(0, slots), cols] = value[k * slots : (k + 1) * slots]

            input_term(parts.at[rows], w_both, c * columns, columns, keep_routed)
            crossed[step, c] = net.start(
                terms.at[c, 1, at], from_core(step, c), routed.partner
            )

    def absorb(step, at, c):
        crossed[step, c].wait_recv()
        mine = terms.at[c, 0, at]
        total(mine, [mine, from_core(step, c)])

    def half_rows(ref, *lead):
        half = ref.shape[-2] // 2
        return lambda h: ref.at[(*lead, pl.ds(h * half, half))]

    y_rings = [
        RingSum(
            net, y, routed.right, routed.left,
            lambda position, h, c=c: half_rows(terms, c, 0, position)(h),
            half_rows(y_relayed, c), half_rows(y_left, c), half_rows(y_right, c),
        )
        for c in range(2)
    ]
    routed.arrive("own")
    expert_rows(0, y)
    routed.take(0)
    join_far()
    dense.flush()
    for step, (name, at) in enumerate((("left", 3), ("right", 1), ("far", 2))):
        routed.arrive(name, (0,))
        early_rows(step + 1, turn(y, at))
    routed.take_and_relay(1)
    sums.middle()
    routed.arrive("left", (1,))
    expert_rows(1, turn(y, 3))
    for c in range(2):
        absorb(1, turn(y, 3), c)
        y_rings[c].start_behind()
    routed.arrive("right", (1,))
    expert_rows(2, turn(y, 1))
    for c in range(2):
        absorb(2, turn(y, 1), c)
        y_rings[c].start_ahead()
    routed.take_far(1)
    routed.arrive("far", (1,))
    expert_rows(3, turn(y, 2))
    for c in range(2):
        absorb(3, turn(y, 2), c)
        y_rings[c].start_far()
    sums.second()
    share_copies = [
        net.start(shares.at[lax.div(mate[1], CORES)], share_in.at[tensor], mate) for mate in mates
    ]
    for c in range(2):
        absorb(0, y, c)

    written = []

    def weight_tiles(first, last):
        for i in range(first, last):
            cols = pl.ds(i * TILE, TILE)
            w_both[cols] = lax.dot_general(
                rows_x[:, cols], parts[...], TN, preferred_element_type=F32
            ).astype(BF16)
            w_down[cols] = lax.dot_general(
                rows_dy[:, cols], hidden[...], TN, preferred_element_type=F32
            ).astype(BF16)
            written.append(fetch(w_both.at[cols, pl.ds(0, hid)], gate_grad.at[cols]))
            written.append(fetch(w_both.at[cols, pl.ds(hid, hid)], up_grad.at[cols]))
            written.append(fetch(w_down.at[cols], down_grad.at[cols]))

    weight_tiles(0, 2)
    for copy in share_copies:
        copy.wait_recv()
    value = shares[y]
    for k in range(1, count):
        value = value + share_in[lax.rem(tensor + k, count)]
    share_sum[...] = value
    back_shares[node] = value
    returned = [net.start(share_sum, back_shares.at[node], peer) for peer in peers]
    y_rings[0].middle()
    weight_tiles(2, 4)
    y_rings[1].middle()
    weight_tiles(4, 5)
    sums.middle()
    count_tiles = depth // TILE
    short = columns // 2
    for c in range(2):
        weight_tiles(5 + c, 6 + c)
        y_rings[c].finish()
        own, left, right = terms.at[c, 0, y], y_left.at[c], y_right.at[c]
        landed_rows = [ref.at[pl.ds(0, slots)] for ref in (own, left, right)]
        total(own.at[pl.ds(0, slots)], landed_rows)
        for first in range(0, short, HALF_TILE):
            width = min(HALF_TILE, short - first)
            value = jnp.dot(
                back_tables[0], own[pl.ds(0, slots), pl.ds(first, width)], preferred_element_type=F32
            ) + jnp.dot(
                back_tables[1],
                own[pl.ds(0, slots), pl.ds(short + first, width)],
                preferred_element_type=F32,
            )
            for k in range(2):
                y_relayed[c, pl.ds(0, slots), pl.ds(k * short + first, width)] = value[
                    k * slots : (k + 1) * slots
                ].astype(BF16)

        def parted(index, c=c):
            each = slots // block
            rows = pl.multiple_of(lax.rem(index, each) * block, block)
            cols = pl.multiple_of(lax.div(index, each) * short, 128)
            return y_relayed.at[c, pl.ds(rows, block), pl.ds(cols, short)]

        returned += [net.start(parted(peer[0]), rows_of(back.at[c], node), peer) for peer in peers]
        written.append(fetch(parted(node), rows_of(back.at[c], node)))
        total(
            dense_sum.at[:, pl.ds(c * columns, columns)],
            [ref.at[pl.ds(slots, local_rows)] for ref in (own, left, right)],
        )
    weight_tiles(7, count_tiles)
    sums.finish((out_gate, out_up, out_down))
    for copy in returned:
        copy.wait_recv()
    for copy in written:
        copy.wait()
    routed.flush()
    net.drain()


def layer(tokens, out_grad, ids, gates, slots, dense, expert):
    rows, depth = tokens.shape
    hid = dense[0].shape[1]
    count = SIDE * CORES
    nodes = SIDE * SIDE
    node_rows, slot_rows = count * rows, count * slots
    own = depth // nodes
    half = depth // 2
    bands = (2, SIDE, own // 2, 3 * hid)
    shape = jax.ShapeDtypeStruct
    share = (8, CORES * slots)
    return pl.pallas_call(
        layer_kernel,
        out_shape=[
            shape((2, 2 * slots, half // 2), BF16),
            shape((rows, depth), F32),
            shape((nodes,) + share, F32),
        ]
        + [shape((own, hid), BF16)] * 3
        + [shape((depth, hid), BF16)] * 3,
        in_specs=[VMEM] * 4 + [ANY] * 6,
        out_specs=[ANY] + [VMEM] * 5 + [ANY] * 3,
        scratch_shapes=[
            pltpu.VMEM((node_rows, depth), BF16),
            pltpu.VMEM((node_rows, depth), BF16),
            pltpu.VMEM((slot_rows, depth), BF16),
            pltpu.VMEM((slot_rows, depth), BF16),
            pltpu.VMEM((8 * slots, half), BF16),
            pltpu.VMEM((depth, 2 * hid), BF16),
            pltpu.VMEM((depth, hid), BF16),
            pltpu.VMEM((slot_rows, 2 * hid), BF16),
            pltpu.VMEM((slot_rows, hid), BF16),
            pltpu.VMEM((SIDE, SIDE, own, 3 * hid), BF16),
        ]
        + [pltpu.VMEM(bands, BF16)] * 3
        + [
            pltpu.VMEM((2, CORES, SIDE, slots + rows, half), BF16),
            pltpu.VMEM((2 * SIDE - 8 * slots // (slots + rows), slots + rows, half), BF16),
        ]
        + [pltpu.VMEM((2, slots + rows, half), BF16)] * 3
        + [
            pltpu.VMEM((8, 128), F32),
            pltpu.VMEM((8, 128), F32),
            pltpu.VMEM((SIDE,) + share, F32),
            pltpu.VMEM((count,) + share, F32),
            pltpu.VMEM(share, F32),
            pltpu.SemaphoreType.DMA((LAYER_COPIES,)),
            pltpu.SemaphoreType.DMA((LAYER_COPIES,)),
            pltpu.SemaphoreType.DMA((36,)),
        ],
        compiler_params=pltpu.CompilerParams(
            collective_id=0, has_side_effects=True, vmem_limit_bytes=VMEM_BYTES
        ),
        name="layer",
    )(tokens, out_grad, ids, gates, *dense, *expert)


def finish_kernel(out_grad, dense_sum, back, ids, gates, back_shares, *rest):
    sources, input_grad, share, results = rest[:6], rest[6], rest[7], rest[8:14]
    buffers, in_sems, out_sems, meta = rest[14:20], rest[20], rest[21], rest[22]
    loads, stores = [], []
    for source, buffer, result in zip(sources, buffers, results):
        pieces = 1 if source.shape[0] < 1024 else 7
        rows = source.shape[0] // pieces
        for i in range(pieces):
            at = pl.ds(i * rows, rows)
            k = len(loads)
            loads.append(pltpu.make_async_copy(source.at[at], buffer.at[at], in_sems.at[k]))
            stores.append(pltpu.make_async_copy(buffer.at[at], result.at[at], out_sems.at[k]))
            loads[k].start()
    nodes, tokens = SIDE * SIDE, out_grad.shape[0]
    slots, columns = back.shape[1] // 2, back.shape[2]
    block = 2 * slots // nodes
    for load, store in zip(loads, stores):
        load.wait()
        store.start()
    fill(meta, ids, gates)
    named, slot, weight = routing(meta[...], slots, tokens, block)
    first = lax.axis_index("node") * (block // 2)
    first = first + lax.rem(lax.axis_index("tensor"), CORES) * slots
    lane = lax.broadcasted_iota(jnp.int32, (block // 2, CORES * slots), 1)
    wanted = lax.broadcasted_iota(jnp.int32, (block // 2, CORES * slots), 0) + first
    wanted = (lane == wanted).astype(F32).astype(BF16)

    def split(value):
        high = value.astype(BF16)
        return high, (value - high.astype(F32)).astype(BF16)

    mine = sum(
        lax.dot_general(wanted, part, NT, preferred_element_type=F32)
        for part in split(back_shares[:, 0, :])
    )
    index = lax.broadcasted_iota(jnp.int32, (block // 2, tokens), 0).astype(F32)
    for k in range(2):
        value = sum(
            jnp.dot(part, named[k].astype(BF16), preferred_element_type=F32) for part in split(mine)
        )
        value = jnp.sum(jnp.where(index == slot[k], value, 0.0), axis=0, keepdims=True)
        share[pl.ds(k, 1), :] = value / weight[k]
    tables = routing_tables(meta[...], slots, tokens, block)
    for k in range(4):
        cols = pl.ds(k * columns, columns)
        picked = lax.dot_general(tables[k % 2], back[k // 2], TN, preferred_element_type=F32)
        input_grad[:, cols] = (
            out_grad[:, cols].astype(F32) + dense_sum[:, cols] + picked
        ).astype(BF16)
    for store in stores:
        store.wait()


def finish(out_grad, dense_sum, back, ids, gates, back_shares, grads):
    return pl.pallas_call(
        finish_kernel,
        out_shape=[
            jax.ShapeDtypeStruct(out_grad.shape, BF16),
            jax.ShapeDtypeStruct((2, out_grad.shape[0]), F32),
        ]
        + [jax.ShapeDtypeStruct(grad.shape, BF16) for grad in grads],
        in_specs=[VMEM] * 6 + [ANY] * 6,
        out_specs=[VMEM] * 2 + [ANY] * 6,
        scratch_shapes=[pltpu.VMEM(grad.shape, BF16) for grad in grads]
        + [pltpu.SemaphoreType.DMA((24,))] * 2
        + [pltpu.VMEM((8, 128), F32)],
        compiler_params=pltpu.CompilerParams(vmem_limit_bytes=60 << 20),
        name="finish",
    )(out_grad, dense_sum, back, ids, gates, back_shares, *grads)


def local(
    tokens, out_grad, gate_weights, expert_ids, dense_gate, dense_up, dense_down,
    expert_gate, expert_up, expert_down,
):
    slots = 4 * tokens.shape[0]
    ids, gates = expert_ids.T, gate_weights.T
    back, dense_sum, back_shares, *sums = layer(
        tokens, out_grad, ids, gates, slots, (dense_gate, dense_up, dense_down),
        (expert_gate[0], expert_up[0], expert_down[0]),
    )
    input_grad, share, *sums = finish(out_grad, dense_sum, back, ids, gates, back_shares, sums)
    return (input_grad, share.T, *sums[:3], *(value[None] for value in sums[3:]))


def solution(mesh):
    rows = P(("node", "tensor"), None)
    dense = P(None, "tensor")
    expert = P("node", None, "tensor")
    summed = P("node", "tensor")
    return jax.shard_map(
        local,
        mesh=mesh,
        in_specs=(rows,) * 4 + (dense,) * 3 + (expert,) * 3,
        out_specs=(rows, rows) + (summed,) * 3 + (expert,) * 3,
        check_vma=False,
    )
```
